32 devices in a mesh: grp: 2 (over x), seq: 16 (over z, y, core).
Axes of the slice: x: 2, y: 2, z: 4, core: 2. Of those that a mesh axis runs over, the one named last changes fastest.
Arguments:
- inputs: bfloat16 [2, 2048, 1536], P('grp', 'seq'), may hold values from -6 to 6
- cotangent: bfloat16 [2, 2048, 1536], P('grp', 'seq'), may hold values from -6 to 6
- block_ids: int32 [2, 2048], P('grp'), may hold values from 0 to 15, never falling along the last dimension, each value on 1 to 256 neighbouring positions
- piece_order: int32 [16], replicated, may hold values from 0 to 15, each once
- w_query: bfloat16 [1536, 1536], P('seq'), may hold values from -0.15625 to 0.15625
- w_key: bfloat16 [1536, 768], P('seq'), may hold values from -0.15625 to 0.15625
- w_value: bfloat16 [1536, 768], P('seq'), may hold values from -0.15625 to 0.15625
- w_out: bfloat16 [1536, 1536], P('seq'), may hold values from -3.5 to 3.5
- w_gate: bfloat16 [1536, 4096], P('seq'), may hold values from -0.15625 to 0.15625
- w_up: bfloat16 [1536, 4096], P('seq'), may hold values from -0.15625 to 0.15625
- w_down: bfloat16 [4096, 1536], P('seq'), may hold values from -0.09375 to 0.09375
- gain_attn: bfloat16 [1536], P('seq'), may hold values from 0.5 to 1.5
- gain_mlp: bfloat16 [1536], P('seq'), may hold values from 0.5 to 1.5
Outputs:
- output: bfloat16 [2, 2048, 1536], P('grp', 'seq')
- grad_inputs: bfloat16 [2, 2048, 1536], P('grp', 'seq')
- grad_w_query: float32 [1536, 1536], P('seq')
- grad_w_key: float32 [1536, 768], P('seq')
- grad_w_value: float32 [1536, 768], P('seq')
- grad_w_out: float32 [1536, 1536], P('seq')
- grad_w_gate: float32 [1536, 4096], P('seq')
- grad_w_up: float32 [1536, 4096], P('seq')
- grad_w_down: float32 [4096, 1536], P('seq')
- grad_gain_attn: float32 [1536], P('seq')
- grad_gain_mlp: float32 [1536], P('seq')
The draws below stay inside these ranges and needn't reach their ends.
Inputs may be any that keep to these rules, and one draw needn't show every extreme that they name: `block_ids`: along each sequence's positions the block numbers never fall; each block covers 1 to 256 positions, and some block covers exactly 256. `piece_order`: each number appears once.
All inputs are finite; a program needn't handle non-finite values.
Results may differ from the reference program's by a relative error of at most 0.019.
Values may be sent and summed in bfloat16 or wider, within the bound.
No kernel may reach another device: no remote copies, remote signals or barrier semaphores. Data moves between devices by JAX's collectives and lax.ppermute only.
A program may use at most 384 MiB of HBM per device.

```python
import math
import jax
import jax.numpy as jnp
import numpy as np
from jax import lax

D = 1536
HEADS = 16
KV_HEADS = 8
HEAD_DIM = 96
FF = 4096
BLOCK = 256
TOK_DEV = 128
LENGTH = 2048
PIECES = 16
SEQS = 2


def levels(own_key, shape, shards, least, high):
    loudness = 1.0
    for dim, shards_of in shards:
        draws = jax.random.uniform(jax.random.fold_in(jax.random.fold_in(own_key, 6), dim), (shards_of,), jnp.float32, least / len(shards), high / len(shards))
        loudness = loudness * jnp.repeat(jnp.exp(draws), shape[dim] // shards_of).reshape((-1,) + (1,) * (len(shape) - 1 - dim))
    return loudness


def length_profile(number_of, total, limit, slope):
    loads = [(1 << 20) // math.isqrt(standing ** slope) + 1 for standing in range(2, number_of + 1)]
    rest, counts = total - limit - (number_of - 1), [1] * (number_of - 1)
    while rest > 0:
        candidates = [i for i in range(number_of - 1) if counts[i] < limit]
        mass, left = sum([loads[i] for i in candidates]), rest
        for i in candidates:
            addition = min(limit - counts[i], max(1, left * loads[i] // mass), rest)
            counts[i] = counts[i] + addition
            rest = rest - addition
    return np.array([limit] + counts)


def ragged_sizes(key, amount, total, bound, lean):
    if amount == 2:
        one = jax.random.randint(key, (), max(1, total - bound), min(bound, total - 1) + 1)
        return jnp.stack([one, total - one])
    tallies = jnp.asarray(length_profile(amount, total, bound, lean), jnp.int32)
    couples = (amount - 1) // 2
    source_of, receiver = tallies[1:1 + 2 * couples:2], tallies[2:2 + 2 * couples:2]
    slack = jnp.minimum(source_of - 1, bound - receiver)
    passed = jax.random.randint(jax.random.fold_in(key, 1), (couples,), 0, 1 << 20) % (slack + 1)
    tallies = tallies.at[1:1 + 2 * couples:2].set(source_of - passed).at[2:2 + 2 * couples:2].set(receiver + passed)
    return tallies[jax.random.permutation(jax.random.fold_in(key, 2), amount)]


def bell_draw(stream_key, shape, deviation, most, shards=(), held_as=jnp.bfloat16):
    drawn = deviation * jax.random.normal(stream_key, shape, jnp.float32)
    if shards:
        drawn = drawn * levels(stream_key, shape, shards, -0.22, 0.18)
    return jnp.clip(drawn, -most, most).astype(held_as)


def setup_inputs(seed: int = 0) -> dict:
    key_of = jax.random.split(jax.random.key(seed), 14)
    inputs = bell_draw(key_of[0], (SEQS, LENGTH, D), 1.0, 6.0, ((0, 2), (1, 16)))
    cotangent = bell_draw(key_of[1], (SEQS, LENGTH, D), 1.0, 6.0, ((0, 2), (1, 16)))
    block_ids = jax.vmap(lambda own: jnp.searchsorted(jnp.cumsum(ragged_sizes(own, LENGTH // (BLOCK // 2), LENGTH, BLOCK, 0)), jnp.arange(LENGTH), side="right"))(jax.random.split(key_of[2], SEQS)).reshape((SEQS, LENGTH)).astype(jnp.int32)
    piece_order = jax.random.permutation(key_of[3], PIECES).astype(jnp.int32)
    w_query = bell_draw(key_of[4], (D, HEADS * HEAD_DIM), D ** -0.5, 0.15625, ((0, 16),))
    w_key = bell_draw(key_of[5], (D, KV_HEADS * HEAD_DIM), D ** -0.5, 0.15625, ((0, 16),))
    w_value = bell_draw(key_of[6], (D, KV_HEADS * HEAD_DIM), D ** -0.5, 0.15625, ((0, 16),))
    w_out = bell_draw(key_of[7], (HEADS * HEAD_DIM, D), (max(1, 4 * D // LENGTH)) ** -0.5, 3.5, ((0, 16),))
    w_gate = bell_draw(key_of[8], (D, FF), D ** -0.5, 0.15625, ((0, 16),))
    w_up = bell_draw(key_of[9], (D, FF), D ** -0.5, 0.15625, ((0, 16),))
    w_down = bell_draw(key_of[10], (FF, D), FF ** -0.5, 0.09375, ((0, 16),))
    gain_attn = jnp.clip(1.0 + 0.1 * jax.random.normal(key_of[11], (D,), jnp.float32), 0.5, 1.5).astype(jnp.bfloat16)
    gain_mlp = jnp.clip(1.0 + 0.1 * jax.random.normal(key_of[12], (D,), jnp.float32), 0.5, 1.5).astype(jnp.bfloat16)
    return {"inputs": inputs, "cotangent": cotangent, "block_ids": block_ids, "piece_order": piece_order, "w_query": w_query, "w_key": w_key, "w_value": w_value, "w_out": w_out, "w_gate": w_gate, "w_up": w_up, "w_down": w_down, "gain_attn": gain_attn, "gain_mlp": gain_mlp}


@jax.custom_vjp
def low(v):
    return lax.optimization_barrier(v.astype(jnp.bfloat16)).astype(jnp.float32)

@jax.custom_vjp
def low_back(v):
    return v

def low_keep(v):
    return (low(v), None)

def low_pass(kept, grad):
    return (grad,)

def back_keep(v):
    return (v, None)

def back_low(kept, grad):
    return (low(grad),)
low.defvjp(low_keep, low_pass)
low_back.defvjp(back_keep, back_low)

def product(left, right):
    return jnp.dot(left, right, preferred_element_type=jnp.float32, precision=lax.Precision.HIGHEST)

def rms_norm(rows_in, gain_row):
    return rows_in * lax.rsqrt(lax.optimization_barrier(jnp.mean(rows_in * rows_in, axis=-1, keepdims=True)) + 1e-05) * gain_row

def rotary_tables(positions, head_dim):
    half_dim = head_dim // 2
    frequency = 100000.0 ** (-jnp.arange(half_dim, dtype=jnp.float32) * 2.0 / head_dim)
    angles = positions.astype(jnp.float32)[:, None] * frequency[None, :]
    return (jnp.cos(angles)[:, None, :], jnp.sin(angles)[:, None, :])

def rotate(vectors, cosine_table, sine_table):
    half_dim = vectors.shape[-1] // 2
    front_half = vectors[..., :half_dim]
    back_half = vectors[..., half_dim:]
    return jnp.concatenate([front_half * cosine_table - back_half * sine_table, back_half * cosine_table + front_half * sine_table], axis=-1)

def attend(queries, keys, values, blocks):
    length = queries.shape[0]
    block_rows = min(256, length)
    grouped = queries.reshape(length // block_rows, block_rows, KV_HEADS, HEADS // KV_HEADS, HEAD_DIM)
    query_blocks = blocks.reshape(length // block_rows, block_rows)

    def one_block(pair):
        query_part, part_blocks = pair
        scores = jnp.einsum('qkgd,tkd->kgqt', query_part, keys, precision=lax.Precision.HIGHEST) * HEAD_DIM ** (-0.5)
        scores = low_back(scores)
        allowed = blocks[None, None, None, :] <= part_blocks[None, None, :, None]
        scores = jnp.where(allowed, scores, -1e+30)
        chance = low(jax.nn.softmax(scores, axis=-1))
        return jnp.einsum('kgqt,tkd->qkgd', chance, values, precision=lax.Precision.HIGHEST)
    mixed = lax.map(jax.checkpoint(one_block), (grouped, query_blocks))
    return mixed.reshape(length, HEADS * HEAD_DIM)

def layer_forward(residual, blocks, cosine_table, sine_table, params):
    w_query, w_key, w_value, w_out, w_gate, w_up, w_down, gain_one, gain_two = params
    length = residual.shape[0]
    normed_attn = low(rms_norm(residual, gain_one))
    query_pre = low_back(product(normed_attn, w_query)).reshape(length, HEADS, HEAD_DIM)
    queries = low(rotate(query_pre, cosine_table, sine_table))
    key_pre = low_back(product(normed_attn, w_key)).reshape(length, KV_HEADS, HEAD_DIM)
    keys = low(rotate(key_pre, cosine_table, sine_table))
    values = low(low_back(product(normed_attn, w_value))).reshape(length, KV_HEADS, HEAD_DIM)
    attended = low(low_back(attend(queries, keys, values, blocks)))
    middle = residual + low_back(product(attended, w_out))
    normed_mlp = low(rms_norm(middle, gain_two))
    gate_value = low_back(product(normed_mlp, w_gate))
    upward = low_back(product(normed_mlp, w_up))
    hidden = low(jax.nn.silu(gate_value) * upward)
    return middle + product(hidden, w_down)

def reference(inputs, cotangent, block_ids, piece_order, w_query, w_key, w_value, w_out, w_gate, w_up, w_down, gain_attn, gain_mlp):
    rows_all = jnp.arange(LENGTH, dtype=jnp.int32)
    positions = jnp.take(piece_order, rows_all // TOK_DEV) * TOK_DEV + rows_all % TOK_DEV
    cosine_table, sine_table = rotary_tables(positions, HEAD_DIM)
    blocks_all = jnp.take(block_ids, positions, axis=1)
    params = (w_query.astype(jnp.float32), w_key.astype(jnp.float32), w_value.astype(jnp.float32), w_out.astype(jnp.float32), w_gate.astype(jnp.float32), w_up.astype(jnp.float32), w_down.astype(jnp.float32), gain_attn.astype(jnp.float32), gain_mlp.astype(jnp.float32))

    def whole_fn(weights, sequences):

        def one_sequence(pair):
            return layer_forward(pair[0], pair[1], cosine_table, sine_table, weights)
        return lax.map(one_sequence, (sequences, blocks_all))
    outputs, pullback = jax.vjp(whole_fn, params, inputs.astype(jnp.float32))
    grad_params, grad_seqs = pullback(cotangent.astype(jnp.float32))
    return (outputs.astype(jnp.bfloat16), grad_seqs.astype(jnp.bfloat16), grad_params[0], grad_params[1], grad_params[2], grad_params[3], grad_params[4], grad_params[5], grad_params[6], grad_params[7], grad_params[8])
```

```python
import functools

import jax
import jax.numpy as jnp
from jax import lax
from jax.experimental import pallas as pl
from jax.experimental.pallas import tpu as pltpu
from jax.sharding import PartitionSpec as P

HEADS = 16
KV_HEADS = 8
HEAD_DIM = 96


eps_norm = 1e-05
rope_base = 100000.0
masked_score = -1e30


def rms_scale(rows_in):
    return lax.rsqrt(jnp.mean(rows_in * rows_in, axis=-1, keepdims=True) + eps_norm)


def norm_back(grad_normed, rows_in, row_scale, gain_row):
    normed = rows_in * row_scale
    grad_gain = jnp.sum(grad_normed * normed, axis=0)
    scaled_grad = grad_normed * gain_row
    grad_rows = row_scale * (
        scaled_grad - normed * jnp.mean(scaled_grad * normed, axis=-1, keepdims=True)
    )
    return (grad_rows, grad_gain)


def rotary_tables(positions, head_dim):
    half_dim = head_dim // 2
    frequency = rope_base ** (-jnp.arange(half_dim, dtype=jnp.float32) * 2.0 / head_dim)
    angles = positions.astype(jnp.float32)[:, None] * frequency[None, :]
    return (jnp.cos(angles)[:, None, :], jnp.sin(angles)[:, None, :])


def rotate(vectors, cosine_table, sine_table):
    half_dim = vectors.shape[-1] // 2
    front_half = vectors[..., :half_dim]
    back_half = vectors[..., half_dim:]
    return jnp.concatenate(
        [
            front_half * cosine_table - back_half * sine_table,
            back_half * cosine_table + front_half * sine_table,
        ],
        axis=-1,
    )


def unrotate(grads, cosine_table, sine_table):
    half_dim = grads.shape[-1] // 2
    front_half = grads[..., :half_dim]
    back_half = grads[..., half_dim:]
    return jnp.concatenate(
        [
            front_half * cosine_table + back_half * sine_table,
            back_half * cosine_table - front_half * sine_table,
        ],
        axis=-1,
    )


def over_rows(left, right):
    return lax.dot_general(
        left, right, (((0,), (0,)), ((), ())), preferred_element_type=jnp.float32
    )


def times_back(left, right):
    return lax.dot_general(
        left, right, (((1,), (1,)), ((), ())), preferred_element_type=jnp.float32
    )


def key_block_rows(key_count):
    block_rows = min(key_count, 1024)
    return block_rows


def masked_scores(query_part, key_part, query_blocks, key_blocks, score_scale):
    scores = (
        jnp.einsum("qkgd,tkd->kgqt", query_part, key_part, preferred_element_type=jnp.float32)
        * score_scale
    )
    allowed = key_blocks[None, None, None, :] <= query_blocks[None, None, :, None]
    return jnp.where(allowed, scores, masked_score)


def forward_block(running, query_part, query_blocks, key_part, value_part, key_blocks, score_scale):
    row_max, row_sum, running_sum = running
    scores = masked_scores(query_part, key_part, query_blocks, key_blocks, score_scale)
    new_max = jnp.maximum(row_max, jnp.max(scores, axis=-1))
    likely = jnp.exp(scores - new_max[..., None])
    fading = jnp.exp(row_max - new_max)
    row_sum = row_sum * fading + jnp.sum(likely, axis=-1)
    running_sum = running_sum * fading[..., None] + jnp.einsum(
        "kgqt,tkd->kgqd",
        likely.astype(jnp.bfloat16),
        value_part,
        preferred_element_type=jnp.float32,
    )
    return (new_max, row_sum, running_sum)


def backward_block(
    grad_query,
    query_part,
    query_blocks,
    key_part,
    value_part,
    key_blocks,
    log_total,
    grad_heads,
    delta_rows,
    score_scale,
):
    scores = masked_scores(query_part, key_part, query_blocks, key_blocks, score_scale)
    chance = jnp.exp(scores - log_total[..., None])
    grad_value = jnp.einsum(
        "kgqt,kgqd->tkd",
        chance.astype(jnp.bfloat16),
        grad_heads,
        preferred_element_type=jnp.float32,
    )
    grad_chance = jnp.einsum(
        "kgqd,tkd->kgqt", grad_heads, value_part, preferred_element_type=jnp.float32
    )
    grad_scores = (chance * (grad_chance - delta_rows[..., None])).astype(jnp.bfloat16)
    grad_query = (
        grad_query
        + jnp.einsum("kgqt,tkd->kgqd", grad_scores, key_part, preferred_element_type=jnp.float32)
        * score_scale
    )
    grad_key = (
        jnp.einsum("kgqt,qkgd->tkd", grad_scores, query_part, preferred_element_type=jnp.float32)
        * score_scale
    )
    return (grad_query, grad_key, grad_value)


BIT_X, BIT_ZH, BIT_ZL, BIT_Y, BIT_C = 16, 8, 4, 2, 1
DEVICES = 32
AXES = ("grp", "seq")
SQUARE = ((64, (BIT_X, BIT_Y, BIT_C)), (64, (BIT_Y, BIT_X, BIT_C)))
CUBE = (
    (48, (BIT_X, BIT_Y, BIT_ZL, BIT_C)),
    (48, (BIT_Y, BIT_ZL, BIT_X, BIT_C)),
    (32, (BIT_ZL, BIT_X, BIT_Y, BIT_C)),
)
VMEM_LIMIT = 48 * 1024 * 1024


def swap(value, mask, sends=None):
    pairs = [(i, i ^ mask) for i in range(DEVICES) if sends is None or sends(i)]
    return lax.ppermute(value, AXES, pairs)


def bit_of(index, mask):
    return 1 if index & mask else 0


def gather_rows(rows, parts):
    first, gathered = 0, []
    for count, order in parts:
        held = rows[first : first + count]
        for mask in order:
            held = jnp.concatenate([held, swap(held, mask)], axis=0)
        gathered.append(held)
        first += count
    return gathered


def scatter_rows(pieces, parts):
    totals = []
    for held, (count, order) in zip(pieces, parts):
        for mask in reversed(order):
            half = held.shape[0] // 2
            arrived = swap(held[half:], mask)
            total = held[:half].astype(jnp.float32) + arrived.astype(jnp.float32)
            held = total if half == count else total.astype(jnp.bfloat16)
        totals.append(held)
    return jnp.concatenate(totals, axis=0)


def z_of(index):
    return (index // 4) % 4


def line_gather(value, z_index):
    below, above = [], []
    rising, falling = value, value
    for step in range(3):
        rising = lax.ppermute(
            rising, AXES, [(i, i + 4) for i in range(DEVICES) if step <= z_of(i) < 3]
        )
        falling = lax.ppermute(
            falling, AXES, [(i, i - 4) for i in range(DEVICES) if 0 < z_of(i) <= 3 - step]
        )
        below.append(rising)
        above.append(falling)
    slots = jnp.stack([below[2], below[1], below[0], value, above[0], above[1], above[2]])
    return lax.dynamic_slice_in_dim(slots, 3 - z_index, 4, axis=0)


def line_scatter(terms, z_index):
    def term_for(z_to):
        return lax.dynamic_index_in_dim(terms, jnp.clip(z_to, 0, 3), 0, keepdims=False)

    rising, falling = None, None
    for step in (3, 2, 1):
        up, down = term_for(z_index + step), term_for(z_index - step)
        if rising is not None:
            up = (up.astype(jnp.float32) + rising.astype(jnp.float32)).astype(jnp.bfloat16)
            down = (down.astype(jnp.float32) + falling.astype(jnp.float32)).astype(jnp.bfloat16)
        rising = lax.ppermute(
            up, AXES, [(i, i + 4) for i in range(DEVICES) if z_of(i) + step <= 3]
        )
        falling = lax.ppermute(
            down, AXES, [(i, i - 4) for i in range(DEVICES) if z_of(i) - step >= 0]
        )
    own = term_for(z_index).astype(jnp.float32)
    return own + rising.astype(jnp.float32) + falling.astype(jnp.float32)


def trade_blocks(blocks, masks):
    for count, mask in enumerate(masks):
        axis = count
        keep = lax.index_in_dim(blocks, 0, axis, keepdims=False)
        send = lax.index_in_dim(blocks, 1, axis, keepdims=False)
        blocks = jnp.stack([keep, swap(send, mask)])
    return blocks


def permute_blocks(table, blocks, out_dtype):
    count = table.shape[0]
    rows, columns = blocks.shape[1:]

    def body(table_ref, in_ref, out_ref):
        out_ref[...] = in_ref[...].astype(out_dtype)

    return pl.pallas_call(
        body,
        out_shape=jax.ShapeDtypeStruct((count, rows, columns), out_dtype),
        grid_spec=pltpu.PrefetchScalarGridSpec(
            num_scalar_prefetch=1,
            grid=(count,),
            in_specs=[pl.BlockSpec((1, rows, columns), lambda i, t: (t[i], 0, 0))],
            out_specs=pl.BlockSpec((1, rows, columns), lambda i, t: (i, 0, 0)),
        ),
    )(table, blocks)


def pick_columns(table, first, second, gain_rows, width):
    count, rows = table.shape[0], first.shape[0]

    def body(table_ref, first_ref, second_ref, gain_ref, out_ref):
        gain = gain_ref[...]
        out_ref[0, :, :width] = (first_ref[...].astype(jnp.float32) * gain).astype(jnp.bfloat16)
        out_ref[0, :, width:] = (second_ref[...].astype(jnp.float32) * gain).astype(jnp.bfloat16)

    return pl.pallas_call(
        body,
        out_shape=jax.ShapeDtypeStruct((count, rows, 2 * width), jnp.bfloat16),
        grid_spec=pltpu.PrefetchScalarGridSpec(
            num_scalar_prefetch=1,
            grid=(count,),
            in_specs=[
                pl.BlockSpec((rows, width), lambda i, t: (0, t[i])),
                pl.BlockSpec((rows, width), lambda i, t: (0, t[i])),
                pl.BlockSpec((rows, 1), lambda i, t: (0, 0)),
            ],
            out_specs=pl.BlockSpec((1, rows, 2 * width), lambda i, t: (i, 0, 0)),
        ),
    )(table, first, second, gain_rows)


def spread_columns(table, blocks, gain_rows, width):
    count, rows = table.shape[0], blocks.shape[1]

    def body(table_ref, in_ref, gain_ref, first_ref, second_ref):
        gain = gain_ref[...]
        first_ref[...] = in_ref[0, :, :width].astype(jnp.float32) * gain
        second_ref[...] = in_ref[0, :, width:].astype(jnp.float32) * gain

    return pl.pallas_call(
        body,
        out_shape=[jax.ShapeDtypeStruct((rows, count * width), jnp.float32)] * 2,
        grid_spec=pltpu.PrefetchScalarGridSpec(
            num_scalar_prefetch=1,
            grid=(count,),
            in_specs=[
                pl.BlockSpec((1, rows, 2 * width), lambda i, t: (t[i], 0, 0)),
                pl.BlockSpec((rows, 1), lambda i, t: (0, 0)),
            ],
            out_specs=[pl.BlockSpec((rows, width), lambda i, t: (0, i))] * 2,
        ),
    )(table, blocks, gain_rows)


def attend_forward(queries, keys, values, query_blk, key_blk, score_scale):
    seqs, heads, rows, depth = queries.shape
    key_count = keys.shape[1]
    tile = 256

    def body(q_ref, k_ref, v_ref, qb_ref, kb_ref, out_ref, total_ref):
        scores = times_back(q_ref[0, 0], k_ref[0]) * score_scale
        scores = jnp.where(kb_ref[0] <= qb_ref[0], scores, masked_score)
        top = jnp.max(scores, axis=-1, keepdims=True)
        likely = jnp.exp(scores - top)
        row_sum = jnp.sum(likely, axis=-1, keepdims=True)
        mixed = jnp.dot(
            likely.astype(jnp.bfloat16), v_ref[0], preferred_element_type=jnp.float32
        )
        out_ref[0, 0] = mixed / row_sum
        total_ref[0, 0] = top + jnp.log(row_sum)

    q_spec = pl.BlockSpec((1, 1, tile, depth), lambda s, h, t: (s, h, t, 0))
    k_spec = pl.BlockSpec((1, key_count, depth), lambda s, h, t: (s, 0, 0))
    return pl.pallas_call(
        body,
        out_shape=[
            jax.ShapeDtypeStruct((seqs, heads, rows, depth), jnp.float32),
            jax.ShapeDtypeStruct((seqs, heads, rows, 1), jnp.float32),
        ],
        grid=(seqs, heads, rows // tile),
        in_specs=[
            q_spec,
            k_spec,
            k_spec,
            pl.BlockSpec((1, tile, 1), lambda s, h, t: (s, t, 0)),
            pl.BlockSpec((1, 1, key_count), lambda s, h, t: (s, 0, 0)),
        ],
        out_specs=[
            q_spec,
            pl.BlockSpec((1, 1, tile, 1), lambda s, h, t: (s, h, t, 0)),
        ],
        compiler_params=pltpu.CompilerParams(vmem_limit_bytes=VMEM_LIMIT),
        cost_estimate=pl.CostEstimate(
            flops=4 * seqs * heads * rows * key_count * depth,
            bytes_accessed=8 * 1024 * 1024,
            transcendentals=seqs * heads * rows * key_count,
        ),
    )(queries, keys, values, query_blk, key_blk)


def attend_backward(
    queries, keys, values, attention, grad_heads, totals, query_blk, key_blk, score_scale
):
    seqs, heads, rows, depth = queries.shape
    key_count = keys.shape[1]
    tile = 256

    def body(
        q_ref, k_ref, v_ref, a_ref, g_ref, total_ref, qb_ref, kb_ref, dq_ref, dk_ref, dv_ref
    ):
        first = (pl.program_id(1) == 0) & (pl.program_id(2) == 0)

        @pl.when(first)
        def _():
            dk_ref[...] = jnp.zeros_like(dk_ref)
            dv_ref[...] = jnp.zeros_like(dv_ref)

        grads = g_ref[0, 0]
        delta = jnp.sum(grads.astype(jnp.float32) * a_ref[0, 0], axis=-1, keepdims=True)
        scores = times_back(q_ref[0, 0], k_ref[0]) * score_scale
        scores = jnp.where(kb_ref[0] <= qb_ref[0], scores, masked_score)
        chance = jnp.exp(scores - total_ref[0, 0])
        dv_ref[0] += over_rows(chance.astype(jnp.bfloat16), grads)
        grad_chance = times_back(grads, v_ref[0])
        grad_scores = (chance * (grad_chance - delta)).astype(jnp.bfloat16)
        dq_ref[0, 0] = (
            jnp.dot(grad_scores, k_ref[0], preferred_element_type=jnp.float32) * score_scale
        )
        dk_ref[0] += over_rows(grad_scores, q_ref[0, 0]) * score_scale

    q_spec = pl.BlockSpec((1, 1, tile, depth), lambda s, h, t: (s, h, t, 0))
    k_spec = pl.BlockSpec((1, key_count, depth), lambda s, h, t: (s, 0, 0))
    return pl.pallas_call(
        body,
        out_shape=[
            jax.ShapeDtypeStruct((seqs, heads, rows, depth), jnp.float32),
            jax.ShapeDtypeStruct((seqs, key_count, depth), jnp.float32),
            jax.ShapeDtypeStruct((seqs, key_count, depth), jnp.float32),
        ],
        grid=(seqs, heads, rows // tile),
        in_specs=[
            q_spec,
            k_spec,
            k_spec,
            q_spec,
            q_spec,
            pl.BlockSpec((1, 1, tile, 1), lambda s, h, t: (s, h, t, 0)),
            pl.BlockSpec((1, tile, 1), lambda s, h, t: (s, t, 0)),
            pl.BlockSpec((1, 1, key_count), lambda s, h, t: (s, 0, 0)),
        ],
        out_specs=[q_spec, k_spec, k_spec],
        compiler_params=pltpu.CompilerParams(vmem_limit_bytes=VMEM_LIMIT),
        cost_estimate=pl.CostEstimate(
            flops=10 * seqs * heads * rows * key_count * depth,
            bytes_accessed=16 * 1024 * 1024,
            transcendentals=seqs * heads * rows * key_count,
        ),
    )(queries, keys, values, attention, grad_heads, totals, query_blk, key_blk)


def by_sequence(parts):
    width = parts[0].shape[1]
    first = parts[0].reshape(2, 2, 2, 64, width).transpose(2, 1, 0, 3, 4)
    second = parts[1].reshape(2, 2, 2, 64, width).transpose(1, 2, 0, 3, 4)
    return jnp.stack([first, second], axis=3).reshape(2, 512, width)


def by_arrival(rows):
    width = rows.shape[2]
    split = rows.reshape(2, 2, 2, 2, 64, width)
    first = split[:, :, :, 0].transpose(2, 1, 0, 3, 4).reshape(512, width)
    second = split[:, :, :, 1].transpose(2, 0, 1, 3, 4).reshape(512, width)
    return [first, second]


def rotate_wide(rows, cosine, sine, heads):
    return rotate(
        rows.reshape(2, 512, heads, HEAD_DIM), cosine[None, :, None], sine[None, :, None]
    )


def unrotate_wide(rows, cosine, sine, heads):
    return unrotate(
        rows.reshape(2, 512, heads, HEAD_DIM), cosine[None, :, None], sine[None, :, None]
    )


def cube_plan(
    inputs,
    cotangent,
    block_ids,
    piece_order,
    w_query,
    w_key,
    w_value,
    w_out,
    w_gate,
    w_up,
    w_down,
    gain_attn,
    gain_mlp,
):
    low, wide = jnp.bfloat16, jnp.float32
    x = lax.axis_index("grp")
    seq_at = lax.axis_index("seq")
    z = seq_at // 4
    zh, zl, y, c = (seq_at >> 3) & 1, (seq_at >> 2) & 1, (seq_at >> 1) & 1, seq_at & 1
    pair = [(a, b) for a in (0, 1) for b in (0, 1)]
    score_scale = HEAD_DIM ** (-0.5)
    gain_rows_attn = gain_attn.astype(wide)[:, None]
    gain_rows_mlp = gain_mlp.astype(wide)[:, None]

    residual = inputs[0].astype(wide)
    scale_first = rms_scale(residual)
    normed_first = residual * scale_first
    normed_parts = gather_rows(normed_first.astype(low), SQUARE)

    packed = jnp.concatenate(
        [w_query.reshape(96, 8, 192), w_key.reshape(96, 8, 96), w_value.reshape(96, 8, 96)],
        axis=2,
    )
    packed = (packed.astype(wide) * gain_rows_attn[:, :, None]).astype(low).transpose(1, 0, 2)
    near = jnp.stack([(x ^ c ^ jc) * 4 + (c ^ jc) * 2 + (y ^ jy) for jc, jy in pair])
    wanted = permute_blocks(near, packed, low).reshape(2, 2, 96, 384)
    traded = trade_blocks(wanted, (BIT_C, BIT_Y))
    heads_rows = line_gather(traded.reshape(4, 96, 384), z).reshape(16, 96, 384)
    natural = jnp.stack(
        [zz * 4 + (yy ^ y) * 2 + (cc ^ c) for zz in range(4) for yy, cc in pair]
    )
    w_heads = permute_blocks(natural, heads_rows, low).reshape(1536, 384)

    def owns_out(i):
        return bit_of(i, BIT_ZL) == bit_of(i, BIT_X) ^ bit_of(i, BIT_ZH)

    out_owner = zl == x ^ zh
    side = x ^ zh
    near_block = swap(w_out, BIT_ZL, owns_out)
    near_block = jnp.where(out_owner, w_out, near_block)
    far_block = swap(near_block, BIT_ZH)
    kept_block = jnp.where(c == side, near_block, far_block)
    sent_block = jnp.where(c == side, far_block, near_block)
    other_block = swap(sent_block, BIT_C)
    w_out_heads = jnp.where(
        c == 0,
        jnp.concatenate([kept_block, other_block], axis=0),
        jnp.concatenate([other_block, kept_block], axis=0),
    )

    wanted_mlp = jnp.stack(
        [
            (x ^ c ^ jc) * 8 + (zl ^ jl) * 4 + (y ^ jy) * 2 + (c ^ jc)
            for jc in (0, 1)
            for jy, jl in pair
        ]
    )
    picked = pick_columns(wanted_mlp, w_gate, w_up, gain_rows_mlp, 256)
    traded = trade_blocks(picked.reshape(2, 2, 2, 96, 512), (BIT_C, BIT_Y, BIT_ZL))
    near_rows = traded.reshape(8, 96, 512)
    all_rows = jnp.concatenate([near_rows, swap(near_rows, BIT_ZH)], axis=0)
    natural_mlp = seq_at ^ jnp.arange(16, dtype=jnp.int32)
    w_both = permute_blocks(natural_mlp, all_rows, low).reshape(1536, 512)

    def owns_down(i):
        return bit_of(i, BIT_X) ^ bit_of(i, BIT_C) == bit_of(i, BIT_ZH)

    down_owner = (x ^ c) == zh
    w_rows = jnp.where(down_owner, w_down, swap(w_down, BIT_ZH, owns_down))

    grads_parts = gather_rows(cotangent[0], CUBE)

    pieces = jnp.stack(
        [piece_order[zz * 4 + (y ^ jy) * 2 + (c ^ jc)] for zz in range(4) for jy, jc in pair]
    )
    own_pieces = lax.dynamic_slice_in_dim(pieces, z * 4, 4)
    own_pos = (own_pieces[:, None] * 128 + jnp.arange(128, dtype=jnp.int32)[None, :]).reshape(512)
    frequency = rope_base ** (-jnp.arange(HEAD_DIM // 2, dtype=wide) * 2.0 / HEAD_DIM)
    angles = own_pos.astype(wide)[:, None] * frequency[None, :]
    cosine, sine = jnp.cos(angles), jnp.sin(angles)
    ids = jnp.concatenate([block_ids, swap(block_ids, BIT_X)], axis=0).reshape(2, 16, 128)
    chosen = (pieces[:, None] == jnp.arange(16, dtype=jnp.int32)[None, :]).astype(wide)
    key_blk = jnp.einsum(
        "kp,spr->skr", chosen, ids.astype(wide), precision=lax.Precision.HIGHEST
    )
    query_blk = lax.dynamic_slice_in_dim(key_blk, z * 4, 4, axis=1).reshape(2, 512, 1)
    key_blk = key_blk.reshape(2, 1, 2048)

    projected = by_sequence(
        [jnp.dot(part, w_heads, preferred_element_type=wide) for part in normed_parts]
    )
    turned = rotate_wide(projected[:, :, :288], cosine, sine, 3).astype(low)
    queries = turned[:, :, :2].transpose(0, 2, 1, 3)
    own_keys = turned[:, :, 2]
    own_values = projected[:, :, 288:].astype(low)
    sent_kv = jnp.concatenate(
        [own_keys[0], own_keys[1], own_values[0], own_values[1]], axis=1
    )
    all_kv = line_gather(sent_kv, z).reshape(2048, 4, HEAD_DIM).transpose(1, 0, 2)
    keys, values = all_kv[:2], all_kv[2:]
    attention, totals = attend_forward(
        queries, keys, values, query_blk, key_blk, score_scale
    )
    attended = by_arrival(attention.astype(low).transpose(0, 2, 1, 3).reshape(2, 512, 192))
    mixed = scatter_rows(
        [
            jnp.dot(part, w_out_heads, preferred_element_type=wide).astype(low)
            for part in attended
        ],
        SQUARE,
    )
    middle = residual + mixed

    scale_second = rms_scale(middle)
    normed_second = middle * scale_second
    mlp_parts = gather_rows(normed_second.astype(low), CUBE)
    out_terms, back_terms, grad_both_terms, grad_down_terms = [], [], [], []
    for rows, grads in zip(mlp_parts, grads_parts):
        both = jnp.dot(rows, w_both, preferred_element_type=wide)
        gate, up = both[:, :256], both[:, 256:]
        bend = jax.nn.sigmoid(gate)
        hidden = (gate * bend * up).astype(low)
        grad_hidden = times_back(grads, w_rows)
        grad_gate = (grad_hidden * up * bend * (1.0 + gate * (1.0 - bend))).astype(low)
        grad_up = (grad_hidden * gate * bend).astype(low)
        grad_both = jnp.concatenate([grad_gate, grad_up], axis=1)
        back_terms.append(times_back(grad_both, w_both).astype(low))
        out_terms.append(jnp.dot(hidden, w_rows, preferred_element_type=wide).astype(low))
        grad_both_terms.append(over_rows(rows, grad_both))
        grad_down_terms.append(over_rows(hidden, grads))
    scaled_second = scatter_rows(back_terms, CUBE)
    output = (middle + scatter_rows(out_terms, CUBE)).astype(low)
    upstream = cotangent[0].astype(wide)
    grad_middle = upstream + scale_second * (
        scaled_second
        - normed_second * jnp.mean(scaled_second * normed_second, axis=-1, keepdims=True)
    )

    middle_parts = gather_rows(grad_middle.astype(low), SQUARE)
    grad_attended = by_sequence([times_back(part, w_out_heads).astype(low) for part in middle_parts])
    grad_heads = grad_attended.reshape(2, 512, 2, HEAD_DIM).transpose(0, 2, 1, 3)
    grad_out_heads = sum(
        over_rows(left, right) for left, right in zip(attended, middle_parts)
    )
    grad_queries, grad_keys, grad_values = attend_backward(
        queries,
        keys,
        values,
        attention,
        grad_heads,
        totals,
        query_blk,
        key_blk,
        score_scale,
    )
    kv_terms = jnp.concatenate(
        [grad_keys[0], grad_keys[1], grad_values[0], grad_values[1]], axis=1
    ).astype(low)
    kv_own = line_scatter(kv_terms.reshape(4, 512, 384), z)
    kv_own = kv_own.reshape(512, 2, 2, HEAD_DIM)
    grad_key_pre = unrotate_wide(kv_own[:, 0].transpose(1, 0, 2), cosine, sine, 1)
    grad_value_pre = kv_own[:, 1].transpose(1, 0, 2)
    grad_query_pre = unrotate_wide(grad_queries.transpose(0, 2, 1, 3), cosine, sine, 2)
    grad_heads_pre = jnp.concatenate(
        [
            grad_query_pre.reshape(2, 512, 192),
            grad_key_pre.reshape(2, 512, 96),
            grad_value_pre,
        ],
        axis=2,
    ).astype(low)
    pre_parts = by_arrival(grad_heads_pre)
    scaled_first = scatter_rows(
        [times_back(part, w_heads).astype(low) for part in pre_parts], SQUARE
    )
    grad_inputs = grad_middle + scale_first * (
        scaled_first
        - normed_first * jnp.mean(scaled_first * normed_first, axis=-1, keepdims=True)
    )

    grad_heads_w = sum(over_rows(left, right) for left, right in zip(normed_parts, pre_parts))
    away = jnp.stack(
        [zz * 4 + (y ^ jy) * 2 + (c ^ jc) for zz in range(4) for jc, jy in pair]
    )
    terms = permute_blocks(away, grad_heads_w.reshape(16, 96, 384), low)
    mine = line_scatter(terms.reshape(4, 4, 96, 384), z).astype(low)
    held = trade_blocks(mine.reshape(2, 2, 96, 384), (BIT_C, BIT_Y)).reshape(4, 96, 384)
    held = jnp.concatenate([held, swap(held, BIT_X)], axis=0)
    home = jnp.stack(
        [
            (k2 ^ k1 ^ x) * 4 + (k0 ^ y) * 2 + (k1 ^ c)
            for k2 in (0, 1)
            for k1, k0 in pair
        ]
    )
    raw = permute_blocks(home, held, wide).transpose(1, 0, 2)
    own_heads = packed_rows(w_query, w_key, w_value)
    grad_gain_attn = jnp.sum(raw * own_heads, axis=(1, 2))
    raw = raw * gain_rows_attn[:, :, None]
    grad_w_query = raw[:, :, :192].reshape(96, 1536)
    grad_w_key = raw[:, :, 192:288].reshape(96, 768)
    grad_w_value = raw[:, :, 288:].reshape(96, 768)

    first_half, second_half = grad_out_heads[:96].astype(low), grad_out_heads[96:].astype(low)
    kept = jnp.where(c == 0, first_half, second_half)
    arrived = swap(jnp.where(c == 0, second_half, first_half), BIT_C)
    stays = jnp.where(c == side, kept, arrived)
    leaves = jnp.where(c == side, arrived, kept)
    total = (stays.astype(wide) + swap(leaves, BIT_ZH).astype(wide)).astype(low)
    total = total.astype(wide) + swap(total, BIT_ZL, lambda i: not owns_out(i)).astype(wide)
    grad_w_out = jnp.where(
        out_owner, total, swap(total.astype(low), BIT_X, owns_out).astype(wide)
    )

    grad_down = sum(grad_down_terms)
    total = grad_down + swap(
        grad_down.astype(low), BIT_ZH, lambda i: not owns_down(i)
    ).astype(wide)
    grad_w_down = jnp.where(
        down_owner, total, swap(total.astype(low), BIT_X, owns_down).astype(wide)
    )

    grad_both_w = sum(grad_both_terms)
    away_mlp = jnp.stack(
        [
            seq_at ^ (jh * 8 + jl * 4 + jy * 2 + jc)
            for jh in (0, 1)
            for jc in (0, 1)
            for jy, jl in pair
        ]
    )
    terms = permute_blocks(away_mlp, grad_both_w.reshape(16, 96, 512), low)
    arrived = swap(terms[8:], BIT_ZH)
    mine = (terms[:8].astype(wide) + arrived.astype(wide)).astype(low)
    held = trade_blocks(mine.reshape(2, 2, 2, 96, 512), (BIT_C, BIT_Y, BIT_ZL))
    held = held.reshape(8, 96, 512)
    held = jnp.concatenate([held, swap(held, BIT_X)], axis=0)
    home_mlp = jnp.stack(
        [
            (h ^ cc ^ x) * 8 + (ll ^ zl) * 4 + (yy ^ y) * 2 + (cc ^ c)
            for h in (0, 1)
            for ll in (0, 1)
            for yy, cc in pair
        ]
    )
    grad_w_gate, grad_w_up = spread_columns(home_mlp, held, gain_rows_mlp, 256)
    grad_gain_mlp = (
        jnp.sum(
            grad_w_gate * w_gate.astype(wide) + grad_w_up * w_up.astype(wide), axis=1
        )
        / gain_rows_mlp[:, 0]
    )
    return (
        output[None],
        grad_inputs.astype(low)[None],
        grad_w_query,
        grad_w_key,
        grad_w_value,
        grad_w_out,
        grad_w_gate,
        grad_w_up,
        grad_w_down,
        grad_gain_attn,
        grad_gain_mlp,
    )


def packed_rows(w_query, w_key, w_value):
    return jnp.concatenate(
        [w_query.reshape(96, 8, 192), w_key.reshape(96, 8, 96), w_value.reshape(96, 8, 96)],
        axis=2,
    ).astype(jnp.float32)


def ring_plan(
    inputs,
    cotangent,
    block_ids,
    piece_order,
    w_query,
    w_key,
    w_value,
    w_out,
    w_gate,
    w_up,
    w_down,
    gain_attn,
    gain_mlp,
):
    shards = (w_query, w_key, w_value, w_out, w_gate, w_up, w_down, gain_attn, gain_mlp)
    (
        full_query,
        full_key,
        full_value,
        full_out,
        full_gate,
        full_up,
        full_down,
        gain_one,
        gain_two,
    ) = (
        lax.all_gather(shards[0], "seq", axis=0, tiled=True),
        lax.all_gather(shards[1], "seq", axis=0, tiled=True),
        lax.all_gather(shards[2], "seq", axis=0, tiled=True),
        lax.all_gather(shards[3], "seq", axis=0, tiled=True),
        lax.all_gather(shards[4], "seq", axis=0, tiled=True),
        lax.all_gather(shards[5], "seq", axis=0, tiled=True),
        lax.all_gather(shards[6], "seq", axis=0, tiled=True),
        lax.all_gather(shards[7], "seq", axis=0, tiled=True),
        lax.all_gather(shards[8], "seq", axis=0, tiled=True),
    )
    seq_count, tok_rows, model_width = inputs.shape
    row_count = seq_count * tok_rows
    head_count = HEADS
    kv_heads = KV_HEADS
    head_dim = HEAD_DIM
    groups = head_count // kv_heads
    kv_width = kv_heads * head_dim
    q_width = head_count * head_dim
    score_scale = head_dim ** (-0.5)
    own_first = jnp.take(piece_order, lax.axis_index("seq")) * tok_rows
    local_pos = own_first + jnp.arange(tok_rows, dtype=jnp.int32)
    cosine_table, sine_table = rotary_tables(local_pos, head_dim)
    query_blk = jnp.take(block_ids, local_pos, axis=1)

    def key_positions(key_count):
        stored = jnp.arange(key_count, dtype=jnp.int32)
        return jnp.take(piece_order, stored // tok_rows) * tok_rows + stored % tok_rows

    residual = inputs.reshape(row_count, model_width).astype(jnp.float32)
    gain_first = gain_one.astype(jnp.float32)
    gain_second = gain_two.astype(jnp.float32)
    scale_first = rms_scale(residual)
    normed_attn = (residual * scale_first * gain_first).astype(jnp.bfloat16)
    query_pre = jnp.dot(normed_attn, full_query, preferred_element_type=jnp.float32)
    key_pre = jnp.dot(normed_attn, full_key, preferred_element_type=jnp.float32)
    value_pre = jnp.dot(normed_attn, full_value, preferred_element_type=jnp.float32)
    queries = rotate(
        query_pre.reshape(seq_count, tok_rows, head_count, head_dim), cosine_table, sine_table
    ).astype(jnp.bfloat16)
    key_rot = rotate(
        key_pre.reshape(seq_count, tok_rows, kv_heads, head_dim), cosine_table, sine_table
    ).astype(jnp.bfloat16)
    values = value_pre.astype(jnp.bfloat16)
    kv_local = jnp.concatenate(
        [
            key_rot.reshape(seq_count, tok_rows, kv_width),
            values.reshape(seq_count, tok_rows, kv_width),
        ],
        axis=2,
    )
    query_grouped = queries.reshape(seq_count, tok_rows, kv_heads, groups, head_dim)
    start_max = jnp.full((seq_count, kv_heads, groups, tok_rows), masked_score, jnp.float32)
    start_sum = jnp.zeros((seq_count, kv_heads, groups, tok_rows), jnp.float32)
    start_acc = jnp.zeros((seq_count, kv_heads, groups, tok_rows, head_dim), jnp.float32)
    state_in = (start_max, start_sum, start_acc)
    key_piece = lax.all_gather(kv_local, "seq", axis=1, tiled=True)
    key_count = key_piece.shape[1]
    block_rows = key_block_rows(key_count)
    key_pos = key_positions(key_count)
    member = 0
    key_blk = jnp.take(block_ids[member], key_pos).reshape(key_count // block_rows, block_rows)
    kv_rows = key_piece[member].reshape(key_count // block_rows, block_rows, 2 * kv_width)
    own_query = query_grouped[member]
    own_blocks = query_blk[member]

    def forward_key_step(running, block_in):
        kv_block, blk_block = block_in
        key_part = kv_block[:, :kv_width].reshape(block_rows, kv_heads, head_dim)
        value_part = kv_block[:, kv_width:].reshape(block_rows, kv_heads, head_dim)
        running = forward_block(
            running, own_query, own_blocks, key_part, value_part, blk_block, score_scale
        )
        return (running, None)

    running, unused = lax.scan(
        forward_key_step,
        (state_in[0][member], state_in[1][member], state_in[2][member]),
        (kv_rows, key_blk),
    )
    results = [running]
    row_max = jnp.stack([entry[0] for entry in results])
    row_sum = jnp.stack([entry[1] for entry in results])
    running_sum = jnp.stack([entry[2] for entry in results])
    log_total = row_max + jnp.log(row_sum)
    attention = running_sum / row_sum[..., None]
    attended = (
        jnp.transpose(attention, (0, 3, 1, 2, 4)).reshape(row_count, q_width).astype(jnp.bfloat16)
    )
    middle = residual + jnp.dot(attended, full_out, preferred_element_type=jnp.float32)
    scale_second = rms_scale(middle)
    normed_mlp = (middle * scale_second * gain_second).astype(jnp.bfloat16)
    gate_value = jnp.dot(normed_mlp, full_gate, preferred_element_type=jnp.float32)
    upward = jnp.dot(normed_mlp, full_up, preferred_element_type=jnp.float32)
    sigmoid_gate = jax.nn.sigmoid(gate_value)
    hidden = (gate_value * sigmoid_gate * upward).astype(jnp.bfloat16)
    output = (middle + jnp.dot(hidden, full_down, preferred_element_type=jnp.float32)).astype(
        jnp.bfloat16
    )
    (
        full_query,
        full_key,
        full_value,
        full_out,
        full_gate,
        full_up,
        full_down,
        gain_one,
        gain_two,
    ) = (
        lax.all_gather(shards[0], "seq", axis=0, tiled=True),
        lax.all_gather(shards[1], "seq", axis=0, tiled=True),
        lax.all_gather(shards[2], "seq", axis=0, tiled=True),
        lax.all_gather(shards[3], "seq", axis=0, tiled=True),
        lax.all_gather(shards[4], "seq", axis=0, tiled=True),
        lax.all_gather(shards[5], "seq", axis=0, tiled=True),
        lax.all_gather(shards[6], "seq", axis=0, tiled=True),
        lax.all_gather(shards[7], "seq", axis=0, tiled=True),
        lax.all_gather(shards[8], "seq", axis=0, tiled=True),
    )
    gain_first = gain_one.astype(jnp.float32)
    gain_second = gain_two.astype(jnp.float32)
    upstream = cotangent.reshape(row_count, model_width)
    grad_down = over_rows(hidden, upstream)
    grad_hidden = times_back(upstream, full_down)
    grad_gate = (
        grad_hidden * upward * sigmoid_gate * (1.0 + gate_value * (1.0 - sigmoid_gate))
    ).astype(jnp.bfloat16)
    grad_upward = (grad_hidden * gate_value * sigmoid_gate).astype(jnp.bfloat16)
    grad_w_gate = over_rows(normed_mlp, grad_gate)
    grad_w_up = over_rows(normed_mlp, grad_upward)
    grad_normed_mlp = times_back(grad_gate, full_gate) + times_back(grad_upward, full_up)
    grad_mid_norm, grad_gain_mlp = norm_back(grad_normed_mlp, middle, scale_second, gain_second)
    grad_middle = upstream.astype(jnp.float32) + grad_mid_norm
    grad_middle_low = grad_middle.astype(jnp.bfloat16)
    grad_w_out = over_rows(attended, grad_middle_low)
    grad_attended = times_back(grad_middle_low, full_out).astype(jnp.bfloat16)
    grad_heads = jnp.transpose(
        grad_attended.reshape(seq_count, tok_rows, kv_heads, groups, head_dim), (0, 2, 3, 1, 4)
    )
    delta_rows = jnp.sum(grad_heads.astype(jnp.float32) * attention, axis=-1)
    start_query = jnp.zeros((seq_count, kv_heads, groups, tok_rows, head_dim), jnp.float32)
    start_kv = jnp.zeros((seq_count, block_ids.shape[1], 2 * kv_width), jnp.float32)
    state_in = (start_query, start_kv)
    key_piece = lax.all_gather(kv_local, "seq", axis=1, tiled=True)
    key_count = key_piece.shape[1]
    backward_block_rows = key_block_rows(key_count)
    key_pos = key_positions(key_count)
    member = 0
    key_blk = jnp.take(block_ids[member], key_pos).reshape(
        key_count // backward_block_rows, backward_block_rows
    )
    kv_rows = key_piece[member].reshape(
        key_count // backward_block_rows, backward_block_rows, 2 * kv_width
    )
    backward_own_query = query_grouped[member]
    backward_own_blocks = query_blk[member]
    own_total = log_total[member]
    own_grads = grad_heads[member]
    own_delta = delta_rows[member]

    def backward_key_step(grad_query, block_in):
        kv_block, blk_block = block_in
        key_part = kv_block[:, :kv_width].reshape(backward_block_rows, kv_heads, head_dim)
        value_part = kv_block[:, kv_width:].reshape(backward_block_rows, kv_heads, head_dim)
        result = backward_block(
            grad_query,
            backward_own_query,
            backward_own_blocks,
            key_part,
            value_part,
            blk_block,
            own_total,
            own_grads,
            own_delta,
            score_scale,
        )
        return (result[0], (result[1], result[2]))

    grad_query, key_grads = lax.scan(backward_key_step, state_in[0][member], (kv_rows, key_blk))
    fresh = jnp.concatenate(
        [key_grads[0].reshape(key_count, kv_width), key_grads[1].reshape(key_count, kv_width)],
        axis=1,
    )
    query_grads = [grad_query]
    kv_grads = [fresh]
    grad_query_all = jnp.stack(query_grads)
    grad_kv_all = jnp.stack(kv_grads)
    grad_kv_own = lax.psum_scatter(grad_kv_all, "seq", scatter_dimension=1, tiled=True)
    grad_query_rows = jnp.transpose(grad_query_all, (0, 3, 1, 2, 4)).reshape(
        seq_count, tok_rows, head_count, head_dim
    )
    grad_query_pre = (
        unrotate(grad_query_rows, cosine_table, sine_table)
        .reshape(row_count, q_width)
        .astype(jnp.bfloat16)
    )
    grad_key_rows = grad_kv_own[:, :, :kv_width].reshape(seq_count, tok_rows, kv_heads, head_dim)
    grad_key_pre = (
        unrotate(grad_key_rows, cosine_table, sine_table)
        .reshape(row_count, kv_width)
        .astype(jnp.bfloat16)
    )
    grad_value_pre = grad_kv_own[:, :, kv_width:].reshape(row_count, kv_width).astype(jnp.bfloat16)
    grad_w_query = over_rows(normed_attn, grad_query_pre)
    grad_w_key = over_rows(normed_attn, grad_key_pre)
    grad_w_value = over_rows(normed_attn, grad_value_pre)
    grad_normed_attn = (
        times_back(grad_query_pre, full_query)
        + times_back(grad_key_pre, full_key)
        + times_back(grad_value_pre, full_value)
    )
    grad_in_norm, grad_gain_attn = norm_back(grad_normed_attn, residual, scale_first, gain_first)
    grad_inputs = (
        (grad_middle + grad_in_norm).astype(jnp.bfloat16).reshape(seq_count, tok_rows, model_width)
    )
    terms = (
        grad_w_query,
        grad_w_key,
        grad_w_value,
        grad_w_out,
        grad_w_gate,
        grad_w_up,
        grad_down,
        grad_gain_attn,
        grad_gain_mlp,
    )
    shares = (
        lax.psum_scatter(terms[0], "seq", scatter_dimension=0, tiled=True),
        lax.psum_scatter(terms[1], "seq", scatter_dimension=0, tiled=True),
        lax.psum_scatter(terms[2], "seq", scatter_dimension=0, tiled=True),
        lax.psum_scatter(terms[3], "seq", scatter_dimension=0, tiled=True),
        lax.psum_scatter(terms[4], "seq", scatter_dimension=0, tiled=True),
        lax.psum_scatter(terms[5], "seq", scatter_dimension=0, tiled=True),
        lax.psum_scatter(terms[6], "seq", scatter_dimension=0, tiled=True),
        lax.psum_scatter(terms[7], "seq", scatter_dimension=0, tiled=True),
        lax.psum_scatter(terms[8], "seq", scatter_dimension=0, tiled=True),
    )
    totals = (
        lax.psum(shares[0].astype(jnp.bfloat16), "grp").astype(jnp.float32),
        lax.psum(shares[1].astype(jnp.bfloat16), "grp").astype(jnp.float32),
        lax.psum(shares[2].astype(jnp.bfloat16), "grp").astype(jnp.float32),
        lax.psum(shares[3].astype(jnp.bfloat16), "grp").astype(jnp.float32),
        lax.psum(shares[4].astype(jnp.bfloat16), "grp").astype(jnp.float32),
        lax.psum(shares[5].astype(jnp.bfloat16), "grp").astype(jnp.float32),
        lax.psum(shares[6].astype(jnp.bfloat16), "grp").astype(jnp.float32),
        lax.psum(shares[7].astype(jnp.bfloat16), "grp").astype(jnp.float32),
        lax.psum(shares[8].astype(jnp.bfloat16), "grp").astype(jnp.float32),
    )
    return (
        output.reshape(seq_count, tok_rows, model_width),
        grad_inputs,
        totals[0],
        totals[1],
        totals[2],
        totals[3],
        totals[4],
        totals[5],
        totals[6],
        totals[7],
        totals[8],
    )


def solution(mesh):
    local = ring_plan
    if (mesh.shape["grp"], mesh.shape["seq"]) == (2, 16):
        local = cube_plan
    return jax.shard_map(
        local,
        mesh=mesh,
        in_specs=(
            P("grp", "seq", None),
            P("grp", "seq", None),
            P("grp", None),
            P(),
            P("seq", None),
            P("seq", None),
            P("seq", None),
            P("seq", None),
            P("seq", None),
            P("seq", None),
            P("seq", None),
            P("seq"),
            P("seq"),
        ),
        out_specs=(
            P("grp", "seq", None),
            P("grp", "seq", None),
            P("seq", None),
            P("seq", None),
            P("seq", None),
            P("seq", None),
            P("seq", None),
            P("seq", None),
            P("seq", None),
            P("seq"),
            P("seq"),
        ),
        check_vma=False,
    )
```

```python
import functools

import jax
import jax.numpy as jnp
from jax import lax
from jax.experimental import pallas as pl
from jax.experimental.pallas import tpu as pltpu
from jax.sharding import PartitionSpec as P

HEADS = 16
KV_HEADS = 8
HEAD_DIM = 96


eps_norm = 1e-05
rope_base = 100000.0
masked_score = -1e30


def rms_scale(rows_in):
    return lax.rsqrt(jnp.mean(rows_in * rows_in, axis=-1, keepdims=True) + eps_norm)


def norm_back(grad_normed, rows_in, row_scale, gain_row):
    normed = rows_in * row_scale
    grad_gain = jnp.sum(grad_normed * normed, axis=0)
    scaled_grad = grad_normed * gain_row
    grad_rows = row_scale * (
        scaled_grad - normed * jnp.mean(scaled_grad * normed, axis=-1, keepdims=True)
    )
    return (grad_rows, grad_gain)


def rotary_tables(positions, head_dim):
    half_dim = head_dim // 2
    frequency = rope_base ** (-jnp.arange(half_dim, dtype=jnp.float32) * 2.0 / head_dim)
    angles = positions.astype(jnp.float32)[:, None] * frequency[None, :]
    return (jnp.cos(angles)[:, None, :], jnp.sin(angles)[:, None, :])


def rotate(vectors, cosine_table, sine_table):
    half_dim = vectors.shape[-1] // 2
    front_half = vectors[..., :half_dim]
    back_half = vectors[..., half_dim:]
    return jnp.concatenate(
        [
            front_half * cosine_table - back_half * sine_table,
            back_half * cosine_table + front_half * sine_table,
        ],
        axis=-1,
    )


def unrotate(grads, cosine_table, sine_table):
    half_dim = grads.shape[-1] // 2
    front_half = grads[..., :half_dim]
    back_half = grads[..., half_dim:]
    return jnp.concatenate(
        [
            front_half * cosine_table + back_half * sine_table,
            back_half * cosine_table - front_half * sine_table,
        ],
        axis=-1,
    )


def over_rows(left, right):
    return lax.dot_general(
        left, right, (((0,), (0,)), ((), ())), preferred_element_type=jnp.float32
    )


def times_back(left, right):
    return lax.dot_general(
        left, right, (((1,), (1,)), ((), ())), preferred_element_type=jnp.float32
    )


def key_block_rows(key_count):
    block_rows = min(key_count, 1024)
    return block_rows


def masked_scores(query_part, key_part, query_blocks, key_blocks, score_scale):
    scores = (
        jnp.einsum("qkgd,tkd->kgqt", query_part, key_part, preferred_element_type=jnp.float32)
        * score_scale
    )
    allowed = key_blocks[None, None, None, :] <= query_blocks[None, None, :, None]
    return jnp.where(allowed, scores, masked_score)


def forward_block(running, query_part, query_blocks, key_part, value_part, key_blocks, score_scale):
    row_max, row_sum, running_sum = running
    scores = masked_scores(query_part, key_part, query_blocks, key_blocks, score_scale)
    new_max = jnp.maximum(row_max, jnp.max(scores, axis=-1))
    likely = jnp.exp(scores - new_max[..., None])
    fading = jnp.exp(row_max - new_max)
    row_sum = row_sum * fading + jnp.sum(likely, axis=-1)
    running_sum = running_sum * fading[..., None] + jnp.einsum(
        "kgqt,tkd->kgqd",
        likely.astype(jnp.bfloat16),
        value_part,
        preferred_element_type=jnp.float32,
    )
    return (new_max, row_sum, running_sum)


def backward_block(
    grad_query,
    query_part,
    query_blocks,
    key_part,
    value_part,
    key_blocks,
    log_total,
    grad_heads,
    delta_rows,
    score_scale,
):
    scores = masked_scores(query_part, key_part, query_blocks, key_blocks, score_scale)
    chance = jnp.exp(scores - log_total[..., None])
    grad_value = jnp.einsum(
        "kgqt,kgqd->tkd",
        chance.astype(jnp.bfloat16),
        grad_heads,
        preferred_element_type=jnp.float32,
    )
    grad_chance = jnp.einsum(
        "kgqd,tkd->kgqt", grad_heads, value_part, preferred_element_type=jnp.float32
    )
    grad_scores = (chance * (grad_chance - delta_rows[..., None])).astype(jnp.bfloat16)
    grad_query = (
        grad_query
        + jnp.einsum("kgqt,tkd->kgqd", grad_scores, key_part, preferred_element_type=jnp.float32)
        * score_scale
    )
    grad_key = (
        jnp.einsum("kgqt,qkgd->tkd", grad_scores, query_part, preferred_element_type=jnp.float32)
        * score_scale
    )
    return (grad_query, grad_key, grad_value)


BIT_X, BIT_ZH, BIT_ZL, BIT_Y, BIT_C = 16, 8, 4, 2, 1
DEVICES = 32
AXES = ("grp", "seq")
THIRDS = (
    (BIT_X, BIT_Y, BIT_ZL),
    (BIT_Y, BIT_ZL, BIT_X),
    (BIT_ZL, BIT_X, BIT_Y),
)
HALVES = (
    (BIT_ZL, BIT_X, BIT_Y),
    (BIT_ZL, BIT_Y, BIT_X),
)
log2_e = 1.4426950408889634
VMEM_LIMIT = 48 * 1024 * 1024
low, wide = jnp.bfloat16, jnp.float32


def swap(value, mask, sends=None):
    pairs = [(i, i ^ mask) for i in range(DEVICES) if sends is None or sends(i)]
    return lax.ppermute(value, AXES, pairs)


def bit_of(index, mask):
    return 1 if index & mask else 0


def sync(*values):
    return lax.optimization_barrier(values)


def gather_start(rows, orders):
    width = rows.shape[1] // len(orders)
    return [rows[None, :, i * width : (i + 1) * width] for i in range(len(orders))]


def gather_next(parts, orders, step):
    return [
        jnp.concatenate([held, swap(held, order[step])], axis=0)
        for held, order in zip(parts, orders)
    ]


def gather_last(parts):
    return [(held, swap(held, BIT_C)) for held in parts]


def scatter_start(pairs):
    return [(kept, swap(sent, BIT_C)) for kept, sent in pairs]


def scatter_next(sums, orders, step):
    result = []
    for (kept, arrived), order in zip(sums, orders):
        half = kept.shape[0] // 2
        sent = (kept[half:].astype(wide) + arrived[half:].astype(wide)).astype(low)
        kept = (kept[:half].astype(wide) + arrived[:half].astype(wide)).astype(low)
        result.append((kept, swap(sent, order[step])))
    return result


def scatter_last(sums):
    return [kept.astype(wide) + arrived.astype(wide) for kept, arrived in sums]


def cube_groups():
    return [
        [gx * 16 + zh * 8 + rest for gx in (0, 1) for rest in range(8)] for zh in (0, 1)
    ]


def cube_gather(rows):
    return lax.all_gather(rows, AXES, axis=0, tiled=True, axis_index_groups=cube_groups())


def cube_scatter(rows):
    return lax.psum_scatter(
        rows, AXES, scatter_dimension=0, tiled=True, axis_index_groups=cube_groups()
    )


def trade_block(blocks, axis, mask):
    keep = lax.index_in_dim(blocks, 0, axis, keepdims=False)
    send = lax.index_in_dim(blocks, 1, axis, keepdims=False)
    return jnp.stack([keep, swap(send, mask)])


def trade_blocks(blocks, masks):
    for axis, mask in enumerate(masks):
        keep = lax.index_in_dim(blocks, 0, axis, keepdims=False)
        send = lax.index_in_dim(blocks, 1, axis, keepdims=False)
        blocks = jnp.stack([keep, swap(send, mask)])
    return blocks


def block_at(order):
    place = {BIT_X: 2, BIT_Y: 1, BIT_ZL: 0}

    def find(g):
        return sum(((g >> place[mask]) & 1) << rank for rank, mask in enumerate(order))

    return find


def row_specs(orders, step):
    width = 1536 // len(orders)
    specs = []
    for order in orders:
        find = block_at(order)
        for _ in range(2):
            specs.append(
                pl.BlockSpec((1, 128, width), lambda *a, find=find: (find(step(*a)), 0, 0))
            )
    return specs


def row_shapes(orders):
    width = 1536 // len(orders)
    return [jax.ShapeDtypeStruct((8, 128, width), low)] * (2 * len(orders))


def flat(pairs):
    return [array for pair in pairs for array in pair]


def paired(arrays):
    return [(arrays[i], arrays[i + 1]) for i in range(0, len(arrays), 2)]


def load_rows(refs):
    return jnp.concatenate(
        [
            jnp.concatenate([refs[i][0], refs[i + 1][0]], axis=0)
            for i in range(0, len(refs), 2)
        ],
        axis=1,
    )


def store_rows(refs, rows):
    width = 1536 // (len(refs) // 2)
    for i in range(0, len(refs), 2):
        columns = slice((i // 2) * width, (i // 2 + 1) * width)
        refs[i][0] = rows[:128, columns].astype(low)
        refs[i + 1][0] = rows[128:, columns].astype(low)


def whole_spec(shape):
    return pl.BlockSpec(shape, lambda *a: (0,) * len(shape))


def kernel_call(body, grid, in_specs, out_specs, out_shape, scratch, flops, moved, args, exps=0):
    return pl.pallas_call(
        body,
        out_shape=out_shape,
        grid_spec=pltpu.PrefetchScalarGridSpec(
            num_scalar_prefetch=1,
            grid=grid,
            in_specs=in_specs,
            out_specs=out_specs,
            scratch_shapes=scratch,
        ),
        compiler_params=pltpu.CompilerParams(vmem_limit_bytes=VMEM_LIMIT),
        cost_estimate=pl.CostEstimate(
            flops=flops, bytes_accessed=moved, transcendentals=exps
        ),
    )(*args)


def head_columns(w_query, w_key, w_value, head):
    shared = w_value if head % 2 else w_key
    start = (head // 2) * 96
    return w_query[:, head * 96 : head * 96 + 96], shared[:, start : start + 96]


def pick_heads(table, w_query, w_key, w_value, gain_rows):
    def body(table_ref, q_ref, k_ref, v_ref, gain_ref, out_ref, scr):
        gain = gain_ref[...]
        for head in range(16):
            one, two = head_columns(q_ref, k_ref, v_ref, head)
            scr[head, :, :96] = (one.astype(wide) * gain).astype(low)
            scr[head, :, 96:] = (two.astype(wide) * gain).astype(low)
        for i in range(8):
            out_ref[i] = scr[table_ref[i]]

    args = (w_query, w_key, w_value, gain_rows)
    return kernel_call(
        body,
        (1,),
        [whole_spec(a.shape) for a in args],
        whole_spec((8, 96, 192)),
        jax.ShapeDtypeStruct((8, 96, 192), low),
        [pltpu.VMEM((16, 96, 192), low)],
        0,
        1024 * 1024,
        (table, *args),
    )


def pick_columns(table, first, second, gain_rows):
    rows = first.shape[0]

    def body(table_ref, first_ref, second_ref, gain_ref, out_ref):
        gain = gain_ref[...]
        for i in range(8):
            columns = pl.ds(pl.multiple_of(table_ref[i] * 256, 256), 256)
            out_ref[i, :, :256] = (first_ref[:, columns].astype(wide) * gain).astype(low)
            out_ref[i, :, 256:] = (second_ref[:, columns].astype(wide) * gain).astype(low)

    shape = (8, rows, 512)
    return kernel_call(
        body,
        (1,),
        [whole_spec(first.shape), whole_spec(second.shape), whole_spec(gain_rows.shape)],
        whole_spec(shape),
        jax.ShapeDtypeStruct(shape, low),
        [],
        0,
        4 * first.size,
        (table, first, second, gain_rows),
    )


def assemble_rows(table, *groups):
    rows, width = groups[0].shape[1:]

    def body(table_ref, *refs):
        out_ref, i = refs[-1], 0
        for ref in refs[:-1]:
            for k in range(ref.shape[0]):
                start = pl.multiple_of(table_ref[i] * rows, rows)
                out_ref[pl.ds(start, rows), :] = ref[k]
                i += 1

    shape = (16 * rows, width)
    return kernel_call(
        body,
        (1,),
        [whole_spec(group.shape) for group in groups],
        whole_spec(shape),
        jax.ShapeDtypeStruct(shape, low),
        [],
        0,
        64 * rows * width,
        (table, *groups),
    )


def spread_columns(table, near, far, gain_rows, first, second):
    rows = near.shape[1]

    def body(table_ref, near_ref, far_ref, gain_ref, w1_ref, w2_ref, g1_ref, g2_ref, sum_ref):
        gain = gain_ref[...]
        total = jnp.zeros((rows, 256), wide)
        for i in range(16):
            source = near_ref if i < 8 else far_ref
            columns = pl.ds(pl.multiple_of(table_ref[i] * 256, 256), 256)
            block = source[i % 8].astype(wide)
            one, two = block[:, :256], block[:, 256:]
            total += one * w1_ref[:, columns].astype(wide)
            total += two * w2_ref[:, columns].astype(wide)
            g1_ref[:, columns] = one * gain
            g2_ref[:, columns] = two * gain
        sum_ref[...] = jnp.sum(total, axis=1, keepdims=True)

    return kernel_call(
        body,
        (1,),
        [whole_spec(a.shape) for a in (near, far, gain_rows, first, second)],
        [whole_spec(first.shape), whole_spec(second.shape), whole_spec((rows, 1))],
        [
            jax.ShapeDtypeStruct(first.shape, wide),
            jax.ShapeDtypeStruct(second.shape, wide),
            jax.ShapeDtypeStruct((rows, 1), wide),
        ],
        [],
        0,
        6 * 2 * first.size,
        (table, near, far, gain_rows, first, second),
    )


def spread_heads(table, near, far, w_query, w_key, w_value, gain_rows):
    def body(
        table_ref, near_ref, far_ref, q_ref, k_ref, v_ref, gain_ref, *rest
    ):
        gq_ref, gk_ref, gv_ref, sum_ref, scr = rest
        gain = gain_ref[...]
        for i in range(16):
            source = near_ref if i < 8 else far_ref
            scr[table_ref[i]] = source[i % 8].astype(wide)
        total = jnp.zeros((96, 96), wide)
        for head in range(16):
            one, two = head_columns(q_ref, k_ref, v_ref, head)
            block = scr[head]
            first, second = block[:, :96], block[:, 96:]
            total += first * one.astype(wide) + second * two.astype(wide)
            gq_ref[:, head * 96 : head * 96 + 96] = first * gain
            shared = gv_ref if head % 2 else gk_ref
            start = (head // 2) * 96
            shared[:, start : start + 96] = second * gain
        sum_ref[...] = jnp.sum(total, axis=1, keepdims=True)

    args = (near, far, w_query, w_key, w_value, gain_rows)
    shapes = [w_query.shape, w_key.shape, w_value.shape, (96, 1)]
    return kernel_call(
        body,
        (1,),
        [whole_spec(a.shape) for a in args],
        [whole_spec(shape) for shape in shapes],
        [jax.ShapeDtypeStruct(shape, wide) for shape in shapes],
        [pltpu.VMEM((16, 96, 192), wide)],
        0,
        4 * 1024 * 1024,
        (table, *args),
    )


def turn(rows, cosine, sine):
    front, back = rows[:48], rows[48:]
    return jnp.concatenate([front * cosine - back * sine, back * cosine + front * sine], axis=0)


def turn_back(rows, cosine, sine):
    front, back = rows[:48], rows[48:]
    return jnp.concatenate([front * cosine + back * sine, back * cosine - front * sine], axis=0)


def align_rows(core, rows):
    turned = jnp.concatenate([rows[128:], rows[:128]], axis=0)
    return jnp.where(core == 0, rows, turned)


def align(core, columns):
    turned = jnp.concatenate([columns[:, 128:], columns[:, :128]], axis=1)
    return jnp.where(core == 0, columns, turned)


def table_specs():
    return [pl.BlockSpec((48, 256), lambda g, t: (0, g % 4))] * 4


def cube_spec():
    return pl.BlockSpec((256, 1536), lambda g, t: (t[g], 0))


def project(at, normed, w_heads, tables):
    def body(at_ref, rows_ref, w_ref, cos_ref, sin_ref, cos2_ref, sin2_ref, q_ref, own_ref, wt_scr):
        @pl.when(pl.program_id(0) == 0)
        def _():
            wt_scr[...] = w_ref[...].astype(wide).T.astype(low)

        made = times_back(wt_scr[...], rows_ref[...])
        q_ref[0] = turn(made[:96], cos_ref[...], sin_ref[...]).astype(low)
        own_ref[0] = turn(made[96:], cos2_ref[...], sin2_ref[...]).astype(low)

    out_spec = pl.BlockSpec((1, 96, 256), lambda g, t: (g // 4, 0, g % 4))
    shape = jax.ShapeDtypeStruct((2, 96, 1024), low)
    return kernel_call(
        body,
        (8,),
        [cube_spec(), whole_spec((1536, 192))] + table_specs(),
        [out_spec, out_spec],
        [shape, shape],
        [pltpu.VMEM((192, 1536), low)],
        2 * 2048 * 1536 * 192,
        8 * 1024 * 1024,
        (at, normed, w_heads, *tables),
    )


def head_specs():
    kv = pl.BlockSpec((1, 96, 1024), lambda s, t, a: (s, 0, 0))
    other = pl.BlockSpec((1, 1, 96, 1024), lambda s, t, a: (0, s, 0, 0))
    other_far = pl.BlockSpec((1, 1, 96, 1024), lambda s, t, a: (1, s, 0, 0))
    return [kv, kv, other, other_far]


def key_and_value(core, own_ref, far_ref, other_ref, other_far_ref):
    mine = jnp.concatenate([own_ref[0], far_ref[0]], axis=1)
    theirs = jnp.concatenate([other_ref[0, 0], other_far_ref[0, 0]], axis=1)
    keyed = core == 0
    return jnp.where(keyed, mine, theirs), jnp.where(keyed, theirs, mine)


def masked(scores, key_column, query_ref, score_scale):
    return jnp.where(key_column <= query_ref[0], scores * (score_scale * log2_e), masked_score)


def attend_forward(at, queries, held, query_blk, key_blk, score_scale):
    def body(at_ref, q_ref, a_ref, b_ref, c_ref, d_ref, qb_ref, kb_ref, *rest):
        keep_ref, send_ref, att_ref, total_ref, k_scr, v_scr, kb_scr = rest

        @pl.when(pl.program_id(1) == 0)
        def _():
            key_part, value_part = key_and_value(at_ref[8], a_ref, b_ref, c_ref, d_ref)
            k_scr[...] = key_part.astype(wide).T.astype(low)
            v_scr[...] = value_part
            kb_scr[...] = jnp.broadcast_to(kb_ref[0], (128, 2048)).T[:, :1]

        scores = jnp.dot(k_scr[...], q_ref[0], preferred_element_type=wide)
        scores = masked(scores, kb_scr[...], qb_ref, score_scale)
        top = jnp.max(scores, axis=0, keepdims=True)
        likely = jnp.exp2(scores - top)
        column_sum = jnp.sum(likely, axis=0, keepdims=True)
        mixed = jnp.dot(v_scr[...], likely.astype(low), preferred_element_type=wide)
        mixed = mixed / column_sum
        att_ref[0] = mixed
        total_ref[0] = top + jnp.log(column_sum) * log2_e
        mixed = align(at_ref[8], mixed).astype(low)
        keep_ref[0] = mixed[:, :128]
        send_ref[0] = mixed[:, 128:]

    q_spec = pl.BlockSpec((1, 96, 256), lambda s, t, a: (s, 0, t))
    one_spec = pl.BlockSpec((1, 1, 256), lambda s, t, a: (s, 0, t))
    block_spec = pl.BlockSpec((1, 96, 128), lambda s, t, a: (s * 4 + t, 0, 0))
    return kernel_call(
        body,
        (2, 4),
        [q_spec]
        + head_specs()
        + [one_spec, pl.BlockSpec((1, 1, 2048), lambda s, t, a: (s, 0, 0))],
        [block_spec, block_spec, q_spec, one_spec],
        [
            jax.ShapeDtypeStruct((8, 96, 128), low),
            jax.ShapeDtypeStruct((8, 96, 128), low),
            jax.ShapeDtypeStruct((2, 96, 1024), wide),
            jax.ShapeDtypeStruct((2, 1, 1024), wide),
        ],
        [
            pltpu.VMEM((2048, 96), low),
            pltpu.VMEM((96, 2048), low),
            pltpu.VMEM((2048, 1), wide),
        ],
        4 * 2 * 1024 * 2048 * 96,
        12 * 1024 * 1024,
        (at, queries, *held, query_blk, key_blk),
        exps=2 * 1024 * 2048,
    )


def out_project(at, blocks, w_full, residual):
    def body(at_ref, in_ref, w_ref, x_ref, middle_ref, scale_ref, normed_ref, att_ref):
        for i in range(16):
            start = pl.multiple_of(at_ref[i] * 96, 96)
            att_ref[pl.ds(start, 96), :] = in_ref[i]
        rows = att_ref[...].astype(wide).T.astype(low)
        middle = x_ref[...] + jnp.dot(rows, w_ref[...], preferred_element_type=wide)
        scale = rms_scale(middle)
        middle_ref[...] = middle
        scale_ref[...] = scale
        normed_ref[...] = (middle * scale).astype(low)

    shapes = [
        jax.ShapeDtypeStruct((128, 1536), wide),
        jax.ShapeDtypeStruct((128, 1), wide),
        jax.ShapeDtypeStruct((128, 1536), low),
    ]
    return kernel_call(
        body,
        (1,),
        [whole_spec(a.shape) for a in (blocks, w_full, residual)],
        [whole_spec(shape.shape) for shape in shapes],
        shapes,
        [pltpu.VMEM((1536, 128), low)],
        2 * 128 * 1536 * 1536,
        6 * 1024 * 1024,
        (at, blocks, w_full, residual),
    )


def out_back(at, grad_out, sums, middle, scale, w_full):
    def body(at_ref, dy_ref, a_ref, b_ref, c_ref, x_ref, scale_ref, w_ref, *rest):
        middle_ref, low_ref, keep_ref, send_ref, scr = rest
        scaled = jnp.concatenate([a_ref[0], b_ref[0], c_ref[0]], axis=1)
        scale = scale_ref[...]
        normed = x_ref[...] * scale
        grad = dy_ref[...].astype(wide) + scale * (
            scaled - normed * jnp.mean(scaled * normed, axis=-1, keepdims=True)
        )
        middle_ref[...] = grad
        grad = grad.astype(low)
        low_ref[...] = grad
        scr[...] = times_back(w_ref[...], grad).astype(low)
        for i in range(8):
            start = pl.multiple_of(at_ref[i] * 96, 96)
            keep_ref[i] = scr[pl.ds(start, 96), :]
            start = pl.multiple_of(at_ref[8 + i] * 96, 96)
            send_ref[i] = scr[pl.ds(start, 96), :]

    args = (grad_out, *sums, middle, scale, w_full)
    shapes = [
        jax.ShapeDtypeStruct((128, 1536), wide),
        jax.ShapeDtypeStruct((128, 1536), low),
        jax.ShapeDtypeStruct((8, 96, 128), low),
        jax.ShapeDtypeStruct((8, 96, 128), low),
    ]
    return kernel_call(
        body,
        (1,),
        [whole_spec(a.shape) for a in args],
        [whole_spec(shape.shape) for shape in shapes],
        shapes,
        [pltpu.VMEM((1536, 128), low)],
        4 * 128 * 1536 * 1536,
        14 * 1024 * 1024,
        (at, *args),
    )


def attend_backward(
    at, queries, held, query_blk, key_blk, attention, totals, grad_blocks, tables, score_scale
):
    def body(at_ref, q_ref, a_ref, b_ref, c_ref, d_ref, qb_ref, kb_ref, *rest):
        att_ref, total_ref, cos_ref, sin_ref = rest[:4]
        own_ref, core_ref = rest[4:6]
        dq_ref, mine_ref, sent_ref = rest[6:9]
        k_scr, kt_scr, v_scr, dk_scr, dv_scr, kb_scr = rest[9:]
        tile = pl.program_id(1)

        @pl.when(tile == 0)
        def _():
            key_part, value_part = key_and_value(at_ref[8], a_ref, b_ref, c_ref, d_ref)
            kt_scr[...] = key_part
            kb_scr[...] = jnp.broadcast_to(kb_ref[0], (128, 2048)).T[:, :1]
            k_scr[...] = key_part.astype(wide).T.astype(low)
            v_scr[...] = value_part.astype(wide).T.astype(low)
            dk_scr[...] = jnp.zeros_like(dk_scr)
            dv_scr[...] = jnp.zeros_like(dv_scr)

        att = att_ref[0]
        grad_att = align(
            at_ref[8], jnp.concatenate([own_ref[0, 0], core_ref[0, 0]], axis=1).astype(wide)
        ).astype(low)
        delta = jnp.sum(grad_att.astype(wide) * att, axis=0, keepdims=True)
        scores = jnp.dot(k_scr[...], q_ref[0], preferred_element_type=wide)
        scores = masked(scores, kb_scr[...], qb_ref, score_scale)
        chance = jnp.exp2(scores - total_ref[0])
        dv_scr[...] += times_back(grad_att, chance.astype(low))
        grad_chance = jnp.dot(v_scr[...], grad_att, preferred_element_type=wide)
        grad_scores = (chance * (grad_chance - delta)).astype(low)
        grad_query = jnp.dot(kt_scr[...], grad_scores, preferred_element_type=wide)
        dq_ref[0] = turn_back(grad_query * score_scale, cos_ref[...], sin_ref[...]).astype(low)
        dk_scr[...] += times_back(q_ref[0], grad_scores)

        @pl.when(tile == 3)
        def _():
            grad_key = dk_scr[...] * score_scale
            grad_value = dv_scr[...]
            keyed = at_ref[8] == 0
            mine = jnp.where(keyed, grad_key, grad_value)
            sent = jnp.where(keyed, grad_value, grad_key)
            mine_ref[0, 0] = mine[:, :1024].astype(low)
            mine_ref[1, 0] = mine[:, 1024:].astype(low)
            sent_ref[0, 0] = sent[:, :1024].astype(low)
            sent_ref[1, 0] = sent[:, 1024:].astype(low)

    q_spec = pl.BlockSpec((1, 96, 256), lambda s, t, a: (s, 0, t))
    one_spec = pl.BlockSpec((1, 1, 256), lambda s, t, a: (s, 0, t))
    kv_out = pl.BlockSpec((2, 1, 96, 1024), lambda s, t, a: (0, s, 0, 0))
    angle = pl.BlockSpec((48, 256), lambda s, t, a: (0, t))

    def block_of(s, t):
        return (t & 1) * 4 + (t >> 1) * 2 + s

    return kernel_call(
        body,
        (2, 4),
        [q_spec]
        + head_specs()
        + [
            one_spec,
            pl.BlockSpec((1, 1, 2048), lambda s, t, a: (s, 0, 0)),
            q_spec,
            one_spec,
            angle,
            angle,
            pl.BlockSpec((1, 1, 96, 128), lambda s, t, a: (block_of(s, t), 0, 0, 0)),
            pl.BlockSpec((1, 1, 96, 128), lambda s, t, a: (block_of(s, t), 1, 0, 0)),
        ],
        [q_spec, kv_out, kv_out],
        [
            jax.ShapeDtypeStruct((2, 96, 1024), low),
            jax.ShapeDtypeStruct((2, 2, 96, 1024), low),
            jax.ShapeDtypeStruct((2, 2, 96, 1024), low),
        ],
        [
            pltpu.VMEM((2048, 96), low),
            pltpu.VMEM((96, 2048), low),
            pltpu.VMEM((2048, 96), low),
            pltpu.VMEM((96, 2048), wide),
            pltpu.VMEM((96, 2048), wide),
            pltpu.VMEM((2048, 1), wide),
        ],
        10 * 2 * 1024 * 2048 * 96,
        12 * 1024 * 1024,
        (
            at,
            queries,
            *held,
            query_blk,
            key_blk,
            attention,
            totals,
            *tables[:2],
            grad_blocks,
            grad_blocks,
        ),
        exps=2 * 1024 * 2048,
    )


def head_grads(dq_ref, ds_ref, cos_ref, sin_ref):
    own = turn_back(ds_ref[0], cos_ref[...], sin_ref[...])
    return jnp.concatenate([dq_ref[0].astype(wide), own], axis=0)


def head_grad_specs():
    q_spec = pl.BlockSpec((1, 96, 256), lambda g, t: (g // 4, 0, g % 4))
    return table_specs()[:2] + [q_spec, q_spec]


def head_weights(at, normed, tables, grad_queries, grad_own):
    def body(at_ref, rows_ref, cos_ref, sin_ref, dq_ref, ds_ref, *rest):
        keep_ref, send_ref, gw_scr, nat_scr = rest
        g = pl.program_id(0)

        @pl.when(g == 0)
        def _():
            gw_scr[...] = jnp.zeros_like(gw_scr)

        both = head_grads(dq_ref, ds_ref, cos_ref, sin_ref)
        gw_scr[...] += jnp.dot(both.astype(low), rows_ref[...], preferred_element_type=wide)

        @pl.when(g == 7)
        def _():
            nat_scr[...] = gw_scr[...].T
            for i in range(8):
                start = pl.multiple_of(at_ref[9 + i] * 96, 96)
                keep_ref[i] = nat_scr[pl.ds(start, 96), :].astype(low)
                start = pl.multiple_of(at_ref[17 + i] * 96, 96)
                send_ref[i] = nat_scr[pl.ds(start, 96), :].astype(low)

    blocks = jax.ShapeDtypeStruct((8, 96, 192), low)
    return kernel_call(
        body,
        (8,),
        [cube_spec()] + head_grad_specs(),
        [whole_spec((8, 96, 192))] * 2,
        [blocks, blocks],
        [pltpu.VMEM((192, 1536), wide), pltpu.VMEM((1536, 192), wide)],
        2 * 2048 * 1536 * 192,
        8 * 1024 * 1024,
        (at, normed, *tables[2:], grad_queries, grad_own),
    )


def project_back(at, w_heads, tables, grad_queries, grad_own):
    def body(at_ref, w_ref, cos_ref, sin_ref, dq_ref, ds_ref, *rest):
        outs, wt_scr = rest[:6], rest[6]

        @pl.when(pl.program_id(0) == 0)
        def _():
            wt_scr[...] = w_ref[...].astype(wide).T.astype(low)

        both = align(at_ref[8], head_grads(dq_ref, ds_ref, cos_ref, sin_ref))
        store_rows(outs, jnp.dot(both.T.astype(low), wt_scr[...], preferred_element_type=wide))

    return kernel_call(
        body,
        (8,),
        [whole_spec((1536, 192))] + head_grad_specs(),
        row_specs(THIRDS, lambda g, t: g),
        row_shapes(THIRDS),
        [pltpu.VMEM((192, 1536), low)],
        2 * 2048 * 1536 * 192,
        8 * 1024 * 1024,
        (at, w_heads, *tables[2:], grad_queries, grad_own),
    )


def hidden_back(at, grads, w_rows):
    def body(at_ref, *refs):
        rows, (w_ref, out_ref) = refs[:6], refs[6:]
        out_ref[...] = align_rows(at_ref[8], times_back(load_rows(rows), w_ref[...]))

    return kernel_call(
        body,
        (8,),
        row_specs(THIRDS, lambda g, t: g) + [whole_spec((256, 1536))],
        pl.BlockSpec((256, 256), lambda g, t: (g, 0)),
        jax.ShapeDtypeStruct((2048, 256), wide),
        [],
        2 * 2048 * 1536 * 256,
        8 * 1024 * 1024,
        (at, *flat(grads), w_rows),
    )


def feed_back(at, normed, w_both, grad_hidden):
    def body(at_ref, rows_ref, w_ref, dh_ref, *rest):
        outs, (hidden_ref, both_ref, wt_scr) = rest[:6], rest[6:]

        @pl.when(pl.program_id(0) == 0)
        def _():
            wt_scr[...] = w_ref[...].astype(wide).T.astype(low)

        both = jnp.dot(rows_ref[...], w_ref[...], preferred_element_type=wide)
        gate, up = both[:, :256], both[:, 256:]
        bend = jax.nn.sigmoid(gate)
        smooth = gate * bend
        grad_hidden = dh_ref[...]
        hidden_ref[...] = (smooth * up).astype(low)
        grad_gate = grad_hidden * up * (bend + smooth * (1.0 - bend))
        grad_both = jnp.concatenate([grad_gate, grad_hidden * smooth], axis=1).astype(low)
        both_ref[...] = grad_both
        grad_both = align_rows(at_ref[8], grad_both.astype(wide)).astype(low)
        store_rows(outs, jnp.dot(grad_both, wt_scr[...], preferred_element_type=wide))

    return kernel_call(
        body,
        (8,),
        [cube_spec(), whole_spec((1536, 512)), pl.BlockSpec((256, 256), lambda g, t: (g, 0))],
        row_specs(THIRDS, lambda g, t: g)
        + [
            pl.BlockSpec((256, 256), lambda g, t: (g, 0)),
            pl.BlockSpec((256, 512), lambda g, t: (g, 0)),
        ],
        row_shapes(THIRDS)
        + [
            jax.ShapeDtypeStruct((2048, 256), low),
            jax.ShapeDtypeStruct((2048, 512), low),
        ],
        [pltpu.VMEM((512, 1536), low)],
        4 * 2048 * 1536 * 512,
        18 * 1024 * 1024,
        (at, normed, w_both, grad_hidden),
        exps=2048 * 256,
    )


def feed_out(at, hidden, w_rows):
    def body(at_ref, hidden_ref, w_ref, *outs):
        made = jnp.dot(hidden_ref[...], w_ref[...], preferred_element_type=wide)
        store_rows(outs, align_rows(at_ref[8], made))

    return kernel_call(
        body,
        (8,),
        [pl.BlockSpec((256, 256), lambda g, t: (g, 0)), whole_spec((256, 1536))],
        row_specs(HALVES, lambda g, t: g),
        row_shapes(HALVES),
        [],
        2 * 2048 * 1536 * 256,
        8 * 1024 * 1024,
        (at, hidden, w_rows),
    )


def down_weights(at, hidden, grads):
    def body(at_ref, *refs):
        rows, (hidden_ref, gw_ref, gw_scr) = refs[:6], refs[6:]
        g = pl.program_id(0)

        @pl.when(g == 0)
        def _():
            gw_scr[...] = jnp.zeros_like(gw_scr)

        held = align_rows(at_ref[8], hidden_ref[...].astype(wide)).astype(low)
        gw_scr[...] += over_rows(held, load_rows(rows))

        @pl.when(g == 7)
        def _():
            gw_ref[...] = gw_scr[...].astype(low)

    return kernel_call(
        body,
        (8,),
        row_specs(THIRDS, lambda g, t: g) + [pl.BlockSpec((256, 256), lambda g, t: (g, 0))],
        whole_spec((256, 1536)),
        jax.ShapeDtypeStruct((256, 1536), low),
        [pltpu.VMEM((256, 1536), wide)],
        2 * 2048 * 1536 * 256,
        8 * 1024 * 1024,
        (at, *flat(grads), hidden),
    )


def out_weights(at, attention, grads):
    def body(at_ref, att_ref, rows_ref, gw_ref, gw_scr):
        g = pl.program_id(0)

        @pl.when(g == 0)
        def _():
            gw_scr[...] = jnp.zeros_like(gw_scr)

        gw_scr[...] += jnp.dot(
            att_ref[0].astype(low), rows_ref[...], preferred_element_type=wide
        )

        @pl.when(g == 7)
        def _():
            gw_ref[...] = gw_scr[...].astype(low)

    return kernel_call(
        body,
        (8,),
        [pl.BlockSpec((1, 96, 256), lambda g, t: (g // 4, 0, g % 4)), cube_spec()],
        whole_spec((96, 1536)),
        jax.ShapeDtypeStruct((96, 1536), low),
        [pltpu.VMEM((96, 1536), wide)],
        2 * 2048 * 1536 * 96,
        8 * 1024 * 1024,
        (at, attention, grads),
    )


def feed_weights(at, normed, grad_both):
    def body(at_ref, rows_ref, both_ref, keep_ref, send_ref, gw_scr, nat_scr):
        g = pl.program_id(0)

        @pl.when(g == 0)
        def _():
            gw_scr[...] = jnp.zeros_like(gw_scr)

        gw_scr[...] += over_rows(both_ref[...], rows_ref[...])

        @pl.when(g == 7)
        def _():
            nat_scr[...] = gw_scr[...].T
            for i in range(8):
                start = pl.multiple_of(at_ref[9 + i] * 96, 96)
                keep_ref[i] = nat_scr[pl.ds(start, 96), :].astype(low)
                start = pl.multiple_of(at_ref[17 + i] * 96, 96)
                send_ref[i] = nat_scr[pl.ds(start, 96), :].astype(low)

    return kernel_call(
        body,
        (8,),
        [cube_spec(), pl.BlockSpec((256, 512), lambda g, t: (g, 0))],
        [whole_spec((8, 96, 512))] * 2,
        [jax.ShapeDtypeStruct((8, 96, 512), low)] * 2,
        [pltpu.VMEM((512, 1536), wide), pltpu.VMEM((1536, 512), wide)],
        2 * 2048 * 1536 * 512,
        14 * 1024 * 1024,
        (at, normed, grad_both),
    )


def sum_low(left, right):
    return (left.astype(wide) + right.astype(wide)).astype(low)


def cube_plan(
    inputs,
    cotangent,
    block_ids,
    piece_order,
    w_query,
    w_key,
    w_value,
    w_out,
    w_gate,
    w_up,
    w_down,
    gain_attn,
    gain_mlp,
):
    x = lax.axis_index("grp")
    seq_at = lax.axis_index("seq")
    zh, c = seq_at >> 3, seq_at & 1
    score_scale = HEAD_DIM ** (-0.5)
    gain_rows_attn = gain_attn.astype(wide)[:, None]
    gain_rows_mlp = gain_mlp.astype(wide)[:, None]
    eight = jnp.arange(8, dtype=jnp.int32)
    sixteen = jnp.arange(16, dtype=jnp.int32)
    cyl = (eight >> 2) + (eight & 2) + ((eight & 1) << 2)
    place = c.astype(jnp.int32)[None]
    natural = seq_at ^ sixteen

    def owns_out(i):
        return bit_of(i, BIT_X) == bit_of(i, BIT_ZH)

    def owns_down(i):
        return bit_of(i, BIT_X) ^ bit_of(i, BIT_C) == bit_of(i, BIT_ZH)

    def lacks_out(i):
        return not owns_out(i)

    def lacks_down(i):
        return not owns_down(i)

    out_owner, down_owner = x == zh, (x ^ c) == zh

    order = ((sixteen & 8)) | ((sixteen & 4) >> 1) | ((sixteen & 2) << 1) | (sixteen & 1)
    stored = (seq_at & 14) ^ order
    pieces = jnp.sum(
        jnp.where(stored[:, None] == sixteen[None, :], piece_order[None, :], 0), axis=1
    )
    own_pos = (pieces[:8, None] * 128 + jnp.arange(128, dtype=jnp.int32)[None, :]).reshape(1024)
    frequency = rope_base ** (-jnp.arange(HEAD_DIM // 2, dtype=wide) * 2.0 / HEAD_DIM)
    angles = frequency[:, None] * own_pos.astype(wide)[None, :]
    cosine, sine = jnp.cos(angles), jnp.sin(angles)
    keyed = c == 0
    tables = (
        cosine,
        sine,
        jnp.where(keyed, cosine, 1.0),
        jnp.where(keyed, sine, 0.0),
    )

    low_zy = ((eight & 1) << 2) | (eight & 2)
    side_of = x ^ (eight >> 2)
    spots = jnp.concatenate([side_of * 4 + (((seq_at ^ low_zy) & 7) >> 1), place])
    spots_rows = jnp.concatenate([spots, natural])
    head_for = jnp.concatenate(
        [side_of * 8 + ((seq_at ^ low_zy ^ core) & 7) for core in (0, 1)]
    )

    residual = inputs[0].astype(wide)
    scale_first = rms_scale(residual)
    normed_first = residual * scale_first
    normed = cube_gather(normed_first.astype(low))
    head_of = x * 8 + ((seq_at ^ cyl) & 7)
    heads = pick_heads(head_of, w_query, w_key, w_value, gain_rows_attn)
    heads = trade_block(heads.reshape(2, 2, 2, 96, 192), 0, BIT_C)
    heads, w_out_held = sync(heads, w_out)
    out_near = swap(w_out_held, BIT_ZH, owns_out)
    heads = trade_block(heads, 1, BIT_Y)
    heads, ids_held, up_held = sync(heads, block_ids, w_up)
    heads = trade_block(heads, 2, BIT_ZL)
    other_ids = swap(ids_held, BIT_X)
    wanted_mlp = (x ^ ((seq_at ^ cyl) & 1)) * 8 + ((seq_at ^ cyl) & 7)
    both_blocks = pick_columns(wanted_mlp, w_gate, up_held, gain_rows_mlp)
    heads, out_near, both_blocks = sync(heads, out_near, both_blocks)
    heads = heads.reshape(8, 96, 192)
    heads_far = swap(heads, BIT_ZH)
    both_blocks = trade_block(both_blocks.reshape(2, 2, 2, 96, 512), 0, BIT_C)
    both_blocks = trade_block(both_blocks, 1, BIT_Y)
    w_out_head = jnp.where(out_owner, w_out, out_near)
    heads, heads_far, both_blocks, w_down_held, tables = sync(
        heads, heads_far, both_blocks, w_down, tables
    )
    w_heads = assemble_rows(natural, heads, heads_far)
    ids = jnp.concatenate([block_ids, other_ids], axis=0).reshape(2, 16, 128)
    chosen = (pieces[:, None] == sixteen[None, :]).astype(low)
    blocks = jnp.einsum(
        "kp,spr->skr", chosen, ids.astype(low), preferred_element_type=wide
    ).reshape(2, 1, 2048)
    query_blk, key_blk = blocks[:, :, :1024], blocks
    normed, w_heads, both_blocks, w_out_head, query_blk, key_blk, rows_dy = sync(
        normed, w_heads, both_blocks, w_out_head, query_blk, key_blk, cotangent[0]
    )

    out_full = cube_gather(w_out_head)
    grads = gather_next(gather_start(rows_dy, THIRDS), THIRDS, 0)
    queries, own_part = project(spots, normed, w_heads, tables)
    queries, own_part, grads, both_blocks = sync(queries, own_part, grads, both_blocks)
    far_part = swap(own_part, BIT_ZH)
    grads = gather_next(grads, THIRDS, 1)
    far_part, grads, both_blocks = sync(far_part, grads, both_blocks)
    other_parts = swap(jnp.stack([own_part, far_part]), BIT_C)
    both_blocks = trade_block(both_blocks, 2, BIT_ZL)
    other_parts, far_part, grads = sync(other_parts, far_part, grads)
    held = (own_part, far_part, other_parts, other_parts)
    grads = gather_next(grads, THIRDS, 2)
    down_near = swap(w_down_held, BIT_ZH, owns_down)
    keep, send, attention, totals = attend_forward(
        spots, queries, held, query_blk, key_blk, score_scale
    )
    keep, send, attention, totals, both_blocks, grads, out_full = sync(
        keep, send, attention, totals, both_blocks, grads, out_full
    )

    near_rows = [both_blocks[0].reshape(4, 96, 512), both_blocks[1].reshape(4, 96, 512)]
    traded = jnp.stack([keep, swap(send, BIT_C)]).reshape(2, 2, 2, 2, 96, 128)
    grads = gather_last(grads)
    traded, grads, down_near, near_rows = sync(traded, grads, down_near, near_rows)
    far_first = swap(near_rows[0], BIT_ZH)
    traded = trade_block(traded, 1, BIT_X)
    traded, near_rows = sync(traded, near_rows)
    traded = trade_block(traded, 2, BIT_Y)
    traded, far_first, near_rows = sync(traded, far_first, near_rows)
    far_second = swap(near_rows[1], BIT_ZH)
    traded = trade_block(traded, 3, BIT_ZL).reshape(16, 96, 128)
    traded, residual = sync(traded, residual)
    lyxc = ((sixteen & 8) >> 1) | ((sixteen & 4) >> 1) | (sixteen & 1)
    head_from = (x ^ ((sixteen & 2) >> 1)) * 8 + ((seq_at ^ lyxc) & 7)
    middle, scale_second, rows_second = out_project(head_from, traded, out_full, residual)

    rows_second, middle, scale_second, grads = sync(rows_second, middle, scale_second, grads)
    normed_mlp = cube_gather(rows_second)
    w_rows = jnp.where(down_owner, w_down_held, down_near)
    grad_hidden = hidden_back(spots, grads, w_rows)
    grad_hidden, far_second = sync(grad_hidden, far_second)
    w_both = assemble_rows(natural, *near_rows, far_first, far_second)
    normed_mlp, grad_hidden, w_both = sync(normed_mlp, grad_hidden, w_both)
    made = feed_back(spots, normed_mlp, w_both, grad_hidden)
    hidden, grad_both = made[6:]
    sums = scatter_start(paired(made[:6]))
    sums, hidden, grad_both = sync(sums, hidden, grad_both)
    sums = scatter_next(sums, THIRDS, 2)
    keep_both, send_both = feed_weights(spots_rows, normed_mlp, grad_both)
    sums, keep_both, send_both = sync(sums, keep_both, send_both)
    sums = scatter_next(sums, THIRDS, 1)
    sums, = sync(sums)
    sums = scatter_next(sums, THIRDS, 0)
    sums, hidden, send_both = sync(sums, hidden, send_both)

    parts = scatter_last(sums)
    grad_middle, grad_low, keep, send = out_back(
        head_for, cotangent[0], parts, middle, scale_second, out_full
    )
    grad_middle, grad_low, keep, send, hidden, send_both = sync(
        grad_middle, grad_low, keep, send, hidden, send_both
    )
    middle_rows = cube_gather(grad_low)
    arrived_first = swap(send_both[:4], BIT_ZH)
    traded = jnp.stack([keep, swap(send, BIT_C)]).reshape(2, 2, 2, 2, 96, 128)
    traded, hidden = sync(traded, hidden)
    out_terms = feed_out(spots, hidden, w_rows)
    traded = trade_block(traded, 1, BIT_X)
    traded, out_terms, hidden = sync(traded, out_terms, hidden)
    grad_down = down_weights(spots, hidden, grads)
    traded = trade_block(traded, 2, BIT_Y)
    traded, grad_down, arrived_first, send_both, out_terms = sync(
        traded, grad_down, arrived_first, send_both, out_terms
    )
    arrived_second = swap(send_both[4:], BIT_ZH)
    traded = trade_block(traded, 3, BIT_ZL).reshape(8, 2, 96, 128)
    out_sums = scatter_start(paired(out_terms))
    traded, out_sums = sync(traded, out_sums)
    out_sums = scatter_next(out_sums, HALVES, 2)
    made = attend_backward(
        spots,
        queries,
        held,
        query_blk,
        key_blk,
        attention,
        totals,
        traded,
        tables,
        score_scale,
    )
    made, out_sums, arrived_second = sync(made, out_sums, arrived_second)
    grad_queries, mine, sent = made
    both_sum = sum_low(keep_both, jnp.concatenate([arrived_first, arrived_second], axis=0))
    arrived = swap(sent, BIT_C)
    arrived, both_sum, grad_down = sync(arrived, both_sum, grad_down)
    far_terms = sum_low(mine[1], arrived[1])
    far_terms, out_sums, both_sum = sync([far_terms[0], far_terms[1]], out_sums, both_sum)
    far_first = swap(far_terms[0], BIT_ZH)
    out_sums = scatter_next(out_sums, HALVES, 1)
    both_sum = trade_block(both_sum.reshape(2, 2, 2, 96, 512), 0, BIT_ZL)
    far_first, far_terms, out_sums, both_sum, middle_rows = sync(
        far_first, far_terms, out_sums, both_sum, middle_rows
    )
    far_second = swap(far_terms[1], BIT_ZH)
    both_sum = trade_block(both_sum, 1, BIT_Y)
    grad_out_head = out_weights(spots, attention, middle_rows)
    far_second, both_sum, grad_out_head, out_sums = sync(
        far_second, both_sum, grad_out_head, out_sums
    )
    grad_own = (
        mine[0].astype(wide)
        + arrived[0].astype(wide)
        + jnp.stack([far_first, far_second]).astype(wide)
    )
    out_sums = scatter_next(out_sums, HALVES, 0)
    down_arrived = swap(grad_down, BIT_ZH, lacks_down)
    both_near = trade_block(both_sum, 2, BIT_C).reshape(8, 96, 512)
    made = project_back(spots, w_heads, tables, grad_queries, grad_own)
    sums = scatter_start(paired(made))
    sums, grad_own, both_near = sync(sums, grad_own, both_near)
    both_far = swap(both_near, BIT_X)
    keep_heads, send_heads = head_weights(
        spots_rows, normed, tables, grad_queries, grad_own
    )
    sums = scatter_next(sums, THIRDS, 2)
    sums, keep_heads, send_heads, out_sums, down_arrived = sync(
        sums, keep_heads, send_heads, out_sums, down_arrived
    )
    heads_first = swap(send_heads, BIT_ZH)
    output = jnp.concatenate([part[0] for part in scatter_last(out_sums)], axis=1)
    output = (middle + output).astype(low)
    down_sum = sum_low(grad_down, down_arrived)
    sums = scatter_next(sums, THIRDS, 1)
    sums, output, down_sum, both_far = sync(sums, output, down_sum, both_far)
    down_far = swap(down_sum, BIT_X, owns_down)
    sums = scatter_next(sums, THIRDS, 0)
    sums, heads_first, grad_out_head = sync(sums, heads_first, grad_out_head)
    out_arrived = swap(grad_out_head, BIT_ZH, lacks_out)
    heads_sum = sum_low(keep_heads, heads_first)
    heads_sum = trade_block(heads_sum.reshape(2, 2, 2, 96, 192), 0, BIT_ZL)
    scaled_first = jnp.concatenate([part[0] for part in scatter_last(sums)], axis=1)
    grad_inputs = grad_middle + scale_first * (
        scaled_first
        - normed_first * jnp.mean(scaled_first * normed_first, axis=-1, keepdims=True)
    )
    heads_sum = trade_block(heads_sum, 1, BIT_Y)
    heads_near = trade_block(heads_sum, 2, BIT_C).reshape(8, 96, 192)
    heads_near, out_arrived = sync(heads_near, out_arrived)
    heads_far = swap(heads_near, BIT_X)
    out_sum = sum_low(grad_out_head, out_arrived)
    out_far = swap(out_sum, BIT_X, owns_out)

    back = seq_at ^ cyl
    home = jnp.concatenate([x * 8 + (back & 7), (1 - x) * 8 + (back & 7)])
    grad_w_query, grad_w_key, grad_w_value, grad_gain_attn = spread_heads(
        home, heads_near, heads_far, w_query, w_key, w_value, gain_rows_attn
    )
    grad_w_out = jnp.where(out_owner, out_sum, out_far).astype(wide)
    grad_w_down = jnp.where(down_owner, down_sum, down_far).astype(wide)
    side = (back & 1) ^ x
    home = jnp.concatenate([side * 8 + (back & 7), (1 - side) * 8 + (back & 7)])
    grad_w_gate, grad_w_up, grad_gain_mlp = spread_columns(
        home, both_near, both_far, gain_rows_mlp, w_gate, w_up
    )
    return (
        output[None],
        grad_inputs.astype(low)[None],
        grad_w_query,
        grad_w_key,
        grad_w_value,
        grad_w_out,
        grad_w_gate,
        grad_w_up,
        grad_w_down,
        grad_gain_attn[:, 0],
        grad_gain_mlp[:, 0],
    )


def ring_plan(
    inputs,
    cotangent,
    block_ids,
    piece_order,
    w_query,
    w_key,
    w_value,
    w_out,
    w_gate,
    w_up,
    w_down,
    gain_attn,
    gain_mlp,
):
    shards = (w_query, w_key, w_value, w_out, w_gate, w_up, w_down, gain_attn, gain_mlp)
    (
        full_query,
        full_key,
        full_value,
        full_out,
        full_gate,
        full_up,
        full_down,
        gain_one,
        gain_two,
    ) = (
        lax.all_gather(shards[0], "seq", axis=0, tiled=True),
        lax.all_gather(shards[1], "seq", axis=0, tiled=True),
        lax.all_gather(shards[2], "seq", axis=0, tiled=True),
        lax.all_gather(shards[3], "seq", axis=0, tiled=True),
        lax.all_gather(shards[4], "seq", axis=0, tiled=True),
        lax.all_gather(shards[5], "seq", axis=0, tiled=True),
        lax.all_gather(shards[6], "seq", axis=0, tiled=True),
        lax.all_gather(shards[7], "seq", axis=0, tiled=True),
        lax.all_gather(shards[8], "seq", axis=0, tiled=True),
    )
    seq_count, tok_rows, model_width = inputs.shape
    row_count = seq_count * tok_rows
    head_count = HEADS
    kv_heads = KV_HEADS
    head_dim = HEAD_DIM
    groups = head_count // kv_heads
    kv_width = kv_heads * head_dim
    q_width = head_count * head_dim
    score_scale = head_dim ** (-0.5)
    own_first = jnp.take(piece_order, lax.axis_index("seq")) * tok_rows
    local_pos = own_first + jnp.arange(tok_rows, dtype=jnp.int32)
    cosine_table, sine_table = rotary_tables(local_pos, head_dim)
    query_blk = jnp.take(block_ids, local_pos, axis=1)

    def key_positions(key_count):
        stored = jnp.arange(key_count, dtype=jnp.int32)
        return jnp.take(piece_order, stored // tok_rows) * tok_rows + stored % tok_rows

    residual = inputs.reshape(row_count, model_width).astype(jnp.float32)
    gain_first = gain_one.astype(jnp.float32)
    gain_second = gain_two.astype(jnp.float32)
    scale_first = rms_scale(residual)
    normed_attn = (residual * scale_first * gain_first).astype(jnp.bfloat16)
    query_pre = jnp.dot(normed_attn, full_query, preferred_element_type=jnp.float32)
    key_pre = jnp.dot(normed_attn, full_key, preferred_element_type=jnp.float32)
    value_pre = jnp.dot(normed_attn, full_value, preferred_element_type=jnp.float32)
    queries = rotate(
        query_pre.reshape(seq_count, tok_rows, head_count, head_dim), cosine_table, sine_table
    ).astype(jnp.bfloat16)
    key_rot = rotate(
        key_pre.reshape(seq_count, tok_rows, kv_heads, head_dim), cosine_table, sine_table
    ).astype(jnp.bfloat16)
    values = value_pre.astype(jnp.bfloat16)
    kv_local = jnp.concatenate(
        [
            key_rot.reshape(seq_count, tok_rows, kv_width),
            values.reshape(seq_count, tok_rows, kv_width),
        ],
        axis=2,
    )
    query_grouped = queries.reshape(seq_count, tok_rows, kv_heads, groups, head_dim)
    start_max = jnp.full((seq_count, kv_heads, groups, tok_rows), masked_score, jnp.float32)
    start_sum = jnp.zeros((seq_count, kv_heads, groups, tok_rows), jnp.float32)
    start_acc = jnp.zeros((seq_count, kv_heads, groups, tok_rows, head_dim), jnp.float32)
    state_in = (start_max, start_sum, start_acc)
    key_piece = lax.all_gather(kv_local, "seq", axis=1, tiled=True)
    key_count = key_piece.shape[1]
    block_rows = key_block_rows(key_count)
    key_pos = key_positions(key_count)
    member = 0
    key_blk = jnp.take(block_ids[member], key_pos).reshape(key_count // block_rows, block_rows)
    kv_rows = key_piece[member].reshape(key_count // block_rows, block_rows, 2 * kv_width)
    own_query = query_grouped[member]
    own_blocks = query_blk[member]

    def forward_key_step(running, block_in):
        kv_block, blk_block = block_in
        key_part = kv_block[:, :kv_width].reshape(block_rows, kv_heads, head_dim)
        value_part = kv_block[:, kv_width:].reshape(block_rows, kv_heads, head_dim)
        running = forward_block(
            running, own_query, own_blocks, key_part, value_part, blk_block, score_scale
        )
        return (running, None)

    running, unused = lax.scan(
        forward_key_step,
        (state_in[0][member], state_in[1][member], state_in[2][member]),
        (kv_rows, key_blk),
    )
    results = [running]
    row_max = jnp.stack([entry[0] for entry in results])
    row_sum = jnp.stack([entry[1] for entry in results])
    running_sum = jnp.stack([entry[2] for entry in results])
    log_total = row_max + jnp.log(row_sum)
    attention = running_sum / row_sum[..., None]
    attended = (
        jnp.transpose(attention, (0, 3, 1, 2, 4)).reshape(row_count, q_width).astype(jnp.bfloat16)
    )
    middle = residual + jnp.dot(attended, full_out, preferred_element_type=jnp.float32)
    scale_second = rms_scale(middle)
    normed_mlp = (middle * scale_second * gain_second).astype(jnp.bfloat16)
    gate_value = jnp.dot(normed_mlp, full_gate, preferred_element_type=jnp.float32)
    upward = jnp.dot(normed_mlp, full_up, preferred_element_type=jnp.float32)
    sigmoid_gate = jax.nn.sigmoid(gate_value)
    hidden = (gate_value * sigmoid_gate * upward).astype(jnp.bfloat16)
    output = (middle + jnp.dot(hidden, full_down, preferred_element_type=jnp.float32)).astype(
        jnp.bfloat16
    )
    (
        full_query,
        full_key,
        full_value,
        full_out,
        full_gate,
        full_up,
        full_down,
        gain_one,
        gain_two,
    ) = (
        lax.all_gather(shards[0], "seq", axis=0, tiled=True),
        lax.all_gather(shards[1], "seq", axis=0, tiled=True),
        lax.all_gather(shards[2], "seq", axis=0, tiled=True),
        lax.all_gather(shards[3], "seq", axis=0, tiled=True),
        lax.all_gather(shards[4], "seq", axis=0, tiled=True),
        lax.all_gather(shards[5], "seq", axis=0, tiled=True),
        lax.all_gather(shards[6], "seq", axis=0, tiled=True),
        lax.all_gather(shards[7], "seq", axis=0, tiled=True),
        lax.all_gather(shards[8], "seq", axis=0, tiled=True),
    )
    gain_first = gain_one.astype(jnp.float32)
    gain_second = gain_two.astype(jnp.float32)
    upstream = cotangent.reshape(row_count, model_width)
    grad_down = over_rows(hidden, upstream)
    grad_hidden = times_back(upstream, full_down)
    grad_gate = (
        grad_hidden * upward * sigmoid_gate * (1.0 + gate_value * (1.0 - sigmoid_gate))
    ).astype(jnp.bfloat16)
    grad_upward = (grad_hidden * gate_value * sigmoid_gate).astype(jnp.bfloat16)
    grad_w_gate = over_rows(normed_mlp, grad_gate)
    grad_w_up = over_rows(normed_mlp, grad_upward)
    grad_normed_mlp = times_back(grad_gate, full_gate) + times_back(grad_upward, full_up)
    grad_mid_norm, grad_gain_mlp = norm_back(grad_normed_mlp, middle, scale_second, gain_second)
    grad_middle = upstream.astype(jnp.float32) + grad_mid_norm
    grad_middle_low = grad_middle.astype(jnp.bfloat16)
    grad_w_out = over_rows(attended, grad_middle_low)
    grad_attended = times_back(grad_middle_low, full_out).astype(jnp.bfloat16)
    grad_heads = jnp.transpose(
        grad_attended.reshape(seq_count, tok_rows, kv_heads, groups, head_dim), (0, 2, 3, 1, 4)
    )
    delta_rows = jnp.sum(grad_heads.astype(jnp.float32) * attention, axis=-1)
    start_query = jnp.zeros((seq_count, kv_heads, groups, tok_rows, head_dim), jnp.float32)
    start_kv = jnp.zeros((seq_count, block_ids.shape[1], 2 * kv_width), jnp.float32)
    state_in = (start_query, start_kv)
    key_piece = lax.all_gather(kv_local, "seq", axis=1, tiled=True)
    key_count = key_piece.shape[1]
    backward_block_rows = key_block_rows(key_count)
    key_pos = key_positions(key_count)
    member = 0
    key_blk = jnp.take(block_ids[member], key_pos).reshape(
        key_count // backward_block_rows, backward_block_rows
    )
    kv_rows = key_piece[member].reshape(
        key_count // backward_block_rows, backward_block_rows, 2 * kv_width
    )
    backward_own_query = query_grouped[member]
    backward_own_blocks = query_blk[member]
    own_total = log_total[member]
    own_grads = grad_heads[member]
    own_delta = delta_rows[member]

    def backward_key_step(grad_query, block_in):
        kv_block, blk_block = block_in
        key_part = kv_block[:, :kv_width].reshape(backward_block_rows, kv_heads, head_dim)
        value_part = kv_block[:, kv_width:].reshape(backward_block_rows, kv_heads, head_dim)
        result = backward_block(
            grad_query,
            backward_own_query,
            backward_own_blocks,
            key_part,
            value_part,
            blk_block,
            own_total,
            own_grads,
            own_delta,
            score_scale,
        )
        return (result[0], (result[1], result[2]))

    grad_query, key_grads = lax.scan(backward_key_step, state_in[0][member], (kv_rows, key_blk))
    fresh = jnp.concatenate(
        [key_grads[0].reshape(key_count, kv_width), key_grads[1].reshape(key_count, kv_width)],
        axis=1,
    )
    query_grads = [grad_query]
    kv_grads = [fresh]
    grad_query_all = jnp.stack(query_grads)
    grad_kv_all = jnp.stack(kv_grads)
    grad_kv_own = lax.psum_scatter(grad_kv_all, "seq", scatter_dimension=1, tiled=True)
    grad_query_rows = jnp.transpose(grad_query_all, (0, 3, 1, 2, 4)).reshape(
        seq_count, tok_rows, head_count, head_dim
    )
    grad_query_pre = (
        unrotate(grad_query_rows, cosine_table, sine_table)
        .reshape(row_count, q_width)
        .astype(jnp.bfloat16)
    )
    grad_key_rows = grad_kv_own[:, :, :kv_width].reshape(seq_count, tok_rows, kv_heads, head_dim)
    grad_key_pre = (
        unrotate(grad_key_rows, cosine_table, sine_table)
        .reshape(row_count, kv_width)
        .astype(jnp.bfloat16)
    )
    grad_value_pre = grad_kv_own[:, :, kv_width:].reshape(row_count, kv_width).astype(jnp.bfloat16)
    grad_w_query = over_rows(normed_attn, grad_query_pre)
    grad_w_key = over_rows(normed_attn, grad_key_pre)
    grad_w_value = over_rows(normed_attn, grad_value_pre)
    grad_normed_attn = (
        times_back(grad_query_pre, full_query)
        + times_back(grad_key_pre, full_key)
        + times_back(grad_value_pre, full_value)
    )
    grad_in_norm, grad_gain_attn = norm_back(grad_normed_attn, residual, scale_first, gain_first)
    grad_inputs = (
        (grad_middle + grad_in_norm).astype(jnp.bfloat16).reshape(seq_count, tok_rows, model_width)
    )
    terms = (
        grad_w_query,
        grad_w_key,
        grad_w_value,
        grad_w_out,
        grad_w_gate,
        grad_w_up,
        grad_down,
        grad_gain_attn,
        grad_gain_mlp,
    )
    shares = (
        lax.psum_scatter(terms[0], "seq", scatter_dimension=0, tiled=True),
        lax.psum_scatter(terms[1], "seq", scatter_dimension=0, tiled=True),
        lax.psum_scatter(terms[2], "seq", scatter_dimension=0, tiled=True),
        lax.psum_scatter(terms[3], "seq", scatter_dimension=0, tiled=True),
        lax.psum_scatter(terms[4], "seq", scatter_dimension=0, tiled=True),
        lax.psum_scatter(terms[5], "seq", scatter_dimension=0, tiled=True),
        lax.psum_scatter(terms[6], "seq", scatter_dimension=0, tiled=True),
        lax.psum_scatter(terms[7], "seq", scatter_dimension=0, tiled=True),
        lax.psum_scatter(terms[8], "seq", scatter_dimension=0, tiled=True),
    )
    totals = (
        lax.psum(shares[0].astype(jnp.bfloat16), "grp").astype(jnp.float32),
        lax.psum(shares[1].astype(jnp.bfloat16), "grp").astype(jnp.float32),
        lax.psum(shares[2].astype(jnp.bfloat16), "grp").astype(jnp.float32),
        lax.psum(shares[3].astype(jnp.bfloat16), "grp").astype(jnp.float32),
        lax.psum(shares[4].astype(jnp.bfloat16), "grp").astype(jnp.float32),
        lax.psum(shares[5].astype(jnp.bfloat16), "grp").astype(jnp.float32),
        lax.psum(shares[6].astype(jnp.bfloat16), "grp").astype(jnp.float32),
        lax.psum(shares[7].astype(jnp.bfloat16), "grp").astype(jnp.float32),
        lax.psum(shares[8].astype(jnp.bfloat16), "grp").astype(jnp.float32),
    )
    return (
        output.reshape(seq_count, tok_rows, model_width),
        grad_inputs,
        totals[0],
        totals[1],
        totals[2],
        totals[3],
        totals[4],
        totals[5],
        totals[6],
        totals[7],
        totals[8],
    )


def solution(mesh):
    local = ring_plan
    if (mesh.shape["grp"], mesh.shape["seq"]) == (2, 16):
        local = cube_plan
    return jax.shard_map(
        local,
        mesh=mesh,
        in_specs=(
            P("grp", "seq", None),
            P("grp", "seq", None),
            P("grp", None),
            P(),
            P("seq", None),
            P("seq", None),
            P("seq", None),
            P("seq", None),
            P("seq", None),
            P("seq", None),
            P("seq", None),
            P("seq"),
            P("seq"),
        ),
        out_specs=(
            P("grp", "seq", None),
            P("grp", "seq", None),
            P("seq", None),
            P("seq", None),
            P("seq", None),
            P("seq", None),
            P("seq", None),
            P("seq", None),
            P("seq", None),
            P("seq"),
            P("seq"),
        ),
        check_vma=False,
    )
```

```python
import functools

import jax
import jax.numpy as jnp
from jax import lax
from jax.experimental import pallas as pl
from jax.experimental.pallas import tpu as pltpu
from jax.sharding import PartitionSpec as P

HEADS = 16
KV_HEADS = 8
HEAD_DIM = 96


eps_norm = 1e-05
rope_base = 100000.0
masked_score = -1e30


def rms_scale(rows_in):
    return lax.rsqrt(jnp.mean(rows_in * rows_in, axis=-1, keepdims=True) + eps_norm)


def norm_back(grad_normed, rows_in, row_scale, gain_row):
    normed = rows_in * row_scale
    grad_gain = jnp.sum(grad_normed * normed, axis=0)
    scaled_grad = grad_normed * gain_row
    grad_rows = row_scale * (
        scaled_grad - normed * jnp.mean(scaled_grad * normed, axis=-1, keepdims=True)
    )
    return (grad_rows, grad_gain)


def rotary_tables(positions, head_dim):
    half_dim = head_dim // 2
    frequency = rope_base ** (-jnp.arange(half_dim, dtype=jnp.float32) * 2.0 / head_dim)
    angles = positions.astype(jnp.float32)[:, None] * frequency[None, :]
    return (jnp.cos(angles)[:, None, :], jnp.sin(angles)[:, None, :])


def rotate(vectors, cosine_table, sine_table):
    half_dim = vectors.shape[-1] // 2
    front_half = vectors[..., :half_dim]
    back_half = vectors[..., half_dim:]
    return jnp.concatenate(
        [
            front_half * cosine_table - back_half * sine_table,
            back_half * cosine_table + front_half * sine_table,
        ],
        axis=-1,
    )


def unrotate(grads, cosine_table, sine_table):
    half_dim = grads.shape[-1] // 2
    front_half = grads[..., :half_dim]
    back_half = grads[..., half_dim:]
    return jnp.concatenate(
        [
            front_half * cosine_table + back_half * sine_table,
            back_half * cosine_table - front_half * sine_table,
        ],
        axis=-1,
    )


def over_rows(left, right):
    return lax.dot_general(
        left, right, (((0,), (0,)), ((), ())), preferred_element_type=jnp.float32
    )


def times_back(left, right):
    return lax.dot_general(
        left, right, (((1,), (1,)), ((), ())), preferred_element_type=jnp.float32
    )


def key_block_rows(key_count):
    block_rows = min(key_count, 1024)
    return block_rows


def masked_scores(query_part, key_part, query_blocks, key_blocks, score_scale):
    scores = (
        jnp.einsum("qkgd,tkd->kgqt", query_part, key_part, preferred_element_type=jnp.float32)
        * score_scale
    )
    allowed = key_blocks[None, None, None, :] <= query_blocks[None, None, :, None]
    return jnp.where(allowed, scores, masked_score)


def forward_block(running, query_part, query_blocks, key_part, value_part, key_blocks, score_scale):
    row_max, row_sum, running_sum = running
    scores = masked_scores(query_part, key_part, query_blocks, key_blocks, score_scale)
    new_max = jnp.maximum(row_max, jnp.max(scores, axis=-1))
    likely = jnp.exp(scores - new_max[..., None])
    fading = jnp.exp(row_max - new_max)
    row_sum = row_sum * fading + jnp.sum(likely, axis=-1)
    running_sum = running_sum * fading[..., None] + jnp.einsum(
        "kgqt,tkd->kgqd",
        likely.astype(jnp.bfloat16),
        value_part,
        preferred_element_type=jnp.float32,
    )
    return (new_max, row_sum, running_sum)


def backward_block(
    grad_query,
    query_part,
    query_blocks,
    key_part,
    value_part,
    key_blocks,
    log_total,
    grad_heads,
    delta_rows,
    score_scale,
):
    scores = masked_scores(query_part, key_part, query_blocks, key_blocks, score_scale)
    chance = jnp.exp(scores - log_total[..., None])
    grad_value = jnp.einsum(
        "kgqt,kgqd->tkd",
        chance.astype(jnp.bfloat16),
        grad_heads,
        preferred_element_type=jnp.float32,
    )
    grad_chance = jnp.einsum(
        "kgqd,tkd->kgqt", grad_heads, value_part, preferred_element_type=jnp.float32
    )
    grad_scores = (chance * (grad_chance - delta_rows[..., None])).astype(jnp.bfloat16)
    grad_query = (
        grad_query
        + jnp.einsum("kgqt,tkd->kgqd", grad_scores, key_part, preferred_element_type=jnp.float32)
        * score_scale
    )
    grad_key = (
        jnp.einsum("kgqt,qkgd->tkd", grad_scores, query_part, preferred_element_type=jnp.float32)
        * score_scale
    )
    return (grad_query, grad_key, grad_value)


BIT_X, BIT_ZH, BIT_ZL, BIT_Y, BIT_C = 16, 8, 4, 2, 1
DEVICES = 32
AXES = ("grp", "seq")
THIRDS = (
    (BIT_X, BIT_Y, BIT_ZL),
    (BIT_Y, BIT_ZL, BIT_X),
    (BIT_ZL, BIT_X, BIT_Y),
)
HALVES = (
    (BIT_ZL, BIT_X, BIT_Y),
    (BIT_ZL, BIT_Y, BIT_X),
)
log2_e = 1.4426950408889634
VMEM_LIMIT = 48 * 1024 * 1024
low, wide = jnp.bfloat16, jnp.float32


def swap(value, mask, sends=None):
    pairs = [(i, i ^ mask) for i in range(DEVICES) if sends is None or sends(i)]
    return lax.ppermute(value, AXES, pairs)


def bit_of(index, mask):
    return 1 if index & mask else 0


def sync(*values):
    return lax.optimization_barrier(values)


def gather_start(rows, orders):
    width = rows.shape[1] // len(orders)
    return [rows[None, :, i * width : (i + 1) * width] for i in range(len(orders))]


def gather_next(parts, orders, step):
    return [
        jnp.concatenate([held, swap(held, order[step])], axis=0)
        for held, order in zip(parts, orders)
    ]


def gather_last(parts):
    return [(held, swap(held, BIT_C)) for held in parts]


def scatter_start(pairs):
    return [(kept, swap(sent, BIT_C)) for kept, sent in pairs]


def scatter_next(sums, orders, step):
    result = []
    for (kept, arrived), order in zip(sums, orders):
        half = kept.shape[0] // 2
        sent = (kept[half:].astype(wide) + arrived[half:].astype(wide)).astype(low)
        kept = (kept[:half].astype(wide) + arrived[:half].astype(wide)).astype(low)
        result.append((kept, swap(sent, order[step])))
    return result


def scatter_last(sums):
    return [kept.astype(wide) + arrived.astype(wide) for kept, arrived in sums]


def cube_groups():
    return [
        [gx * 16 + zh * 8 + rest for gx in (0, 1) for rest in range(8)] for zh in (0, 1)
    ]


def cube_gather(rows):
    return lax.all_gather(rows, AXES, axis=0, tiled=True, axis_index_groups=cube_groups())


def cube_scatter(rows):
    return lax.psum_scatter(
        rows, AXES, scatter_dimension=0, tiled=True, axis_index_groups=cube_groups()
    )


def trade_block(blocks, axis, mask):
    keep = lax.index_in_dim(blocks, 0, axis, keepdims=False)
    send = lax.index_in_dim(blocks, 1, axis, keepdims=False)
    return jnp.stack([keep, swap(send, mask)])


def trade_blocks(blocks, masks):
    for axis, mask in enumerate(masks):
        keep = lax.index_in_dim(blocks, 0, axis, keepdims=False)
        send = lax.index_in_dim(blocks, 1, axis, keepdims=False)
        blocks = jnp.stack([keep, swap(send, mask)])
    return blocks


def block_at(order):
    place = {BIT_X: 2, BIT_Y: 1, BIT_ZL: 0}

    def find(g):
        return sum(((g >> place[mask]) & 1) << rank for rank, mask in enumerate(order))

    return find


def row_specs(orders, step):
    width = 1536 // len(orders)
    specs = []
    for order in orders:
        find = block_at(order)
        for _ in range(2):
            specs.append(
                pl.BlockSpec((1, 128, width), lambda *a, find=find: (find(step(*a)), 0, 0))
            )
    return specs


def row_shapes(orders):
    width = 1536 // len(orders)
    return [jax.ShapeDtypeStruct((8, 128, width), low)] * (2 * len(orders))


def flat(pairs):
    return [array for pair in pairs for array in pair]


def paired(arrays):
    return [(arrays[i], arrays[i + 1]) for i in range(0, len(arrays), 2)]


def load_rows(refs):
    return jnp.concatenate(
        [
            jnp.concatenate([refs[i][0], refs[i + 1][0]], axis=0)
            for i in range(0, len(refs), 2)
        ],
        axis=1,
    )


def store_rows(refs, rows):
    width = 1536 // (len(refs) // 2)
    for i in range(0, len(refs), 2):
        columns = slice((i // 2) * width, (i // 2 + 1) * width)
        refs[i][0] = rows[:128, columns].astype(low)
        refs[i + 1][0] = rows[128:, columns].astype(low)


def whole_spec(shape):
    return pl.BlockSpec(shape, lambda *a: (0,) * len(shape))


def kernel_call(body, grid, in_specs, out_specs, out_shape, scratch, flops, moved, args, exps=0):
    return pl.pallas_call(
        body,
        out_shape=out_shape,
        grid_spec=pltpu.PrefetchScalarGridSpec(
            num_scalar_prefetch=1,
            grid=grid,
            in_specs=in_specs,
            out_specs=out_specs,
            scratch_shapes=scratch,
        ),
        compiler_params=pltpu.CompilerParams(vmem_limit_bytes=VMEM_LIMIT),
        cost_estimate=pl.CostEstimate(
            flops=flops, bytes_accessed=moved, transcendentals=exps
        ),
    )(*args)


def head_columns(w_query, w_key, w_value, head):
    shared = w_value if head % 2 else w_key
    start = (head // 2) * 96
    return w_query[:, head * 96 : head * 96 + 96], shared[:, start : start + 96]


def pick_heads(table, w_query, w_key, w_value, gain_rows):
    def body(table_ref, q_ref, k_ref, v_ref, gain_ref, out_ref, scr):
        gain = gain_ref[...]
        for head in range(16):
            one, two = head_columns(q_ref, k_ref, v_ref, head)
            scr[head, :, :96] = (one.astype(wide) * gain).astype(low)
            scr[head, :, 96:] = (two.astype(wide) * gain).astype(low)
        for i in range(8):
            out_ref[i] = scr[table_ref[i]]

    args = (w_query, w_key, w_value, gain_rows)
    return kernel_call(
        body,
        (1,),
        [whole_spec(a.shape) for a in args],
        whole_spec((8, 96, 192)),
        jax.ShapeDtypeStruct((8, 96, 192), low),
        [pltpu.VMEM((16, 96, 192), low)],
        0,
        1024 * 1024,
        (table, *args),
    )


def pick_columns(table, first, second, gain_rows):
    rows = first.shape[0]

    def body(table_ref, first_ref, second_ref, gain_ref, out_ref):
        gain = gain_ref[...]
        for i in range(8):
            columns = pl.ds(pl.multiple_of(table_ref[i] * 256, 256), 256)
            out_ref[i, :, :256] = (first_ref[:, columns].astype(wide) * gain).astype(low)
            out_ref[i, :, 256:] = (second_ref[:, columns].astype(wide) * gain).astype(low)

    shape = (8, rows, 512)
    return kernel_call(
        body,
        (1,),
        [whole_spec(first.shape), whole_spec(second.shape), whole_spec(gain_rows.shape)],
        whole_spec(shape),
        jax.ShapeDtypeStruct(shape, low),
        [],
        0,
        4 * first.size,
        (table, first, second, gain_rows),
    )


def assemble_rows(table, *groups):
    rows, width = groups[0].shape[1:]

    def body(table_ref, *refs):
        out_ref, i = refs[-1], 0
        for ref in refs[:-1]:
            for k in range(ref.shape[0]):
                start = pl.multiple_of(table_ref[i] * rows, rows)
                out_ref[pl.ds(start, rows), :] = ref[k]
                i += 1

    shape = (16 * rows, width)
    return kernel_call(
        body,
        (1,),
        [whole_spec(group.shape) for group in groups],
        whole_spec(shape),
        jax.ShapeDtypeStruct(shape, low),
        [],
        0,
        64 * rows * width,
        (table, *groups),
    )


def spread_columns(table, near, far, gain_rows, first, second):
    rows = near.shape[1]

    def body(table_ref, near_ref, far_ref, gain_ref, w1_ref, w2_ref, g1_ref, g2_ref, sum_ref):
        gain = gain_ref[...]
        total = jnp.zeros((rows, 256), wide)
        for i in range(16):
            source = near_ref if i < 8 else far_ref
            columns = pl.ds(pl.multiple_of(table_ref[i] * 256, 256), 256)
            block = source[i % 8].astype(wide)
            one, two = block[:, :256], block[:, 256:]
            total += one * w1_ref[:, columns].astype(wide)
            total += two * w2_ref[:, columns].astype(wide)
            g1_ref[:, columns] = one * gain
            g2_ref[:, columns] = two * gain
        sum_ref[...] = jnp.sum(total, axis=1, keepdims=True)

    return kernel_call(
        body,
        (1,),
        [whole_spec(a.shape) for a in (near, far, gain_rows, first, second)],
        [whole_spec(first.shape), whole_spec(second.shape), whole_spec((rows, 1))],
        [
            jax.ShapeDtypeStruct(first.shape, wide),
            jax.ShapeDtypeStruct(second.shape, wide),
            jax.ShapeDtypeStruct((rows, 1), wide),
        ],
        [],
        0,
        6 * 2 * first.size,
        (table, near, far, gain_rows, first, second),
    )


def spread_heads(table, near, far, w_query, w_key, w_value, gain_rows):
    def body(
        table_ref, near_ref, far_ref, q_ref, k_ref, v_ref, gain_ref, *rest
    ):
        gq_ref, gk_ref, gv_ref, sum_ref, scr = rest
        gain = gain_ref[...]
        for i in range(16):
            source = near_ref if i < 8 else far_ref
            scr[table_ref[i]] = source[i % 8].astype(wide)
        total = jnp.zeros((96, 96), wide)
        for head in range(16):
            one, two = head_columns(q_ref, k_ref, v_ref, head)
            block = scr[head]
            first, second = block[:, :96], block[:, 96:]
            total += first * one.astype(wide) + second * two.astype(wide)
            gq_ref[:, head * 96 : head * 96 + 96] = first * gain
            shared = gv_ref if head % 2 else gk_ref
            start = (head // 2) * 96
            shared[:, start : start + 96] = second * gain
        sum_ref[...] = jnp.sum(total, axis=1, keepdims=True)

    args = (near, far, w_query, w_key, w_value, gain_rows)
    shapes = [w_query.shape, w_key.shape, w_value.shape, (96, 1)]
    return kernel_call(
        body,
        (1,),
        [whole_spec(a.shape) for a in args],
        [whole_spec(shape) for shape in shapes],
        [jax.ShapeDtypeStruct(shape, wide) for shape in shapes],
        [pltpu.VMEM((16, 96, 192), wide)],
        0,
        4 * 1024 * 1024,
        (table, *args),
    )


def turn(rows, cosine, sine):
    front, back = rows[:48], rows[48:]
    return jnp.concatenate([front * cosine - back * sine, back * cosine + front * sine], axis=0)


def turn_back(rows, cosine, sine):
    front, back = rows[:48], rows[48:]
    return jnp.concatenate([front * cosine + back * sine, back * cosine - front * sine], axis=0)


def align_rows(core, rows):
    turned = jnp.concatenate([rows[128:], rows[:128]], axis=0)
    return jnp.where(core == 0, rows, turned)


def align(core, columns):
    turned = jnp.concatenate([columns[:, 128:], columns[:, :128]], axis=1)
    return jnp.where(core == 0, columns, turned)


def table_specs():
    return [pl.BlockSpec((48, 256), lambda g, t: (0, g % 4))] * 4


def cube_spec():
    return pl.BlockSpec((256, 1536), lambda g, t: (t[g], 0))


def project(at, normed, w_heads, tables):
    def body(at_ref, rows_ref, w_ref, cos_ref, sin_ref, cos2_ref, sin2_ref, q_ref, own_ref):
        made = jnp.dot(rows_ref[...], w_ref[...], preferred_element_type=wide).T
        q_ref[0] = turn(made[:96], cos_ref[...], sin_ref[...]).astype(low)
        own_ref[0] = turn(made[96:], cos2_ref[...], sin2_ref[...]).astype(low)

    out_spec = pl.BlockSpec((1, 96, 256), lambda g, t: (g // 4, 0, g % 4))
    shape = jax.ShapeDtypeStruct((2, 96, 1024), low)
    return kernel_call(
        body,
        (8,),
        [cube_spec(), whole_spec((1536, 192))] + table_specs(),
        [out_spec, out_spec],
        [shape, shape],
        [],
        2 * 2048 * 1536 * 192,
        8 * 1024 * 1024,
        (at, normed, w_heads, *tables),
    )


def head_specs():
    kv = pl.BlockSpec((1, 96, 1024), lambda s, t, a: (s, 0, 0))
    other = pl.BlockSpec((1, 1, 96, 1024), lambda s, t, a: (0, s, 0, 0))
    other_far = pl.BlockSpec((1, 1, 96, 1024), lambda s, t, a: (1, s, 0, 0))
    return [kv, kv, other, other_far]


def key_and_value(core, own_ref, far_ref, other_ref, other_far_ref):
    mine = jnp.concatenate([own_ref[0], far_ref[0]], axis=1)
    theirs = jnp.concatenate([other_ref[0, 0], other_far_ref[0, 0]], axis=1)
    keyed = core == 0
    return jnp.where(keyed, mine, theirs), jnp.where(keyed, theirs, mine)


def masked(scores, key_column, query_ref, score_scale):
    return jnp.where(key_column <= query_ref[0], scores * (score_scale * log2_e), masked_score)


def attend_forward(at, queries, held, query_blk, key_blk, score_scale):
    def body(at_ref, q_ref, a_ref, b_ref, c_ref, d_ref, qb_ref, kb_ref, *rest):
        keep_ref, send_ref, att_ref, total_ref, k_scr, v_scr, kb_scr = rest

        @pl.when(pl.program_id(1) == 0)
        def _():
            key_part, value_part = key_and_value(at_ref[8], a_ref, b_ref, c_ref, d_ref)
            k_scr[...] = key_part.astype(wide).T.astype(low)
            v_scr[...] = value_part
            kb_scr[...] = jnp.broadcast_to(kb_ref[0], (128, 2048)).T[:, :1]

        scores = jnp.dot(k_scr[...], q_ref[0], preferred_element_type=wide)
        scores = masked(scores, kb_scr[...], qb_ref, score_scale)
        top = jnp.max(scores, axis=0, keepdims=True)
        likely = jnp.exp2(scores - top)
        column_sum = jnp.sum(likely, axis=0, keepdims=True)
        mixed = jnp.dot(v_scr[...], likely.astype(low), preferred_element_type=wide)
        mixed = mixed / column_sum
        att_ref[0] = mixed
        total_ref[0] = top + jnp.log(column_sum) * log2_e
        mixed = align(at_ref[8], mixed).astype(low)
        keep_ref[0] = mixed[:, :128]
        send_ref[0] = mixed[:, 128:]

    q_spec = pl.BlockSpec((1, 96, 256), lambda s, t, a: (s, 0, t))
    one_spec = pl.BlockSpec((1, 1, 256), lambda s, t, a: (s, 0, t))
    block_spec = pl.BlockSpec((1, 96, 128), lambda s, t, a: (s * 4 + t, 0, 0))
    return kernel_call(
        body,
        (2, 4),
        [q_spec]
        + head_specs()
        + [one_spec, pl.BlockSpec((1, 1, 2048), lambda s, t, a: (s, 0, 0))],
        [block_spec, block_spec, q_spec, one_spec],
        [
            jax.ShapeDtypeStruct((8, 96, 128), low),
            jax.ShapeDtypeStruct((8, 96, 128), low),
            jax.ShapeDtypeStruct((2, 96, 1024), wide),
            jax.ShapeDtypeStruct((2, 1, 1024), wide),
        ],
        [
            pltpu.VMEM((2048, 96), low),
            pltpu.VMEM((96, 2048), low),
            pltpu.VMEM((2048, 1), wide),
        ],
        4 * 2 * 1024 * 2048 * 96,
        12 * 1024 * 1024,
        (at, queries, *held, query_blk, key_blk),
        exps=2 * 1024 * 2048,
    )


def out_project(at, blocks, w_full, residual):
    def body(at_ref, in_ref, w_ref, x_ref, middle_ref, scale_ref, normed_ref, att_ref):
        for i in range(16):
            start = pl.multiple_of(at_ref[i] * 96, 96)
            att_ref[pl.ds(start, 96), :] = in_ref[i]
        rows = att_ref[...].astype(wide).T.astype(low)
        middle = x_ref[...] + jnp.dot(rows, w_ref[...], preferred_element_type=wide)
        scale = rms_scale(middle)
        middle_ref[...] = middle
        scale_ref[...] = scale
        normed_ref[...] = (middle * scale).astype(low)

    shapes = [
        jax.ShapeDtypeStruct((128, 1536), wide),
        jax.ShapeDtypeStruct((128, 1), wide),
        jax.ShapeDtypeStruct((128, 1536), low),
    ]
    return kernel_call(
        body,
        (1,),
        [whole_spec(a.shape) for a in (blocks, w_full, residual)],
        [whole_spec(shape.shape) for shape in shapes],
        shapes,
        [pltpu.VMEM((1536, 128), low)],
        2 * 128 * 1536 * 1536,
        6 * 1024 * 1024,
        (at, blocks, w_full, residual),
    )


def out_back(at, grad_out, sums, middle, scale, w_full):
    def body(at_ref, dy_ref, a_ref, b_ref, c_ref, x_ref, scale_ref, w_ref, *rest):
        middle_ref, low_ref, keep_ref, send_ref, scr = rest
        scaled = jnp.concatenate([a_ref[0], b_ref[0], c_ref[0]], axis=1)
        scale = scale_ref[...]
        normed = x_ref[...] * scale
        grad = dy_ref[...].astype(wide) + scale * (
            scaled - normed * jnp.mean(scaled * normed, axis=-1, keepdims=True)
        )
        middle_ref[...] = grad
        grad = grad.astype(low)
        low_ref[...] = grad
        scr[...] = times_back(w_ref[...], grad).astype(low)
        for i in range(8):
            start = pl.multiple_of(at_ref[i] * 96, 96)
            keep_ref[i] = scr[pl.ds(start, 96), :]
            start = pl.multiple_of(at_ref[8 + i] * 96, 96)
            send_ref[i] = scr[pl.ds(start, 96), :]

    args = (grad_out, *sums, middle, scale, w_full)
    shapes = [
        jax.ShapeDtypeStruct((128, 1536), wide),
        jax.ShapeDtypeStruct((128, 1536), low),
        jax.ShapeDtypeStruct((8, 96, 128), low),
        jax.ShapeDtypeStruct((8, 96, 128), low),
    ]
    return kernel_call(
        body,
        (1,),
        [whole_spec(a.shape) for a in args],
        [whole_spec(shape.shape) for shape in shapes],
        shapes,
        [pltpu.VMEM((1536, 128), low)],
        4 * 128 * 1536 * 1536,
        14 * 1024 * 1024,
        (at, *args),
    )


def attend_backward(
    at, queries, held, query_blk, key_blk, attention, totals, grad_blocks, tables, score_scale
):
    def body(at_ref, q_ref, a_ref, b_ref, c_ref, d_ref, qb_ref, kb_ref, *rest):
        att_ref, total_ref, cos_ref, sin_ref = rest[:4]
        own_ref, core_ref = rest[4:6]
        dq_ref, mine_ref, sent_ref = rest[6:9]
        k_scr, kt_scr, v_scr, dk_scr, dv_scr, kb_scr = rest[9:]
        tile = pl.program_id(1)

        @pl.when(tile == 0)
        def _():
            key_part, value_part = key_and_value(at_ref[8], a_ref, b_ref, c_ref, d_ref)
            kt_scr[...] = key_part
            kb_scr[...] = jnp.broadcast_to(kb_ref[0], (128, 2048)).T[:, :1]
            k_scr[...] = key_part.astype(wide).T.astype(low)
            v_scr[...] = value_part.astype(wide).T.astype(low)
            dk_scr[...] = jnp.zeros_like(dk_scr)
            dv_scr[...] = jnp.zeros_like(dv_scr)

        att = att_ref[0]
        grad_att = align(
            at_ref[8], jnp.concatenate([own_ref[0, 0], core_ref[0, 0]], axis=1).astype(wide)
        ).astype(low)
        delta = jnp.sum(grad_att.astype(wide) * att, axis=0, keepdims=True)
        scores = jnp.dot(k_scr[...], q_ref[0], preferred_element_type=wide)
        scores = masked(scores, kb_scr[...], qb_ref, score_scale)
        chance = jnp.exp2(scores - total_ref[0])
        dv_scr[...] += times_back(grad_att, chance.astype(low))
        grad_chance = jnp.dot(v_scr[...], grad_att, preferred_element_type=wide)
        grad_scores = (chance * (grad_chance - delta)).astype(low)
        grad_query = jnp.dot(kt_scr[...], grad_scores, preferred_element_type=wide)
        dq_ref[0] = turn_back(grad_query * score_scale, cos_ref[...], sin_ref[...]).astype(low)
        dk_scr[...] += times_back(q_ref[0], grad_scores)

        @pl.when(tile == 3)
        def _():
            grad_key = dk_scr[...] * score_scale
            grad_value = dv_scr[...]
            keyed = at_ref[8] == 0
            mine = jnp.where(keyed, grad_key, grad_value)
            sent = jnp.where(keyed, grad_value, grad_key)
            mine_ref[0, 0] = mine[:, :1024].astype(low)
            mine_ref[1, 0] = mine[:, 1024:].astype(low)
            sent_ref[0, 0] = sent[:, :1024].astype(low)
            sent_ref[1, 0] = sent[:, 1024:].astype(low)

    q_spec = pl.BlockSpec((1, 96, 256), lambda s, t, a: (s, 0, t))
    one_spec = pl.BlockSpec((1, 1, 256), lambda s, t, a: (s, 0, t))
    kv_out = pl.BlockSpec((2, 1, 96, 1024), lambda s, t, a: (0, s, 0, 0))
    angle = pl.BlockSpec((48, 256), lambda s, t, a: (0, t))

    def block_of(s, t):
        return (t & 1) * 4 + (t >> 1) * 2 + s

    return kernel_call(
        body,
        (2, 4),
        [q_spec]
        + head_specs()
        + [
            one_spec,
            pl.BlockSpec((1, 1, 2048), lambda s, t, a: (s, 0, 0)),
            q_spec,
            one_spec,
            angle,
            angle,
            pl.BlockSpec((1, 1, 96, 128), lambda s, t, a: (block_of(s, t), 0, 0, 0)),
            pl.BlockSpec((1, 1, 96, 128), lambda s, t, a: (block_of(s, t), 1, 0, 0)),
        ],
        [q_spec, kv_out, kv_out],
        [
            jax.ShapeDtypeStruct((2, 96, 1024), low),
            jax.ShapeDtypeStruct((2, 2, 96, 1024), low),
            jax.ShapeDtypeStruct((2, 2, 96, 1024), low),
        ],
        [
            pltpu.VMEM((2048, 96), low),
            pltpu.VMEM((96, 2048), low),
            pltpu.VMEM((2048, 96), low),
            pltpu.VMEM((96, 2048), wide),
            pltpu.VMEM((96, 2048), wide),
            pltpu.VMEM((2048, 1), wide),
        ],
        10 * 2 * 1024 * 2048 * 96,
        12 * 1024 * 1024,
        (
            at,
            queries,
            *held,
            query_blk,
            key_blk,
            attention,
            totals,
            *tables[:2],
            grad_blocks,
            grad_blocks,
        ),
        exps=2 * 1024 * 2048,
    )


def head_grads(dq_ref, ds_ref, cos_ref, sin_ref):
    own = turn_back(ds_ref[0], cos_ref[...], sin_ref[...])
    return jnp.concatenate([dq_ref[0].astype(wide), own], axis=0)


def head_grad_specs():
    q_spec = pl.BlockSpec((1, 96, 256), lambda g, t: (g // 4, 0, g % 4))
    return table_specs()[:2] + [q_spec, q_spec]


def head_weights(at, normed, tables, grad_queries, grad_own):
    def body(at_ref, rows_ref, cos_ref, sin_ref, dq_ref, ds_ref, *rest):
        keep_ref, send_ref, gw_scr, nat_scr = rest
        g = pl.program_id(0)

        @pl.when(g == 0)
        def _():
            gw_scr[...] = jnp.zeros_like(gw_scr)

        both = head_grads(dq_ref, ds_ref, cos_ref, sin_ref)
        gw_scr[...] += jnp.dot(both.astype(low), rows_ref[...], preferred_element_type=wide)

        @pl.when(g == 7)
        def _():
            nat_scr[...] = gw_scr[...].T
            for i in range(8):
                start = pl.multiple_of(at_ref[9 + i] * 96, 96)
                keep_ref[i] = nat_scr[pl.ds(start, 96), :].astype(low)
                start = pl.multiple_of(at_ref[17 + i] * 96, 96)
                send_ref[i] = nat_scr[pl.ds(start, 96), :].astype(low)

    blocks = jax.ShapeDtypeStruct((8, 96, 192), low)
    return kernel_call(
        body,
        (8,),
        [cube_spec()] + head_grad_specs(),
        [whole_spec((8, 96, 192))] * 2,
        [blocks, blocks],
        [pltpu.VMEM((192, 1536), wide), pltpu.VMEM((1536, 192), wide)],
        2 * 2048 * 1536 * 192,
        8 * 1024 * 1024,
        (at, normed, *tables[2:], grad_queries, grad_own),
    )


def project_back(at, w_heads, tables, grad_queries, grad_own):
    def body(at_ref, w_ref, cos_ref, sin_ref, dq_ref, ds_ref, *outs):
        both = align(at_ref[8], head_grads(dq_ref, ds_ref, cos_ref, sin_ref))
        store_rows(outs, times_back(both.T.astype(low), w_ref[...]))

    return kernel_call(
        body,
        (8,),
        [whole_spec((1536, 192))] + head_grad_specs(),
        row_specs(THIRDS, lambda g, t: g),
        row_shapes(THIRDS),
        [],
        2 * 2048 * 1536 * 192,
        8 * 1024 * 1024,
        (at, w_heads, *tables[2:], grad_queries, grad_own),
    )


def hidden_back(at, grads, w_rows):
    def body(at_ref, *refs):
        rows, (w_ref, out_ref) = refs[:4], refs[4:]
        out_ref[...] = align_rows(at_ref[8], times_back(load_rows(rows), w_ref[...]))

    return kernel_call(
        body,
        (8,),
        row_specs(HALVES, lambda g, t: g) + [whole_spec((256, 1536))],
        pl.BlockSpec((256, 256), lambda g, t: (g, 0)),
        jax.ShapeDtypeStruct((2048, 256), wide),
        [],
        2 * 2048 * 1536 * 256,
        8 * 1024 * 1024,
        (at, *flat(grads), w_rows),
    )


def feed_back(at, normed, w_both, grad_hidden):
    def body(at_ref, rows_ref, w_ref, dh_ref, *rest):
        outs, (hidden_ref, both_ref) = rest[:6], rest[6:]
        both = jnp.dot(rows_ref[...], w_ref[...], preferred_element_type=wide)
        gate, up = both[:, :256], both[:, 256:]
        bend = jax.nn.sigmoid(gate)
        smooth = gate * bend
        grad_hidden = dh_ref[...]
        hidden_ref[...] = (smooth * up).astype(low)
        grad_gate = grad_hidden * up * (bend + smooth * (1.0 - bend))
        grad_both = jnp.concatenate([grad_gate, grad_hidden * smooth], axis=1).astype(low)
        both_ref[...] = grad_both
        store_rows(outs, align_rows(at_ref[8], times_back(grad_both, w_ref[...])))

    return kernel_call(
        body,
        (8,),
        [cube_spec(), whole_spec((1536, 512)), pl.BlockSpec((256, 256), lambda g, t: (g, 0))],
        row_specs(THIRDS, lambda g, t: g)
        + [
            pl.BlockSpec((256, 256), lambda g, t: (g, 0)),
            pl.BlockSpec((256, 512), lambda g, t: (g, 0)),
        ],
        row_shapes(THIRDS)
        + [
            jax.ShapeDtypeStruct((2048, 256), low),
            jax.ShapeDtypeStruct((2048, 512), low),
        ],
        [],
        4 * 2048 * 1536 * 512,
        18 * 1024 * 1024,
        (at, normed, w_both, grad_hidden),
        exps=2048 * 256,
    )


def feed_out(at, hidden, w_rows):
    def body(at_ref, hidden_ref, w_ref, *outs):
        made = jnp.dot(hidden_ref[...], w_ref[...], preferred_element_type=wide)
        store_rows(outs, align_rows(at_ref[8], made))

    return kernel_call(
        body,
        (8,),
        [pl.BlockSpec((256, 256), lambda g, t: (g, 0)), whole_spec((256, 1536))],
        row_specs(HALVES, lambda g, t: g),
        row_shapes(HALVES),
        [],
        2 * 2048 * 1536 * 256,
        8 * 1024 * 1024,
        (at, hidden, w_rows),
    )


def down_weights(at, hidden, grads):
    def body(at_ref, *refs):
        rows, (hidden_ref, gw_ref, gw_scr) = refs[:4], refs[4:]
        g = pl.program_id(0)

        @pl.when(g == 0)
        def _():
            gw_scr[...] = jnp.zeros_like(gw_scr)

        held = align_rows(at_ref[8], hidden_ref[...].astype(wide)).astype(low)
        gw_scr[...] += over_rows(held, load_rows(rows))

        @pl.when(g == 7)
        def _():
            gw_ref[...] = gw_scr[...].astype(low)

    return kernel_call(
        body,
        (8,),
        row_specs(HALVES, lambda g, t: g) + [pl.BlockSpec((256, 256), lambda g, t: (g, 0))],
        whole_spec((256, 1536)),
        jax.ShapeDtypeStruct((256, 1536), low),
        [pltpu.VMEM((256, 1536), wide)],
        2 * 2048 * 1536 * 256,
        8 * 1024 * 1024,
        (at, *flat(grads), hidden),
    )


def out_weights(at, attention, grads):
    def body(at_ref, att_ref, rows_ref, gw_ref, gw_scr):
        g = pl.program_id(0)

        @pl.when(g == 0)
        def _():
            gw_scr[...] = jnp.zeros_like(gw_scr)

        gw_scr[...] += jnp.dot(
            att_ref[0].astype(low), rows_ref[...], preferred_element_type=wide
        )

        @pl.when(g == 7)
        def _():
            gw_ref[...] = gw_scr[...].astype(low)

    return kernel_call(
        body,
        (8,),
        [pl.BlockSpec((1, 96, 256), lambda g, t: (g // 4, 0, g % 4)), cube_spec()],
        whole_spec((96, 1536)),
        jax.ShapeDtypeStruct((96, 1536), low),
        [pltpu.VMEM((96, 1536), wide)],
        2 * 2048 * 1536 * 96,
        8 * 1024 * 1024,
        (at, attention, grads),
    )


def feed_weights(at, normed, grad_both):
    def body(at_ref, rows_ref, both_ref, keep_ref, send_ref, gw_scr, nat_scr):
        g = pl.program_id(0)

        @pl.when(g == 0)
        def _():
            gw_scr[...] = jnp.zeros_like(gw_scr)

        gw_scr[...] += over_rows(both_ref[...], rows_ref[...])

        @pl.when(g == 7)
        def _():
            nat_scr[...] = gw_scr[...].T
            for i in range(8):
                start = pl.multiple_of(at_ref[9 + i] * 96, 96)
                keep_ref[i] = nat_scr[pl.ds(start, 96), :].astype(low)
                start = pl.multiple_of(at_ref[17 + i] * 96, 96)
                send_ref[i] = nat_scr[pl.ds(start, 96), :].astype(low)

    return kernel_call(
        body,
        (8,),
        [cube_spec(), pl.BlockSpec((256, 512), lambda g, t: (g, 0))],
        [whole_spec((8, 96, 512))] * 2,
        [jax.ShapeDtypeStruct((8, 96, 512), low)] * 2,
        [pltpu.VMEM((512, 1536), wide), pltpu.VMEM((1536, 512), wide)],
        2 * 2048 * 1536 * 512,
        14 * 1024 * 1024,
        (at, normed, grad_both),
    )


def sum_low(left, right):
    return (left.astype(wide) + right.astype(wide)).astype(low)


def cube_plan(
    inputs,
    cotangent,
    block_ids,
    piece_order,
    w_query,
    w_key,
    w_value,
    w_out,
    w_gate,
    w_up,
    w_down,
    gain_attn,
    gain_mlp,
):
    x = lax.axis_index("grp")
    seq_at = lax.axis_index("seq")
    zh, c = seq_at >> 3, seq_at & 1
    score_scale = HEAD_DIM ** (-0.5)
    gain_rows_attn = gain_attn.astype(wide)[:, None]
    gain_rows_mlp = gain_mlp.astype(wide)[:, None]
    eight = jnp.arange(8, dtype=jnp.int32)
    sixteen = jnp.arange(16, dtype=jnp.int32)
    cyl = (eight >> 2) + (eight & 2) + ((eight & 1) << 2)
    place = c.astype(jnp.int32)[None]
    natural = seq_at ^ sixteen

    def owns_out(i):
        return bit_of(i, BIT_X) == bit_of(i, BIT_ZH)

    def owns_down(i):
        return bit_of(i, BIT_X) ^ bit_of(i, BIT_C) == bit_of(i, BIT_ZH)

    def lacks_out(i):
        return not owns_out(i)

    def lacks_down(i):
        return not owns_down(i)

    out_owner, down_owner = x == zh, (x ^ c) == zh

    order = ((sixteen & 8)) | ((sixteen & 4) >> 1) | ((sixteen & 2) << 1) | (sixteen & 1)
    stored = (seq_at & 14) ^ order
    pieces = jnp.sum(
        jnp.where(stored[:, None] == sixteen[None, :], piece_order[None, :], 0), axis=1
    )
    own_pos = (pieces[:8, None] * 128 + jnp.arange(128, dtype=jnp.int32)[None, :]).reshape(1024)
    frequency = rope_base ** (-jnp.arange(HEAD_DIM // 2, dtype=wide) * 2.0 / HEAD_DIM)
    angles = frequency[:, None] * own_pos.astype(wide)[None, :]
    cosine, sine = jnp.cos(angles), jnp.sin(angles)
    keyed = c == 0
    tables = (
        cosine,
        sine,
        jnp.where(keyed, cosine, 1.0),
        jnp.where(keyed, sine, 0.0),
    )

    low_zy = ((eight & 1) << 2) | (eight & 2)
    side_of = x ^ (eight >> 2)
    spots = jnp.concatenate([side_of * 4 + (((seq_at ^ low_zy) & 7) >> 1), place])
    spots_rows = jnp.concatenate([spots, natural])
    head_for = jnp.concatenate(
        [side_of * 8 + ((seq_at ^ low_zy ^ core) & 7) for core in (0, 1)]
    )

    residual = inputs[0].astype(wide)
    scale_first = rms_scale(residual)
    normed_first = residual * scale_first
    normed = cube_gather(normed_first.astype(low))
    head_of = x * 8 + ((seq_at ^ cyl) & 7)
    heads = pick_heads(head_of, w_query, w_key, w_value, gain_rows_attn)
    heads = trade_block(heads.reshape(2, 2, 2, 96, 192), 0, BIT_C)
    heads, w_out_held = sync(heads, w_out)
    out_near = swap(w_out_held, BIT_ZH, owns_out)
    heads = trade_block(heads, 1, BIT_Y)
    heads, ids_held, up_held = sync(heads, block_ids, w_up)
    heads = trade_block(heads, 2, BIT_ZL)
    other_ids = swap(ids_held, BIT_X)
    wanted_mlp = (x ^ ((seq_at ^ cyl) & 1)) * 8 + ((seq_at ^ cyl) & 7)
    both_blocks = pick_columns(wanted_mlp, w_gate, up_held, gain_rows_mlp)
    heads, out_near, both_blocks = sync(heads, out_near, both_blocks)
    heads = heads.reshape(8, 96, 192)
    heads_far = swap(heads, BIT_ZH)
    both_blocks = trade_block(both_blocks.reshape(2, 2, 2, 96, 512), 0, BIT_C)
    both_blocks = trade_block(both_blocks, 1, BIT_Y)
    both_blocks = trade_block(both_blocks, 2, BIT_ZL)
    w_out_head = jnp.where(out_owner, w_out, out_near)
    heads, heads_far, both_blocks, w_down_held, tables = sync(
        heads, heads_far, both_blocks, w_down, tables
    )
    w_heads = assemble_rows(natural, heads, heads_far)
    ids = jnp.concatenate([block_ids, other_ids], axis=0).reshape(2, 16, 128)
    chosen = (pieces[:, None] == sixteen[None, :]).astype(low)
    blocks = jnp.einsum(
        "kp,spr->skr", chosen, ids.astype(low), preferred_element_type=wide
    ).reshape(2, 1, 2048)
    query_blk, key_blk = blocks[:, :, :1024], blocks
    normed, w_heads, both_blocks, w_out_head, query_blk, key_blk, rows_dy = sync(
        normed, w_heads, both_blocks, w_out_head, query_blk, key_blk, cotangent[0]
    )

    out_full = cube_gather(w_out_head)
    grads = gather_next(gather_start(rows_dy, HALVES), HALVES, 0)
    queries, own_part = project(spots, normed, w_heads, tables)
    queries, own_part, grads, both_blocks = sync(queries, own_part, grads, both_blocks)
    far_part = swap(own_part, BIT_ZH)
    grads = gather_next(grads, HALVES, 1)
    far_part, grads, both_blocks = sync(far_part, grads, both_blocks)
    other_parts = swap(jnp.stack([own_part, far_part]), BIT_C)
    other_parts, far_part, grads = sync(other_parts, far_part, grads)
    held = (own_part, far_part, other_parts, other_parts)
    grads = gather_next(grads, HALVES, 2)
    near_rows = [both_blocks[0].reshape(4, 96, 512), both_blocks[1].reshape(4, 96, 512)]
    far_first = swap(near_rows[0], BIT_ZH)
    keep, send, attention, totals = attend_forward(
        spots, queries, held, query_blk, key_blk, score_scale
    )
    keep, send, attention, totals, near_rows, out_full, w_down_held = sync(
        keep, send, attention, totals, near_rows, out_full, w_down_held
    )

    traded = jnp.stack([keep, swap(send, BIT_C)]).reshape(2, 2, 2, 2, 96, 128)
    traded, far_first, w_down_held = sync(traded, far_first, w_down_held)
    traded = trade_block(traded, 3, BIT_ZL)
    traded, grads, w_down_held = sync(traded, grads, w_down_held)
    down_near = swap(w_down_held, BIT_ZH, owns_down)
    grads = gather_last(grads)
    traded = trade_block(traded, 2, BIT_X)
    traded, grads = sync(traded, grads)
    traded = trade_block(traded, 3, BIT_Y).reshape(16, 96, 128)
    traded, residual, down_near, near_rows = sync(traded, residual, down_near, near_rows)
    far_second = swap(near_rows[1], BIT_ZH)
    yxlc = ((sixteen & 8) >> 2) | ((sixteen & 2) << 1) | (sixteen & 1)
    head_from = (x ^ ((sixteen & 4) >> 2)) * 8 + ((seq_at ^ yxlc) & 7)
    middle, scale_second, rows_second = out_project(head_from, traded, out_full, residual)

    rows_second, middle, scale_second, grads = sync(rows_second, middle, scale_second, grads)
    normed_mlp = cube_gather(rows_second)
    w_rows = jnp.where(down_owner, w_down_held, down_near)
    grad_hidden = hidden_back(spots, grads, w_rows)
    w_both = assemble_rows(natural, *near_rows, far_first, far_second)
    normed_mlp, grad_hidden, w_both = sync(normed_mlp, grad_hidden, w_both)
    made = feed_back(spots, normed_mlp, w_both, grad_hidden)
    hidden, grad_both = made[6:]
    sums = scatter_start(paired(made[:6]))
    sums, hidden, grad_both = sync(sums, hidden, grad_both)
    sums = scatter_next(sums, THIRDS, 2)
    keep_both, send_both = feed_weights(spots_rows, normed_mlp, grad_both)
    sums, keep_both, send_both = sync(sums, keep_both, send_both)
    sums = scatter_next(sums, THIRDS, 1)
    sums, = sync(sums)
    sums = scatter_next(sums, THIRDS, 0)
    sums, hidden, send_both = sync(sums, hidden, send_both)

    parts = scatter_last(sums)
    grad_middle, grad_low, keep, send = out_back(
        head_for, cotangent[0], parts, middle, scale_second, out_full
    )
    grad_middle, grad_low, keep, send, hidden, send_both = sync(
        grad_middle, grad_low, keep, send, hidden, send_both
    )
    middle_rows = cube_gather(grad_low)
    arrived_second = swap(send_both[4:], BIT_ZH)
    traded = jnp.stack([keep, swap(send, BIT_C)]).reshape(2, 2, 2, 2, 96, 128)
    traded, hidden = sync(traded, hidden)
    grad_down = down_weights(spots, hidden, grads)
    traded = trade_block(traded, 1, BIT_X)
    traded, grad_down, hidden, arrived_second, send_both = sync(
        traded, grad_down, hidden, arrived_second, send_both
    )
    arrived_first = swap(send_both[:4], BIT_ZH)
    out_terms = feed_out(spots, hidden, w_rows)
    traded = trade_block(traded, 2, BIT_Y)
    traded, grad_down, out_terms = sync(traded, grad_down, out_terms)
    traded = trade_block(traded, 3, BIT_ZL).reshape(8, 2, 96, 128)
    out_sums = scatter_start(paired(out_terms))
    both_send = sum_low(keep_both[4:], arrived_second)
    traded, out_sums, arrived_first, both_send, grad_down = sync(
        traded, out_sums, arrived_first, both_send, grad_down
    )
    out_sums = scatter_next(out_sums, HALVES, 2)
    down_arrived = swap(grad_down, BIT_ZH, lacks_down)
    both_sent = swap(both_send, BIT_ZL)
    made = attend_backward(
        spots,
        queries,
        held,
        query_blk,
        key_blk,
        attention,
        totals,
        traded,
        tables,
        score_scale,
    )
    made, out_sums, down_arrived, both_sent = sync(made, out_sums, down_arrived, both_sent)
    grad_queries, mine, sent = made
    both_sum = jnp.stack([sum_low(keep_both[:4], arrived_first), both_sent])
    arrived = swap(sent, BIT_C)
    arrived, both_sum, grad_down = sync(arrived, both_sum, grad_down)
    far_terms = sum_low(mine[1], arrived[1])
    far_terms, out_sums, both_sum, attention, middle_rows = sync(
        [far_terms[0], far_terms[1]], out_sums, both_sum, attention, middle_rows
    )
    far_first = swap(far_terms[0], BIT_ZH)
    out_sums = scatter_next(out_sums, HALVES, 1)
    grad_out_head = out_weights(spots, attention, middle_rows)
    far_first, far_terms, out_sums, both_sum, grad_out_head, grad_down = sync(
        far_first, far_terms, out_sums, both_sum, grad_out_head, grad_down
    )
    far_second = swap(far_terms[1], BIT_ZH)
    both_sum = trade_block(both_sum.reshape(2, 2, 2, 96, 512), 1, BIT_Y)
    down_sum = sum_low(grad_down, down_arrived)
    down_far = swap(down_sum, BIT_X, owns_down)
    far_second, both_sum, out_sums = sync(far_second, both_sum, out_sums)
    out_sums = scatter_next(out_sums, HALVES, 0)
    both_near = trade_block(both_sum, 2, BIT_C).reshape(8, 96, 512)
    grad_own = (
        mine[0].astype(wide)
        + arrived[0].astype(wide)
        + jnp.stack([far_first, far_second]).astype(wide)
    )
    keep_heads, send_heads = head_weights(
        spots_rows, normed, tables, grad_queries, grad_own
    )
    keep_heads, send_heads, grad_own, both_near, down_far = sync(
        keep_heads, send_heads, grad_own, both_near, down_far
    )
    both_far = swap(both_near, BIT_X)
    heads_first = swap(send_heads, BIT_ZH)
    made = project_back(spots, w_heads, tables, grad_queries, grad_own)
    made, heads_first, both_far, out_sums = sync(made, heads_first, both_far, out_sums)
    sums = scatter_start(paired(made))
    heads_sum = sum_low(keep_heads, heads_first)
    sums, heads_sum = sync(sums, heads_sum)
    heads_sum = trade_block(heads_sum.reshape(2, 2, 2, 96, 192), 0, BIT_ZL)
    sums = scatter_next(sums, THIRDS, 2)
    sums, heads_sum, grad_out_head = sync(sums, heads_sum, grad_out_head)
    out_arrived = swap(grad_out_head, BIT_ZH, lacks_out)
    output = jnp.concatenate([part[0] for part in scatter_last(out_sums)], axis=1)
    output = (middle + output).astype(low)
    heads_sum = trade_block(heads_sum, 1, BIT_Y)
    sums = scatter_next(sums, THIRDS, 1)
    sums, output, heads_sum = sync(sums, output, heads_sum)
    heads_near = trade_block(heads_sum, 2, BIT_C).reshape(8, 96, 192)
    heads_far = swap(heads_near, BIT_X)
    sums = scatter_next(sums, THIRDS, 0)
    sums, heads_far, out_arrived = sync(sums, heads_far, out_arrived)
    out_sum = sum_low(grad_out_head, out_arrived)
    out_far = swap(out_sum, BIT_X, owns_out)
    scaled_first = jnp.concatenate([part[0] for part in scatter_last(sums)], axis=1)
    grad_inputs = grad_middle + scale_first * (
        scaled_first
        - normed_first * jnp.mean(scaled_first * normed_first, axis=-1, keepdims=True)
    )

    back = seq_at ^ cyl
    home = jnp.concatenate([x * 8 + (back & 7), (1 - x) * 8 + (back & 7)])
    grad_w_query, grad_w_key, grad_w_value, grad_gain_attn = spread_heads(
        home, heads_near, heads_far, w_query, w_key, w_value, gain_rows_attn
    )
    grad_w_out = jnp.where(out_owner, out_sum, out_far).astype(wide)
    grad_w_down = jnp.where(down_owner, down_sum, down_far).astype(wide)
    side = (back & 1) ^ x
    home = jnp.concatenate([side * 8 + (back & 7), (1 - side) * 8 + (back & 7)])
    grad_w_gate, grad_w_up, grad_gain_mlp = spread_columns(
        home, both_near, both_far, gain_rows_mlp, w_gate, w_up
    )
    return (
        output[None],
        grad_inputs.astype(low)[None],
        grad_w_query,
        grad_w_key,
        grad_w_value,
        grad_w_out,
        grad_w_gate,
        grad_w_up,
        grad_w_down,
        grad_gain_attn[:, 0],
        grad_gain_mlp[:, 0],
    )


def ring_plan(
    inputs,
    cotangent,
    block_ids,
    piece_order,
    w_query,
    w_key,
    w_value,
    w_out,
    w_gate,
    w_up,
    w_down,
    gain_attn,
    gain_mlp,
):
    shards = (w_query, w_key, w_value, w_out, w_gate, w_up, w_down, gain_attn, gain_mlp)
    (
        full_query,
        full_key,
        full_value,
        full_out,
        full_gate,
        full_up,
        full_down,
        gain_one,
        gain_two,
    ) = (
        lax.all_gather(shards[0], "seq", axis=0, tiled=True),
        lax.all_gather(shards[1], "seq", axis=0, tiled=True),
        lax.all_gather(shards[2], "seq", axis=0, tiled=True),
        lax.all_gather(shards[3], "seq", axis=0, tiled=True),
        lax.all_gather(shards[4], "seq", axis=0, tiled=True),
        lax.all_gather(shards[5], "seq", axis=0, tiled=True),
        lax.all_gather(shards[6], "seq", axis=0, tiled=True),
        lax.all_gather(shards[7], "seq", axis=0, tiled=True),
        lax.all_gather(shards[8], "seq", axis=0, tiled=True),
    )
    seq_count, tok_rows, model_width = inputs.shape
    row_count = seq_count * tok_rows
    head_count = HEADS
    kv_heads = KV_HEADS
    head_dim = HEAD_DIM
    groups = head_count // kv_heads
    kv_width = kv_heads * head_dim
    q_width = head_count * head_dim
    score_scale = head_dim ** (-0.5)
    own_first = jnp.take(piece_order, lax.axis_index("seq")) * tok_rows
    local_pos = own_first + jnp.arange(tok_rows, dtype=jnp.int32)
    cosine_table, sine_table = rotary_tables(local_pos, head_dim)
    query_blk = jnp.take(block_ids, local_pos, axis=1)

    def key_positions(key_count):
        stored = jnp.arange(key_count, dtype=jnp.int32)
        return jnp.take(piece_order, stored // tok_rows) * tok_rows + stored % tok_rows

    residual = inputs.reshape(row_count, model_width).astype(jnp.float32)
    gain_first = gain_one.astype(jnp.float32)
    gain_second = gain_two.astype(jnp.float32)
    scale_first = rms_scale(residual)
    normed_attn = (residual * scale_first * gain_first).astype(jnp.bfloat16)
    query_pre = jnp.dot(normed_attn, full_query, preferred_element_type=jnp.float32)
    key_pre = jnp.dot(normed_attn, full_key, preferred_element_type=jnp.float32)
    value_pre = jnp.dot(normed_attn, full_value, preferred_element_type=jnp.float32)
    queries = rotate(
        query_pre.reshape(seq_count, tok_rows, head_count, head_dim), cosine_table, sine_table
    ).astype(jnp.bfloat16)
    key_rot = rotate(
        key_pre.reshape(seq_count, tok_rows, kv_heads, head_dim), cosine_table, sine_table
    ).astype(jnp.bfloat16)
    values = value_pre.astype(jnp.bfloat16)
    kv_local = jnp.concatenate(
        [
            key_rot.reshape(seq_count, tok_rows, kv_width),
            values.reshape(seq_count, tok_rows, kv_width),
        ],
        axis=2,
    )
    query_grouped = queries.reshape(seq_count, tok_rows, kv_heads, groups, head_dim)
    start_max = jnp.full((seq_count, kv_heads, groups, tok_rows), masked_score, jnp.float32)
    start_sum = jnp.zeros((seq_count, kv_heads, groups, tok_rows), jnp.float32)
    start_acc = jnp.zeros((seq_count, kv_heads, groups, tok_rows, head_dim), jnp.float32)
    state_in = (start_max, start_sum, start_acc)
    key_piece = lax.all_gather(kv_local, "seq", axis=1, tiled=True)
    key_count = key_piece.shape[1]
    block_rows = key_block_rows(key_count)
    key_pos = key_positions(key_count)
    member = 0
    key_blk = jnp.take(block_ids[member], key_pos).reshape(key_count // block_rows, block_rows)
    kv_rows = key_piece[member].reshape(key_count // block_rows, block_rows, 2 * kv_width)
    own_query = query_grouped[member]
    own_blocks = query_blk[member]

    def forward_key_step(running, block_in):
        kv_block, blk_block = block_in
        key_part = kv_block[:, :kv_width].reshape(block_rows, kv_heads, head_dim)
        value_part = kv_block[:, kv_width:].reshape(block_rows, kv_heads, head_dim)
        running = forward_block(
            running, own_query, own_blocks, key_part, value_part, blk_block, score_scale
        )
        return (running, None)

    running, unused = lax.scan(
        forward_key_step,
        (state_in[0][member], state_in[1][member], state_in[2][member]),
        (kv_rows, key_blk),
    )
    results = [running]
    row_max = jnp.stack([entry[0] for entry in results])
    row_sum = jnp.stack([entry[1] for entry in results])
    running_sum = jnp.stack([entry[2] for entry in results])
    log_total = row_max + jnp.log(row_sum)
    attention = running_sum / row_sum[..., None]
    attended = (
        jnp.transpose(attention, (0, 3, 1, 2, 4)).reshape(row_count, q_width).astype(jnp.bfloat16)
    )
    middle = residual + jnp.dot(attended, full_out, preferred_element_type=jnp.float32)
    scale_second = rms_scale(middle)
    normed_mlp = (middle * scale_second * gain_second).astype(jnp.bfloat16)
    gate_value = jnp.dot(normed_mlp, full_gate, preferred_element_type=jnp.float32)
    upward = jnp.dot(normed_mlp, full_up, preferred_element_type=jnp.float32)
    sigmoid_gate = jax.nn.sigmoid(gate_value)
    hidden = (gate_value * sigmoid_gate * upward).astype(jnp.bfloat16)
    output = (middle + jnp.dot(hidden, full_down, preferred_element_type=jnp.float32)).astype(
        jnp.bfloat16
    )
    (
        full_query,
        full_key,
        full_value,
        full_out,
        full_gate,
        full_up,
        full_down,
        gain_one,
        gain_two,
    ) = (
        lax.all_gather(shards[0], "seq", axis=0, tiled=True),
        lax.all_gather(shards[1], "seq", axis=0, tiled=True),
        lax.all_gather(shards[2], "seq", axis=0, tiled=True),
        lax.all_gather(shards[3], "seq", axis=0, tiled=True),
        lax.all_gather(shards[4], "seq", axis=0, tiled=True),
        lax.all_gather(shards[5], "seq", axis=0, tiled=True),
        lax.all_gather(shards[6], "seq", axis=0, tiled=True),
        lax.all_gather(shards[7], "seq", axis=0, tiled=True),
        lax.all_gather(shards[8], "seq", axis=0, tiled=True),
    )
    gain_first = gain_one.astype(jnp.float32)
    gain_second = gain_two.astype(jnp.float32)
    upstream = cotangent.reshape(row_count, model_width)
    grad_down = over_rows(hidden, upstream)
    grad_hidden = times_back(upstream, full_down)
    grad_gate = (
        grad_hidden * upward * sigmoid_gate * (1.0 + gate_value * (1.0 - sigmoid_gate))
    ).astype(jnp.bfloat16)
    grad_upward = (grad_hidden * gate_value * sigmoid_gate).astype(jnp.bfloat16)
    grad_w_gate = over_rows(normed_mlp, grad_gate)
    grad_w_up = over_rows(normed_mlp, grad_upward)
    grad_normed_mlp = times_back(grad_gate, full_gate) + times_back(grad_upward, full_up)
    grad_mid_norm, grad_gain_mlp = norm_back(grad_normed_mlp, middle, scale_second, gain_second)
    grad_middle = upstream.astype(jnp.float32) + grad_mid_norm
    grad_middle_low = grad_middle.astype(jnp.bfloat16)
    grad_w_out = over_rows(attended, grad_middle_low)
    grad_attended = times_back(grad_middle_low, full_out).astype(jnp.bfloat16)
    grad_heads = jnp.transpose(
        grad_attended.reshape(seq_count, tok_rows, kv_heads, groups, head_dim), (0, 2, 3, 1, 4)
    )
    delta_rows = jnp.sum(grad_heads.astype(jnp.float32) * attention, axis=-1)
    start_query = jnp.zeros((seq_count, kv_heads, groups, tok_rows, head_dim), jnp.float32)
    start_kv = jnp.zeros((seq_count, block_ids.shape[1], 2 * kv_width), jnp.float32)
    state_in = (start_query, start_kv)
    key_piece = lax.all_gather(kv_local, "seq", axis=1, tiled=True)
    key_count = key_piece.shape[1]
    backward_block_rows = key_block_rows(key_count)
    key_pos = key_positions(key_count)
    member = 0
    key_blk = jnp.take(block_ids[member], key_pos).reshape(
        key_count // backward_block_rows, backward_block_rows
    )
    kv_rows = key_piece[member].reshape(
        key_count // backward_block_rows, backward_block_rows, 2 * kv_width
    )
    backward_own_query = query_grouped[member]
    backward_own_blocks = query_blk[member]
    own_total = log_total[member]
    own_grads = grad_heads[member]
    own_delta = delta_rows[member]

    def backward_key_step(grad_query, block_in):
        kv_block, blk_block = block_in
        key_part = kv_block[:, :kv_width].reshape(backward_block_rows, kv_heads, head_dim)
        value_part = kv_block[:, kv_width:].reshape(backward_block_rows, kv_heads, head_dim)
        result = backward_block(
            grad_query,
            backward_own_query,
            backward_own_blocks,
            key_part,
            value_part,
            blk_block,
            own_total,
            own_grads,
            own_delta,
            score_scale,
        )
        return (result[0], (result[1], result[2]))

    grad_query, key_grads = lax.scan(backward_key_step, state_in[0][member], (kv_rows, key_blk))
    fresh = jnp.concatenate(
        [key_grads[0].reshape(key_count, kv_width), key_grads[1].reshape(key_count, kv_width)],
        axis=1,
    )
    query_grads = [grad_query]
    kv_grads = [fresh]
    grad_query_all = jnp.stack(query_grads)
    grad_kv_all = jnp.stack(kv_grads)
    grad_kv_own = lax.psum_scatter(grad_kv_all, "seq", scatter_dimension=1, tiled=True)
    grad_query_rows = jnp.transpose(grad_query_all, (0, 3, 1, 2, 4)).reshape(
        seq_count, tok_rows, head_count, head_dim
    )
    grad_query_pre = (
        unrotate(grad_query_rows, cosine_table, sine_table)
        .reshape(row_count, q_width)
        .astype(jnp.bfloat16)
    )
    grad_key_rows = grad_kv_own[:, :, :kv_width].reshape(seq_count, tok_rows, kv_heads, head_dim)
    grad_key_pre = (
        unrotate(grad_key_rows, cosine_table, sine_table)
        .reshape(row_count, kv_width)
        .astype(jnp.bfloat16)
    )
    grad_value_pre = grad_kv_own[:, :, kv_width:].reshape(row_count, kv_width).astype(jnp.bfloat16)
    grad_w_query = over_rows(normed_attn, grad_query_pre)
    grad_w_key = over_rows(normed_attn, grad_key_pre)
    grad_w_value = over_rows(normed_attn, grad_value_pre)
    grad_normed_attn = (
        times_back(grad_query_pre, full_query)
        + times_back(grad_key_pre, full_key)
        + times_back(grad_value_pre, full_value)
    )
    grad_in_norm, grad_gain_attn = norm_back(grad_normed_attn, residual, scale_first, gain_first)
    grad_inputs = (
        (grad_middle + grad_in_norm).astype(jnp.bfloat16).reshape(seq_count, tok_rows, model_width)
    )
    terms = (
        grad_w_query,
        grad_w_key,
        grad_w_value,
        grad_w_out,
        grad_w_gate,
        grad_w_up,
        grad_down,
        grad_gain_attn,
        grad_gain_mlp,
    )
    shares = (
        lax.psum_scatter(terms[0], "seq", scatter_dimension=0, tiled=True),
        lax.psum_scatter(terms[1], "seq", scatter_dimension=0, tiled=True),
        lax.psum_scatter(terms[2], "seq", scatter_dimension=0, tiled=True),
        lax.psum_scatter(terms[3], "seq", scatter_dimension=0, tiled=True),
        lax.psum_scatter(terms[4], "seq", scatter_dimension=0, tiled=True),
        lax.psum_scatter(terms[5], "seq", scatter_dimension=0, tiled=True),
        lax.psum_scatter(terms[6], "seq", scatter_dimension=0, tiled=True),
        lax.psum_scatter(terms[7], "seq", scatter_dimension=0, tiled=True),
        lax.psum_scatter(terms[8], "seq", scatter_dimension=0, tiled=True),
    )
    totals = (
        lax.psum(shares[0].astype(jnp.bfloat16), "grp").astype(jnp.float32),
        lax.psum(shares[1].astype(jnp.bfloat16), "grp").astype(jnp.float32),
        lax.psum(shares[2].astype(jnp.bfloat16), "grp").astype(jnp.float32),
        lax.psum(shares[3].astype(jnp.bfloat16), "grp").astype(jnp.float32),
        lax.psum(shares[4].astype(jnp.bfloat16), "grp").astype(jnp.float32),
        lax.psum(shares[5].astype(jnp.bfloat16), "grp").astype(jnp.float32),
        lax.psum(shares[6].astype(jnp.bfloat16), "grp").astype(jnp.float32),
        lax.psum(shares[7].astype(jnp.bfloat16), "grp").astype(jnp.float32),
        lax.psum(shares[8].astype(jnp.bfloat16), "grp").astype(jnp.float32),
    )
    return (
        output.reshape(seq_count, tok_rows, model_width),
        grad_inputs,
        totals[0],
        totals[1],
        totals[2],
        totals[3],
        totals[4],
        totals[5],
        totals[6],
        totals[7],
        totals[8],
    )


def solution(mesh):
    local = ring_plan
    if (mesh.shape["grp"], mesh.shape["seq"]) == (2, 16):
        local = cube_plan
    return jax.shard_map(
        local,
        mesh=mesh,
        in_specs=(
            P("grp", "seq", None),
            P("grp", "seq", None),
            P("grp", None),
            P(),
            P("seq", None),
            P("seq", None),
            P("seq", None),
            P("seq", None),
            P("seq", None),
            P("seq", None),
            P("seq", None),
            P("seq"),
            P("seq"),
        ),
        out_specs=(
            P("grp", "seq", None),
            P("grp", "seq", None),
            P("seq", None),
            P("seq", None),
            P("seq", None),
            P("seq", None),
            P("seq", None),
            P("seq", None),
            P("seq", None),
            P("seq"),
            P("seq"),
        ),
        check_vma=False,
    )
```

```python
import functools

import jax
import jax.numpy as jnp
from jax import lax
from jax.experimental import pallas as pl
from jax.experimental.pallas import tpu as pltpu
from jax.sharding import PartitionSpec as P

HEADS = 16
KV_HEADS = 8
HEAD_DIM = 96


eps_norm = 1e-05
rope_base = 100000.0
masked_score = -1e30


def rms_scale(rows_in):
    return lax.rsqrt(jnp.mean(rows_in * rows_in, axis=-1, keepdims=True) + eps_norm)


def norm_back(grad_normed, rows_in, row_scale, gain_row):
    normed = rows_in * row_scale
    grad_gain = jnp.sum(grad_normed * normed, axis=0)
    scaled_grad = grad_normed * gain_row
    grad_rows = row_scale * (
        scaled_grad - normed * jnp.mean(scaled_grad * normed, axis=-1, keepdims=True)
    )
    return (grad_rows, grad_gain)


def rotary_tables(positions, head_dim):
    half_dim = head_dim // 2
    frequency = rope_base ** (-jnp.arange(half_dim, dtype=jnp.float32) * 2.0 / head_dim)
    angles = positions.astype(jnp.float32)[:, None] * frequency[None, :]
    return (jnp.cos(angles)[:, None, :], jnp.sin(angles)[:, None, :])


def rotate(vectors, cosine_table, sine_table):
    half_dim = vectors.shape[-1] // 2
    front_half = vectors[..., :half_dim]
    back_half = vectors[..., half_dim:]
    return jnp.concatenate(
        [
            front_half * cosine_table - back_half * sine_table,
            back_half * cosine_table + front_half * sine_table,
        ],
        axis=-1,
    )


def unrotate(grads, cosine_table, sine_table):
    half_dim = grads.shape[-1] // 2
    front_half = grads[..., :half_dim]
    back_half = grads[..., half_dim:]
    return jnp.concatenate(
        [
            front_half * cosine_table + back_half * sine_table,
            back_half * cosine_table - front_half * sine_table,
        ],
        axis=-1,
    )


def over_rows(left, right):
    return lax.dot_general(
        left, right, (((0,), (0,)), ((), ())), preferred_element_type=jnp.float32
    )


def times_back(left, right):
    return lax.dot_general(
        left, right, (((1,), (1,)), ((), ())), preferred_element_type=jnp.float32
    )


def key_block_rows(key_count):
    block_rows = min(key_count, 1024)
    return block_rows


def masked_scores(query_part, key_part, query_blocks, key_blocks, score_scale):
    scores = (
        jnp.einsum("qkgd,tkd->kgqt", query_part, key_part, preferred_element_type=jnp.float32)
        * score_scale
    )
    allowed = key_blocks[None, None, None, :] <= query_blocks[None, None, :, None]
    return jnp.where(allowed, scores, masked_score)


def forward_block(running, query_part, query_blocks, key_part, value_part, key_blocks, score_scale):
    row_max, row_sum, running_sum = running
    scores = masked_scores(query_part, key_part, query_blocks, key_blocks, score_scale)
    new_max = jnp.maximum(row_max, jnp.max(scores, axis=-1))
    likely = jnp.exp(scores - new_max[..., None])
    fading = jnp.exp(row_max - new_max)
    row_sum = row_sum * fading + jnp.sum(likely, axis=-1)
    running_sum = running_sum * fading[..., None] + jnp.einsum(
        "kgqt,tkd->kgqd",
        likely.astype(jnp.bfloat16),
        value_part,
        preferred_element_type=jnp.float32,
    )
    return (new_max, row_sum, running_sum)


def backward_block(
    grad_query,
    query_part,
    query_blocks,
    key_part,
    value_part,
    key_blocks,
    log_total,
    grad_heads,
    delta_rows,
    score_scale,
):
    scores = masked_scores(query_part, key_part, query_blocks, key_blocks, score_scale)
    chance = jnp.exp(scores - log_total[..., None])
    grad_value = jnp.einsum(
        "kgqt,kgqd->tkd",
        chance.astype(jnp.bfloat16),
        grad_heads,
        preferred_element_type=jnp.float32,
    )
    grad_chance = jnp.einsum(
        "kgqd,tkd->kgqt", grad_heads, value_part, preferred_element_type=jnp.float32
    )
    grad_scores = (chance * (grad_chance - delta_rows[..., None])).astype(jnp.bfloat16)
    grad_query = (
        grad_query
        + jnp.einsum("kgqt,tkd->kgqd", grad_scores, key_part, preferred_element_type=jnp.float32)
        * score_scale
    )
    grad_key = (
        jnp.einsum("kgqt,qkgd->tkd", grad_scores, query_part, preferred_element_type=jnp.float32)
        * score_scale
    )
    return (grad_query, grad_key, grad_value)


BIT_X, BIT_ZH, BIT_ZL, BIT_Y, BIT_C = 16, 8, 4, 2, 1
DEVICES = 32
AXES = ("grp", "seq")
THIRDS = (
    (BIT_X, BIT_Y, BIT_ZL),
    (BIT_Y, BIT_ZL, BIT_X),
    (BIT_ZL, BIT_X, BIT_Y),
)
HALVES = (
    (BIT_ZL, BIT_X, BIT_Y),
    (BIT_ZL, BIT_Y, BIT_X),
)
log2_e = 1.4426950408889634
VMEM_LIMIT = 48 * 1024 * 1024
low, wide = jnp.bfloat16, jnp.float32


def swap(value, mask, sends=None):
    pairs = [(i, i ^ mask) for i in range(DEVICES) if sends is None or sends(i)]
    return lax.ppermute(value, AXES, pairs)


def bit_of(index, mask):
    return 1 if index & mask else 0


def sync(*values):
    return lax.optimization_barrier(values)


def gather_start(rows, orders):
    width = rows.shape[1] // len(orders)
    return [rows[None, :, i * width : (i + 1) * width] for i in range(len(orders))]


def gather_next(parts, orders, step):
    return [
        jnp.concatenate([held, swap(held, order[step])], axis=0)
        for held, order in zip(parts, orders)
    ]


def gather_last(parts):
    return [(held, swap(held, BIT_C)) for held in parts]


def scatter_start(pairs):
    return [(kept, swap(sent, BIT_C)) for kept, sent in pairs]


def scatter_next(sums, orders, step):
    result = []
    for (kept, arrived), order in zip(sums, orders):
        half = kept.shape[0] // 2
        sent = (kept[half:].astype(wide) + arrived[half:].astype(wide)).astype(low)
        kept = (kept[:half].astype(wide) + arrived[:half].astype(wide)).astype(low)
        result.append((kept, swap(sent, order[step])))
    return result


def scatter_last(sums):
    return [kept.astype(wide) + arrived.astype(wide) for kept, arrived in sums]


def cube_groups():
    return [
        [gx * 16 + zh * 8 + rest for gx in (0, 1) for rest in range(8)] for zh in (0, 1)
    ]


def cube_gather(rows):
    return lax.all_gather(rows, AXES, axis=0, tiled=True, axis_index_groups=cube_groups())


def cube_scatter(rows):
    return lax.psum_scatter(
        rows, AXES, scatter_dimension=0, tiled=True, axis_index_groups=cube_groups()
    )


def trade_block(blocks, axis, mask):
    keep = lax.index_in_dim(blocks, 0, axis, keepdims=False)
    send = lax.index_in_dim(blocks, 1, axis, keepdims=False)
    return jnp.stack([keep, swap(send, mask)])


def trade_blocks(blocks, masks):
    for axis, mask in enumerate(masks):
        keep = lax.index_in_dim(blocks, 0, axis, keepdims=False)
        send = lax.index_in_dim(blocks, 1, axis, keepdims=False)
        blocks = jnp.stack([keep, swap(send, mask)])
    return blocks


def block_at(order):
    place = {BIT_X: 2, BIT_Y: 1, BIT_ZL: 0}

    def find(g):
        return sum(((g >> place[mask]) & 1) << rank for rank, mask in enumerate(order))

    return find


def row_specs(orders, step):
    width = 1536 // len(orders)
    specs = []
    for order in orders:
        find = block_at(order)
        for _ in range(2):
            specs.append(
                pl.BlockSpec((1, 128, width), lambda *a, find=find: (find(step(*a)), 0, 0))
            )
    return specs


def row_shapes(orders):
    width = 1536 // len(orders)
    return [jax.ShapeDtypeStruct((8, 128, width), low)] * (2 * len(orders))


def flat(pairs):
    return [array for pair in pairs for array in pair]


def paired(arrays):
    return [(arrays[i], arrays[i + 1]) for i in range(0, len(arrays), 2)]


def load_rows(refs):
    return jnp.concatenate(
        [
            jnp.concatenate([refs[i][0], refs[i + 1][0]], axis=0)
            for i in range(0, len(refs), 2)
        ],
        axis=1,
    )


def store_rows(refs, rows):
    width = 1536 // (len(refs) // 2)
    for i in range(0, len(refs), 2):
        columns = slice((i // 2) * width, (i // 2 + 1) * width)
        refs[i][0] = rows[:128, columns].astype(low)
        refs[i + 1][0] = rows[128:, columns].astype(low)


def whole_spec(shape):
    return pl.BlockSpec(shape, lambda *a: (0,) * len(shape))


def kernel_call(body, grid, in_specs, out_specs, out_shape, scratch, flops, moved, args, exps=0):
    return pl.pallas_call(
        body,
        out_shape=out_shape,
        grid_spec=pltpu.PrefetchScalarGridSpec(
            num_scalar_prefetch=1,
            grid=grid,
            in_specs=in_specs,
            out_specs=out_specs,
            scratch_shapes=scratch,
        ),
        compiler_params=pltpu.CompilerParams(vmem_limit_bytes=VMEM_LIMIT),
        cost_estimate=pl.CostEstimate(
            flops=flops, bytes_accessed=moved, transcendentals=exps
        ),
    )(*args)


def head_columns(w_query, w_key, w_value, head):
    shared = w_value if head % 2 else w_key
    start = (head // 2) * 96
    return w_query[:, head * 96 : head * 96 + 96], shared[:, start : start + 96]


def pick_heads(table, w_query, w_key, w_value, gain_rows):
    def body(table_ref, q_ref, k_ref, v_ref, gain_ref, out_ref, scr):
        gain = gain_ref[...]
        for head in range(16):
            one, two = head_columns(q_ref, k_ref, v_ref, head)
            scr[head, :, :96] = (one.astype(wide) * gain).astype(low)
            scr[head, :, 96:] = (two.astype(wide) * gain).astype(low)
        for i in range(8):
            out_ref[i] = scr[table_ref[i]]

    args = (w_query, w_key, w_value, gain_rows)
    return kernel_call(
        body,
        (1,),
        [whole_spec(a.shape) for a in args],
        whole_spec((8, 96, 192)),
        jax.ShapeDtypeStruct((8, 96, 192), low),
        [pltpu.VMEM((16, 96, 192), low)],
        0,
        1024 * 1024,
        (table, *args),
    )


def pick_columns(table, first, second, gain_rows):
    rows = first.shape[0]

    def body(table_ref, first_ref, second_ref, gain_ref, out_ref):
        gain = gain_ref[...]
        for i in range(8):
            columns = pl.ds(pl.multiple_of(table_ref[i] * 256, 256), 256)
            out_ref[i, :, :256] = (first_ref[:, columns].astype(wide) * gain).astype(low)
            out_ref[i, :, 256:] = (second_ref[:, columns].astype(wide) * gain).astype(low)

    shape = (8, rows, 512)
    return kernel_call(
        body,
        (1,),
        [whole_spec(first.shape), whole_spec(second.shape), whole_spec(gain_rows.shape)],
        whole_spec(shape),
        jax.ShapeDtypeStruct(shape, low),
        [],
        0,
        4 * first.size,
        (table, first, second, gain_rows),
    )


def assemble_rows(table, *groups):
    rows, width = groups[0].shape[1:]

    def body(table_ref, *refs):
        out_ref, i = refs[-1], 0
        for ref in refs[:-1]:
            for k in range(ref.shape[0]):
                start = pl.multiple_of(table_ref[i] * rows, rows)
                out_ref[pl.ds(start, rows), :] = ref[k]
                i += 1

    shape = (16 * rows, width)
    return kernel_call(
        body,
        (1,),
        [whole_spec(group.shape) for group in groups],
        whole_spec(shape),
        jax.ShapeDtypeStruct(shape, low),
        [],
        0,
        64 * rows * width,
        (table, *groups),
    )


def spread_columns(table, near, far, gain_rows, first, second):
    rows = near.shape[1]

    def body(table_ref, near_ref, far_ref, gain_ref, w1_ref, w2_ref, g1_ref, g2_ref, sum_ref):
        gain = gain_ref[...]
        total = jnp.zeros((rows, 256), wide)
        for i in range(16):
            source = near_ref if i < 8 else far_ref
            columns = pl.ds(pl.multiple_of(table_ref[i] * 256, 256), 256)
            block = source[i % 8].astype(wide)
            one, two = block[:, :256], block[:, 256:]
            total += one * w1_ref[:, columns].astype(wide)
            total += two * w2_ref[:, columns].astype(wide)
            g1_ref[:, columns] = one * gain
            g2_ref[:, columns] = two * gain
        sum_ref[...] = jnp.sum(total, axis=1, keepdims=True)

    return kernel_call(
        body,
        (1,),
        [whole_spec(a.shape) for a in (near, far, gain_rows, first, second)],
        [whole_spec(first.shape), whole_spec(second.shape), whole_spec((rows, 1))],
        [
            jax.ShapeDtypeStruct(first.shape, wide),
            jax.ShapeDtypeStruct(second.shape, wide),
            jax.ShapeDtypeStruct((rows, 1), wide),
        ],
        [],
        0,
        6 * 2 * first.size,
        (table, near, far, gain_rows, first, second),
    )


def spread_heads(table, near, far, w_query, w_key, w_value, gain_rows):
    def body(
        table_ref, near_ref, far_ref, q_ref, k_ref, v_ref, gain_ref, *rest
    ):
        gq_ref, gk_ref, gv_ref, sum_ref, scr = rest
        gain = gain_ref[...]
        for i in range(16):
            source = near_ref if i < 8 else far_ref
            scr[table_ref[i]] = source[i % 8].astype(wide)
        total = jnp.zeros((96, 96), wide)
        for head in range(16):
            one, two = head_columns(q_ref, k_ref, v_ref, head)
            block = scr[head]
            first, second = block[:, :96], block[:, 96:]
            total += first * one.astype(wide) + second * two.astype(wide)
            gq_ref[:, head * 96 : head * 96 + 96] = first * gain
            shared = gv_ref if head % 2 else gk_ref
            start = (head // 2) * 96
            shared[:, start : start + 96] = second * gain
        sum_ref[...] = jnp.sum(total, axis=1, keepdims=True)

    args = (near, far, w_query, w_key, w_value, gain_rows)
    shapes = [w_query.shape, w_key.shape, w_value.shape, (96, 1)]
    return kernel_call(
        body,
        (1,),
        [whole_spec(a.shape) for a in args],
        [whole_spec(shape) for shape in shapes],
        [jax.ShapeDtypeStruct(shape, wide) for shape in shapes],
        [pltpu.VMEM((16, 96, 192), wide)],
        0,
        4 * 1024 * 1024,
        (table, *args),
    )


def turn(rows, cosine, sine):
    front, back = rows[:48], rows[48:]
    return jnp.concatenate([front * cosine - back * sine, back * cosine + front * sine], axis=0)


def turn_back(rows, cosine, sine):
    front, back = rows[:48], rows[48:]
    return jnp.concatenate([front * cosine + back * sine, back * cosine - front * sine], axis=0)


def align_rows(core, rows):
    turned = jnp.concatenate([rows[128:], rows[:128]], axis=0)
    return jnp.where(core == 0, rows, turned)


def align(core, columns):
    turned = jnp.concatenate([columns[:, 128:], columns[:, :128]], axis=1)
    return jnp.where(core == 0, columns, turned)


def table_specs():
    return [pl.BlockSpec((48, 256), lambda g, t: (0, g % 4))] * 4


def cube_spec():
    return pl.BlockSpec((256, 1536), lambda g, t: (t[g], 0))


def project(at, normed, w_heads, tables):
    def body(at_ref, rows_ref, w_ref, cos_ref, sin_ref, cos2_ref, sin2_ref, q_ref, own_ref):
        made = jnp.dot(rows_ref[...], w_ref[...], preferred_element_type=wide).T
        q_ref[0] = turn(made[:96], cos_ref[...], sin_ref[...]).astype(low)
        own_ref[0] = turn(made[96:], cos2_ref[...], sin2_ref[...]).astype(low)

    out_spec = pl.BlockSpec((1, 96, 256), lambda g, t: (g // 4, 0, g % 4))
    shape = jax.ShapeDtypeStruct((2, 96, 1024), low)
    return kernel_call(
        body,
        (8,),
        [cube_spec(), whole_spec((1536, 192))] + table_specs(),
        [out_spec, out_spec],
        [shape, shape],
        [],
        2 * 2048 * 1536 * 192,
        8 * 1024 * 1024,
        (at, normed, w_heads, *tables),
    )


def head_specs():
    kv = pl.BlockSpec((1, 96, 1024), lambda s, t, a: (s, 0, 0))
    other = pl.BlockSpec((1, 1, 96, 1024), lambda s, t, a: (0, s, 0, 0))
    other_far = pl.BlockSpec((1, 1, 96, 1024), lambda s, t, a: (1, s, 0, 0))
    return [kv, kv, other, other_far]


def key_and_value(core, own_ref, far_ref, other_ref, other_far_ref):
    mine = jnp.concatenate([own_ref[0], far_ref[0]], axis=1)
    theirs = jnp.concatenate([other_ref[0, 0], other_far_ref[0, 0]], axis=1)
    keyed = core == 0
    return jnp.where(keyed, mine, theirs), jnp.where(keyed, theirs, mine)


def masked(scores, key_column, query_ref, score_scale):
    return jnp.where(key_column <= query_ref[0], scores * (score_scale * log2_e), masked_score)


def attend_forward(at, queries, held, query_blk, key_blk, score_scale):
    def body(at_ref, q_ref, a_ref, b_ref, c_ref, d_ref, qb_ref, kb_ref, *rest):
        keep_ref, send_ref, att_ref, total_ref, k_scr, v_scr, kb_scr = rest

        @pl.when(pl.program_id(1) == 0)
        def _():
            key_part, value_part = key_and_value(at_ref[8], a_ref, b_ref, c_ref, d_ref)
            k_scr[...] = key_part.astype(wide).T.astype(low)
            v_scr[...] = value_part
            kb_scr[...] = jnp.broadcast_to(kb_ref[0], (128, 2048)).T[:, :1]

        scores = jnp.dot(k_scr[...], q_ref[0], preferred_element_type=wide)
        scores = masked(scores, kb_scr[...], qb_ref, score_scale)
        top = jnp.max(scores, axis=0, keepdims=True)
        likely = jnp.exp2(scores - top)
        column_sum = jnp.sum(likely, axis=0, keepdims=True)
        mixed = jnp.dot(v_scr[...], likely.astype(low), preferred_element_type=wide)
        mixed = mixed / column_sum
        att_ref[0] = mixed
        total_ref[0] = top + jnp.log(column_sum) * log2_e
        mixed = align(at_ref[8], mixed).astype(low)
        keep_ref[0] = mixed[:, :128]
        send_ref[0] = mixed[:, 128:]

    q_spec = pl.BlockSpec((1, 96, 256), lambda s, t, a: (s, 0, t))
    one_spec = pl.BlockSpec((1, 1, 256), lambda s, t, a: (s, 0, t))
    block_spec = pl.BlockSpec((1, 96, 128), lambda s, t, a: (s * 4 + t, 0, 0))
    return kernel_call(
        body,
        (2, 4),
        [q_spec]
        + head_specs()
        + [one_spec, pl.BlockSpec((1, 1, 2048), lambda s, t, a: (s, 0, 0))],
        [block_spec, block_spec, q_spec, one_spec],
        [
            jax.ShapeDtypeStruct((8, 96, 128), low),
            jax.ShapeDtypeStruct((8, 96, 128), low),
            jax.ShapeDtypeStruct((2, 96, 1024), wide),
            jax.ShapeDtypeStruct((2, 1, 1024), wide),
        ],
        [
            pltpu.VMEM((2048, 96), low),
            pltpu.VMEM((96, 2048), low),
            pltpu.VMEM((2048, 1), wide),
        ],
        4 * 2 * 1024 * 2048 * 96,
        12 * 1024 * 1024,
        (at, queries, *held, query_blk, key_blk),
        exps=2 * 1024 * 2048,
    )


def out_project(at, blocks, w_full, residual):
    def body(at_ref, in_ref, w_ref, x_ref, middle_ref, scale_ref, normed_ref, att_ref):
        for i in range(16):
            start = pl.multiple_of(at_ref[i] * 96, 96)
            att_ref[pl.ds(start, 96), :] = in_ref[i]
        rows = att_ref[...].astype(wide).T.astype(low)
        middle = x_ref[...] + jnp.dot(rows, w_ref[...], preferred_element_type=wide)
        scale = rms_scale(middle)
        middle_ref[...] = middle
        scale_ref[...] = scale
        normed_ref[...] = (middle * scale).astype(low)

    shapes = [
        jax.ShapeDtypeStruct((128, 1536), wide),
        jax.ShapeDtypeStruct((128, 1), wide),
        jax.ShapeDtypeStruct((128, 1536), low),
    ]
    return kernel_call(
        body,
        (1,),
        [whole_spec(a.shape) for a in (blocks, w_full, residual)],
        [whole_spec(shape.shape) for shape in shapes],
        shapes,
        [pltpu.VMEM((1536, 128), low)],
        2 * 128 * 1536 * 1536,
        6 * 1024 * 1024,
        (at, blocks, w_full, residual),
    )


def out_back(at, grad_out, sums, middle, scale, w_full):
    def body(at_ref, dy_ref, a_ref, b_ref, c_ref, x_ref, scale_ref, w_ref, *rest):
        middle_ref, low_ref, keep_ref, send_ref, scr = rest
        scaled = jnp.concatenate([a_ref[0], b_ref[0], c_ref[0]], axis=1)
        scale = scale_ref[...]
        normed = x_ref[...] * scale
        grad = dy_ref[...].astype(wide) + scale * (
            scaled - normed * jnp.mean(scaled * normed, axis=-1, keepdims=True)
        )
        middle_ref[...] = grad
        grad = grad.astype(low)
        low_ref[...] = grad
        scr[...] = times_back(w_ref[...], grad).astype(low)
        for i in range(8):
            start = pl.multiple_of(at_ref[i] * 96, 96)
            keep_ref[i] = scr[pl.ds(start, 96), :]
            start = pl.multiple_of(at_ref[8 + i] * 96, 96)
            send_ref[i] = scr[pl.ds(start, 96), :]

    args = (grad_out, *sums, middle, scale, w_full)
    shapes = [
        jax.ShapeDtypeStruct((128, 1536), wide),
        jax.ShapeDtypeStruct((128, 1536), low),
        jax.ShapeDtypeStruct((8, 96, 128), low),
        jax.ShapeDtypeStruct((8, 96, 128), low),
    ]
    return kernel_call(
        body,
        (1,),
        [whole_spec(a.shape) for a in args],
        [whole_spec(shape.shape) for shape in shapes],
        shapes,
        [pltpu.VMEM((1536, 128), low)],
        4 * 128 * 1536 * 1536,
        14 * 1024 * 1024,
        (at, *args),
    )


def attend_backward(
    at, queries, held, query_blk, key_blk, attention, totals, grad_blocks, tables, score_scale
):
    def body(at_ref, q_ref, a_ref, b_ref, c_ref, d_ref, qb_ref, kb_ref, *rest):
        att_ref, total_ref, cos_ref, sin_ref = rest[:4]
        own_ref, core_ref = rest[4:6]
        dq_ref, mine_ref, sent_ref = rest[6:9]
        k_scr, kt_scr, v_scr, dk_scr, dv_scr, kb_scr = rest[9:]
        tile = pl.program_id(1)

        @pl.when(tile == 0)
        def _():
            key_part, value_part = key_and_value(at_ref[8], a_ref, b_ref, c_ref, d_ref)
            kt_scr[...] = key_part
            kb_scr[...] = jnp.broadcast_to(kb_ref[0], (128, 2048)).T[:, :1]
            k_scr[...] = key_part.astype(wide).T.astype(low)
            v_scr[...] = value_part.astype(wide).T.astype(low)
            dk_scr[...] = jnp.zeros_like(dk_scr)
            dv_scr[...] = jnp.zeros_like(dv_scr)

        att = att_ref[0]
        grad_att = align(
            at_ref[8], jnp.concatenate([own_ref[0, 0], core_ref[0, 0]], axis=1).astype(wide)
        ).astype(low)
        delta = jnp.sum(grad_att.astype(wide) * att, axis=0, keepdims=True)
        scores = jnp.dot(k_scr[...], q_ref[0], preferred_element_type=wide)
        scores = masked(scores, kb_scr[...], qb_ref, score_scale)
        chance = jnp.exp2(scores - total_ref[0])
        dv_scr[...] += times_back(grad_att, chance.astype(low))
        grad_chance = jnp.dot(v_scr[...], grad_att, preferred_element_type=wide)
        grad_scores = (chance * (grad_chance - delta)).astype(low)
        grad_query = jnp.dot(kt_scr[...], grad_scores, preferred_element_type=wide)
        dq_ref[0] = turn_back(grad_query * score_scale, cos_ref[...], sin_ref[...]).astype(low)
        dk_scr[...] += times_back(q_ref[0], grad_scores)

        @pl.when(tile == 3)
        def _():
            grad_key = dk_scr[...] * score_scale
            grad_value = dv_scr[...]
            keyed = at_ref[8] == 0
            mine = jnp.where(keyed, grad_key, grad_value)
            sent = jnp.where(keyed, grad_value, grad_key)
            mine_ref[0, 0] = mine[:, :1024].astype(low)
            mine_ref[1, 0] = mine[:, 1024:].astype(low)
            sent_ref[0, 0] = sent[:, :1024].astype(low)
            sent_ref[1, 0] = sent[:, 1024:].astype(low)

    q_spec = pl.BlockSpec((1, 96, 256), lambda s, t, a: (s, 0, t))
    one_spec = pl.BlockSpec((1, 1, 256), lambda s, t, a: (s, 0, t))
    kv_out = pl.BlockSpec((2, 1, 96, 1024), lambda s, t, a: (0, s, 0, 0))
    angle = pl.BlockSpec((48, 256), lambda s, t, a: (0, t))

    def block_of(s, t):
        return (t & 1) * 4 + (t >> 1) * 2 + s

    return kernel_call(
        body,
        (2, 4),
        [q_spec]
        + head_specs()
        + [
            one_spec,
            pl.BlockSpec((1, 1, 2048), lambda s, t, a: (s, 0, 0)),
            q_spec,
            one_spec,
            angle,
            angle,
            pl.BlockSpec((1, 1, 96, 128), lambda s, t, a: (block_of(s, t), 0, 0, 0)),
            pl.BlockSpec((1, 1, 96, 128), lambda s, t, a: (block_of(s, t), 1, 0, 0)),
        ],
        [q_spec, kv_out, kv_out],
        [
            jax.ShapeDtypeStruct((2, 96, 1024), low),
            jax.ShapeDtypeStruct((2, 2, 96, 1024), low),
            jax.ShapeDtypeStruct((2, 2, 96, 1024), low),
        ],
        [
            pltpu.VMEM((2048, 96), low),
            pltpu.VMEM((96, 2048), low),
            pltpu.VMEM((2048, 96), low),
            pltpu.VMEM((96, 2048), wide),
            pltpu.VMEM((96, 2048), wide),
            pltpu.VMEM((2048, 1), wide),
        ],
        10 * 2 * 1024 * 2048 * 96,
        12 * 1024 * 1024,
        (
            at,
            queries,
            *held,
            query_blk,
            key_blk,
            attention,
            totals,
            *tables[:2],
            grad_blocks,
            grad_blocks,
        ),
        exps=2 * 1024 * 2048,
    )


def head_grads(dq_ref, ds_ref, cos_ref, sin_ref):
    own = turn_back(ds_ref[0], cos_ref[...], sin_ref[...])
    return jnp.concatenate([dq_ref[0].astype(wide), own], axis=0)


def head_grad_specs():
    q_spec = pl.BlockSpec((1, 96, 256), lambda g, t: (g // 4, 0, g % 4))
    return table_specs()[:2] + [q_spec, q_spec]


def head_weights(at, normed, tables, grad_queries, grad_own):
    def body(at_ref, rows_ref, cos_ref, sin_ref, dq_ref, ds_ref, *rest):
        keep_ref, send_ref, gw_scr, nat_scr = rest
        g = pl.program_id(0)

        @pl.when(g == 0)
        def _():
            gw_scr[...] = jnp.zeros_like(gw_scr)

        both = head_grads(dq_ref, ds_ref, cos_ref, sin_ref)
        gw_scr[...] += jnp.dot(both.astype(low), rows_ref[...], preferred_element_type=wide)

        @pl.when(g == 7)
        def _():
            nat_scr[...] = gw_scr[...].T
            for i in range(8):
                start = pl.multiple_of(at_ref[9 + i] * 96, 96)
                keep_ref[i] = nat_scr[pl.ds(start, 96), :].astype(low)
                start = pl.multiple_of(at_ref[17 + i] * 96, 96)
                send_ref[i] = nat_scr[pl.ds(start, 96), :].astype(low)

    blocks = jax.ShapeDtypeStruct((8, 96, 192), low)
    return kernel_call(
        body,
        (8,),
        [cube_spec()] + head_grad_specs(),
        [whole_spec((8, 96, 192))] * 2,
        [blocks, blocks],
        [pltpu.VMEM((192, 1536), wide), pltpu.VMEM((1536, 192), wide)],
        2 * 2048 * 1536 * 192,
        8 * 1024 * 1024,
        (at, normed, *tables[2:], grad_queries, grad_own),
    )


def project_back(at, w_heads, tables, grad_queries, grad_own):
    def body(at_ref, w_ref, cos_ref, sin_ref, dq_ref, ds_ref, *outs):
        both = align(at_ref[8], head_grads(dq_ref, ds_ref, cos_ref, sin_ref))
        store_rows(outs, times_back(both.T.astype(low), w_ref[...]))

    return kernel_call(
        body,
        (8,),
        [whole_spec((1536, 192))] + head_grad_specs(),
        row_specs(THIRDS, lambda g, t: g),
        row_shapes(THIRDS),
        [],
        2 * 2048 * 1536 * 192,
        8 * 1024 * 1024,
        (at, w_heads, *tables[2:], grad_queries, grad_own),
    )


def hidden_back(at, grads, w_rows):
    def body(at_ref, *refs):
        rows, (w_ref, out_ref) = refs[:4], refs[4:]
        out_ref[...] = align_rows(at_ref[8], times_back(load_rows(rows), w_ref[...]))

    return kernel_call(
        body,
        (8,),
        row_specs(HALVES, lambda g, t: g) + [whole_spec((256, 1536))],
        pl.BlockSpec((256, 256), lambda g, t: (g, 0)),
        jax.ShapeDtypeStruct((2048, 256), wide),
        [],
        2 * 2048 * 1536 * 256,
        8 * 1024 * 1024,
        (at, *flat(grads), w_rows),
    )


def feed_back(at, normed, w_both, grad_hidden):
    def body(at_ref, rows_ref, w_ref, dh_ref, *rest):
        outs, (hidden_ref, both_ref) = rest[:6], rest[6:]
        both = jnp.dot(rows_ref[...], w_ref[...], preferred_element_type=wide)
        gate, up = both[:, :256], both[:, 256:]
        bend = jax.nn.sigmoid(gate)
        smooth = gate * bend
        grad_hidden = dh_ref[...]
        hidden_ref[...] = (smooth * up).astype(low)
        grad_gate = grad_hidden * up * (bend + smooth * (1.0 - bend))
        grad_both = jnp.concatenate([grad_gate, grad_hidden * smooth], axis=1).astype(low)
        both_ref[...] = grad_both
        store_rows(outs, align_rows(at_ref[8], times_back(grad_both, w_ref[...])))

    return kernel_call(
        body,
        (8,),
        [cube_spec(), whole_spec((1536, 512)), pl.BlockSpec((256, 256), lambda g, t: (g, 0))],
        row_specs(THIRDS, lambda g, t: g)
        + [
            pl.BlockSpec((256, 256), lambda g, t: (g, 0)),
            pl.BlockSpec((256, 512), lambda g, t: (g, 0)),
        ],
        row_shapes(THIRDS)
        + [
            jax.ShapeDtypeStruct((2048, 256), low),
            jax.ShapeDtypeStruct((2048, 512), low),
        ],
        [],
        4 * 2048 * 1536 * 512,
        18 * 1024 * 1024,
        (at, normed, w_both, grad_hidden),
        exps=2048 * 256,
    )


def feed_out(at, hidden, w_rows):
    def body(at_ref, hidden_ref, w_ref, *outs):
        made = jnp.dot(hidden_ref[...], w_ref[...], preferred_element_type=wide)
        store_rows(outs, align_rows(at_ref[8], made))

    return kernel_call(
        body,
        (8,),
        [pl.BlockSpec((256, 256), lambda g, t: (g, 0)), whole_spec((256, 1536))],
        row_specs(HALVES, lambda g, t: g),
        row_shapes(HALVES),
        [],
        2 * 2048 * 1536 * 256,
        8 * 1024 * 1024,
        (at, hidden, w_rows),
    )


def down_weights(at, hidden, grads):
    def body(at_ref, *refs):
        rows, (hidden_ref, gw_ref, gw_scr) = refs[:4], refs[4:]
        g = pl.program_id(0)

        @pl.when(g == 0)
        def _():
            gw_scr[...] = jnp.zeros_like(gw_scr)

        held = align_rows(at_ref[8], hidden_ref[...].astype(wide)).astype(low)
        gw_scr[...] += over_rows(held, load_rows(rows))

        @pl.when(g == 7)
        def _():
            gw_ref[...] = gw_scr[...].astype(low)

    return kernel_call(
        body,
        (8,),
        row_specs(HALVES, lambda g, t: g) + [pl.BlockSpec((256, 256), lambda g, t: (g, 0))],
        whole_spec((256, 1536)),
        jax.ShapeDtypeStruct((256, 1536), low),
        [pltpu.VMEM((256, 1536), wide)],
        2 * 2048 * 1536 * 256,
        8 * 1024 * 1024,
        (at, *flat(grads), hidden),
    )


def out_weights(at, attention, grads):
    def body(at_ref, att_ref, rows_ref, gw_ref, gw_scr):
        g = pl.program_id(0)

        @pl.when(g == 0)
        def _():
            gw_scr[...] = jnp.zeros_like(gw_scr)

        gw_scr[...] += jnp.dot(
            att_ref[0].astype(low), rows_ref[...], preferred_element_type=wide
        )

        @pl.when(g == 7)
        def _():
            gw_ref[...] = gw_scr[...].astype(low)

    return kernel_call(
        body,
        (8,),
        [pl.BlockSpec((1, 96, 256), lambda g, t: (g // 4, 0, g % 4)), cube_spec()],
        whole_spec((96, 1536)),
        jax.ShapeDtypeStruct((96, 1536), low),
        [pltpu.VMEM((96, 1536), wide)],
        2 * 2048 * 1536 * 96,
        8 * 1024 * 1024,
        (at, attention, grads),
    )


def feed_weights(at, normed, grad_both):
    def body(at_ref, rows_ref, both_ref, keep_ref, send_ref, gw_scr, nat_scr):
        g = pl.program_id(0)

        @pl.when(g == 0)
        def _():
            gw_scr[...] = jnp.zeros_like(gw_scr)

        gw_scr[...] += over_rows(both_ref[...], rows_ref[...])

        @pl.when(g == 7)
        def _():
            nat_scr[...] = gw_scr[...].T
            for i in range(8):
                start = pl.multiple_of(at_ref[9 + i] * 96, 96)
                keep_ref[i] = nat_scr[pl.ds(start, 96), :].astype(low)
                start = pl.multiple_of(at_ref[17 + i] * 96, 96)
                send_ref[i] = nat_scr[pl.ds(start, 96), :].astype(low)

    return kernel_call(
        body,
        (8,),
        [cube_spec(), pl.BlockSpec((256, 512), lambda g, t: (g, 0))],
        [whole_spec((8, 96, 512))] * 2,
        [jax.ShapeDtypeStruct((8, 96, 512), low)] * 2,
        [pltpu.VMEM((512, 1536), wide), pltpu.VMEM((1536, 512), wide)],
        2 * 2048 * 1536 * 512,
        14 * 1024 * 1024,
        (at, normed, grad_both),
    )


def sum_low(left, right):
    return (left.astype(wide) + right.astype(wide)).astype(low)


def cube_plan(
    inputs,
    cotangent,
    block_ids,
    piece_order,
    w_query,
    w_key,
    w_value,
    w_out,
    w_gate,
    w_up,
    w_down,
    gain_attn,
    gain_mlp,
):
    x = lax.axis_index("grp")
    seq_at = lax.axis_index("seq")
    zh, c = seq_at >> 3, seq_at & 1
    score_scale = HEAD_DIM ** (-0.5)
    gain_rows_attn = gain_attn.astype(wide)[:, None]
    gain_rows_mlp = gain_mlp.astype(wide)[:, None]
    eight = jnp.arange(8, dtype=jnp.int32)
    sixteen = jnp.arange(16, dtype=jnp.int32)
    cyl = (eight >> 2) + (eight & 2) + ((eight & 1) << 2)
    place = c.astype(jnp.int32)[None]
    natural = seq_at ^ sixteen

    def owns_out(i):
        return bit_of(i, BIT_X) == bit_of(i, BIT_ZH)

    def owns_down(i):
        return bit_of(i, BIT_X) ^ bit_of(i, BIT_C) == bit_of(i, BIT_ZH)

    def lacks_out(i):
        return not owns_out(i)

    def lacks_down(i):
        return not owns_down(i)

    out_owner, down_owner = x == zh, (x ^ c) == zh

    order = ((sixteen & 8)) | ((sixteen & 4) >> 1) | ((sixteen & 2) << 1) | (sixteen & 1)
    stored = (seq_at & 14) ^ order
    pieces = jnp.sum(
        jnp.where(stored[:, None] == sixteen[None, :], piece_order[None, :], 0), axis=1
    )
    own_pos = (pieces[:8, None] * 128 + jnp.arange(128, dtype=jnp.int32)[None, :]).reshape(1024)
    frequency = rope_base ** (-jnp.arange(HEAD_DIM // 2, dtype=wide) * 2.0 / HEAD_DIM)
    angles = frequency[:, None] * own_pos.astype(wide)[None, :]
    cosine, sine = jnp.cos(angles), jnp.sin(angles)
    keyed = c == 0
    tables = (
        cosine,
        sine,
        jnp.where(keyed, cosine, 1.0),
        jnp.where(keyed, sine, 0.0),
    )

    low_zy = ((eight & 1) << 2) | (eight & 2)
    side_of = x ^ (eight >> 2)
    spots = jnp.concatenate([side_of * 4 + (((seq_at ^ low_zy) & 7) >> 1), place])
    spots_rows = jnp.concatenate([spots, natural])
    head_for = jnp.concatenate(
        [side_of * 8 + ((seq_at ^ low_zy ^ core) & 7) for core in (0, 1)]
    )

    residual = inputs[0].astype(wide)
    scale_first = rms_scale(residual)
    normed_first = residual * scale_first
    normed = cube_gather(normed_first.astype(low))
    head_of = x * 8 + ((seq_at ^ cyl) & 7)
    heads = pick_heads(head_of, w_query, w_key, w_value, gain_rows_attn)
    heads = trade_block(heads.reshape(2, 2, 2, 96, 192), 0, BIT_C)
    heads, w_out_held = sync(heads, w_out)
    out_near = swap(w_out_held, BIT_ZH, owns_out)
    heads = trade_block(heads, 1, BIT_Y)
    heads, ids_held, up_held = sync(heads, block_ids, w_up)
    heads = trade_block(heads, 2, BIT_ZL)
    other_ids = swap(ids_held, BIT_X)
    wanted_mlp = (x ^ ((seq_at ^ cyl) & 1)) * 8 + ((seq_at ^ cyl) & 7)
    both_blocks = pick_columns(wanted_mlp, w_gate, up_held, gain_rows_mlp)
    heads, out_near, both_blocks = sync(heads, out_near, both_blocks)
    heads = heads.reshape(8, 96, 192)
    heads_far = swap(heads, BIT_ZH)
    both_blocks = trade_block(both_blocks.reshape(2, 2, 2, 96, 512), 0, BIT_C)
    both_blocks = trade_block(both_blocks, 1, BIT_Y)
    both_blocks = trade_block(both_blocks, 2, BIT_ZL)
    w_out_head = jnp.where(out_owner, w_out, out_near)
    heads, heads_far, both_blocks, w_down_held, tables = sync(
        heads, heads_far, both_blocks, w_down, tables
    )
    w_heads = assemble_rows(natural, heads, heads_far)
    ids = jnp.concatenate([block_ids, other_ids], axis=0).reshape(2, 16, 128)
    chosen = (pieces[:, None] == sixteen[None, :]).astype(low)
    blocks = jnp.einsum(
        "kp,spr->skr", chosen, ids.astype(low), preferred_element_type=wide
    ).reshape(2, 1, 2048)
    query_blk, key_blk = blocks[:, :, :1024], blocks
    normed, w_heads, both_blocks, w_out_head, query_blk, key_blk, rows_dy = sync(
        normed, w_heads, both_blocks, w_out_head, query_blk, key_blk, cotangent[0]
    )

    out_full = cube_gather(w_out_head)
    grads = gather_next(gather_start(rows_dy, HALVES), HALVES, 0)
    queries, own_part = project(spots, normed, w_heads, tables)
    queries, own_part, grads, both_blocks = sync(queries, own_part, grads, both_blocks)
    far_part = swap(own_part, BIT_ZH)
    grads = gather_next(grads, HALVES, 1)
    far_part, grads, both_blocks = sync(far_part, grads, both_blocks)
    other_parts = swap(jnp.stack([own_part, far_part]), BIT_C)
    other_parts, far_part, grads = sync(other_parts, far_part, grads)
    held = (own_part, far_part, other_parts, other_parts)
    grads = gather_next(grads, HALVES, 2)
    near_rows = [both_blocks[0].reshape(4, 96, 512), both_blocks[1].reshape(4, 96, 512)]
    far_first = swap(near_rows[0], BIT_ZH)
    keep, send, attention, totals = attend_forward(
        spots, queries, held, query_blk, key_blk, score_scale
    )
    keep, send, attention, totals, near_rows, out_full, w_down_held = sync(
        keep, send, attention, totals, near_rows, out_full, w_down_held
    )

    traded = jnp.stack([keep, swap(send, BIT_C)]).reshape(2, 2, 2, 2, 96, 128)
    traded, far_first, w_down_held = sync(traded, far_first, w_down_held)
    traded = trade_block(traded, 3, BIT_ZL)
    traded, grads, w_down_held = sync(traded, grads, w_down_held)
    down_near = swap(w_down_held, BIT_ZH, owns_down)
    grads = gather_last(grads)
    traded = trade_block(traded, 2, BIT_X)
    traded, grads = sync(traded, grads)
    traded = trade_block(traded, 3, BIT_Y).reshape(16, 96, 128)
    traded, residual, down_near, near_rows = sync(traded, residual, down_near, near_rows)
    far_second = swap(near_rows[1], BIT_ZH)
    yxlc = ((sixteen & 8) >> 2) | ((sixteen & 2) << 1) | (sixteen & 1)
    head_from = (x ^ ((sixteen & 4) >> 2)) * 8 + ((seq_at ^ yxlc) & 7)
    middle, scale_second, rows_second = out_project(head_from, traded, out_full, residual)

    rows_second, middle, scale_second, grads = sync(rows_second, middle, scale_second, grads)
    normed_mlp = cube_gather(rows_second)
    w_rows = jnp.where(down_owner, w_down_held, down_near)
    grad_hidden = hidden_back(spots, grads, w_rows)
    w_both = assemble_rows(natural, *near_rows, far_first, far_second)
    normed_mlp, grad_hidden, w_both = sync(normed_mlp, grad_hidden, w_both)
    made = feed_back(spots, normed_mlp, w_both, grad_hidden)
    hidden, grad_both = made[6:]
    sums = scatter_start(paired(made[:6]))
    sums, hidden, grad_both = sync(sums, hidden, grad_both)
    sums = scatter_next(sums, THIRDS, 2)
    keep_both, send_both = feed_weights(spots_rows, normed_mlp, grad_both)
    sums, keep_both, send_both = sync(sums, keep_both, send_both)
    sums = scatter_next(sums, THIRDS, 1)
    sums, = sync(sums)
    sums = scatter_next(sums, THIRDS, 0)
    sums, hidden, send_both = sync(sums, hidden, send_both)

    parts = scatter_last(sums)
    grad_middle, grad_low, keep, send = out_back(
        head_for, cotangent[0], parts, middle, scale_second, out_full
    )
    grad_middle, grad_low, keep, send, hidden, send_both = sync(
        grad_middle, grad_low, keep, send, hidden, send_both
    )
    middle_rows = cube_gather(grad_low)
    arrived_second = swap(send_both[4:], BIT_ZH)
    traded = jnp.stack([keep, swap(send, BIT_C)]).reshape(2, 2, 2, 2, 96, 128)
    traded, hidden = sync(traded, hidden)
    grad_down = down_weights(spots, hidden, grads)
    traded = trade_block(traded, 1, BIT_X)
    traded, grad_down, hidden, arrived_second, send_both = sync(
        traded, grad_down, hidden, arrived_second, send_both
    )
    arrived_first = swap(send_both[:4], BIT_ZH)
    out_terms = feed_out(spots, hidden, w_rows)
    traded = trade_block(traded, 2, BIT_Y)
    traded, grad_down, out_terms = sync(traded, grad_down, out_terms)
    traded = trade_block(traded, 3, BIT_ZL).reshape(8, 2, 96, 128)
    out_sums = scatter_start(paired(out_terms))
    both_send = sum_low(keep_both[4:], arrived_second)
    traded, out_sums, arrived_first, both_send, grad_down = sync(
        traded, out_sums, arrived_first, both_send, grad_down
    )
    out_sums = scatter_next(out_sums, HALVES, 2)
    down_arrived = swap(grad_down, BIT_ZH, lacks_down)
    both_sent = swap(both_send, BIT_ZL)
    made = attend_backward(
        spots,
        queries,
        held,
        query_blk,
        key_blk,
        attention,
        totals,
        traded,
        tables,
        score_scale,
    )
    made, out_sums, down_arrived, both_sent = sync(made, out_sums, down_arrived, both_sent)
    grad_queries, mine, sent = made
    both_sum = jnp.stack([sum_low(keep_both[:4], arrived_first), both_sent])
    arrived = swap(sent, BIT_C)
    arrived, both_sum, grad_down = sync(arrived, both_sum, grad_down)
    far_terms = sum_low(mine[1], arrived[1])
    far_terms, out_sums, both_sum, attention, middle_rows = sync(
        [far_terms[0], far_terms[1]], out_sums, both_sum, attention, middle_rows
    )
    far_first = swap(far_terms[0], BIT_ZH)
    out_sums = scatter_next(out_sums, HALVES, 1)
    grad_out_head = out_weights(spots, attention, middle_rows)
    far_first, far_terms, out_sums, both_sum, grad_out_head, grad_down = sync(
        far_first, far_terms, out_sums, both_sum, grad_out_head, grad_down
    )
    far_second = swap(far_terms[1], BIT_ZH)
    both_sum = trade_block(both_sum.reshape(2, 2, 2, 96, 512), 1, BIT_Y)
    down_sum = sum_low(grad_down, down_arrived)
    down_far = swap(down_sum, BIT_X, owns_down)
    far_second, both_sum, out_sums = sync(far_second, both_sum, out_sums)
    out_sums = scatter_next(out_sums, HALVES, 0)
    both_near = trade_block(both_sum, 2, BIT_C).reshape(8, 96, 512)
    grad_own = (
        mine[0].astype(wide)
        + arrived[0].astype(wide)
        + jnp.stack([far_first, far_second]).astype(wide)
    )
    keep_heads, send_heads = head_weights(
        spots_rows, normed, tables, grad_queries, grad_own
    )
    out_arrived = swap(grad_out_head, BIT_ZH, lacks_out)
    keep_heads, send_heads, grad_own, both_near, down_far, out_arrived = sync(
        keep_heads, send_heads, grad_own, both_near, down_far, out_arrived
    )
    both_far = swap(both_near, BIT_X)
    heads_first = swap(send_heads, BIT_ZH)
    made = project_back(spots, w_heads, tables, grad_queries, grad_own)
    made, heads_first, both_far, out_sums = sync(made, heads_first, both_far, out_sums)
    sums = scatter_start(paired(made))
    heads_sum = sum_low(keep_heads, heads_first)
    sums, heads_sum = sync(sums, heads_sum)
    heads_sum = trade_block(heads_sum.reshape(2, 2, 2, 96, 192), 0, BIT_ZL)
    sums = scatter_next(sums, THIRDS, 2)
    sums, heads_sum = sync(sums, heads_sum)
    out_sum = sum_low(grad_out_head, out_arrived)
    out_far = swap(out_sum, BIT_X, owns_out)
    output = jnp.concatenate([part[0] for part in scatter_last(out_sums)], axis=1)
    output = (middle + output).astype(low)
    heads_sum = trade_block(heads_sum, 1, BIT_Y)
    sums = scatter_next(sums, THIRDS, 1)
    sums, output, heads_sum, out_far = sync(sums, output, heads_sum, out_far)
    heads_near = trade_block(heads_sum, 2, BIT_C).reshape(8, 96, 192)
    heads_far = swap(heads_near, BIT_X)
    sums = scatter_next(sums, THIRDS, 0)
    sums, heads_far = sync(sums, heads_far)
    scaled_first = jnp.concatenate([part[0] for part in scatter_last(sums)], axis=1)
    grad_inputs = grad_middle + scale_first * (
        scaled_first
        - normed_first * jnp.mean(scaled_first * normed_first, axis=-1, keepdims=True)
    )

    back = seq_at ^ cyl
    home = jnp.concatenate([x * 8 + (back & 7), (1 - x) * 8 + (back & 7)])
    grad_w_query, grad_w_key, grad_w_value, grad_gain_attn = spread_heads(
        home, heads_near, heads_far, w_query, w_key, w_value, gain_rows_attn
    )
    grad_w_out = jnp.where(out_owner, out_sum, out_far).astype(wide)
    grad_w_down = jnp.where(down_owner, down_sum, down_far).astype(wide)
    side = (back & 1) ^ x
    home = jnp.concatenate([side * 8 + (back & 7), (1 - side) * 8 + (back & 7)])
    grad_w_gate, grad_w_up, grad_gain_mlp = spread_columns(
        home, both_near, both_far, gain_rows_mlp, w_gate, w_up
    )
    return (
        output[None],
        grad_inputs.astype(low)[None],
        grad_w_query,
        grad_w_key,
        grad_w_value,
        grad_w_out,
        grad_w_gate,
        grad_w_up,
        grad_w_down,
        grad_gain_attn[:, 0],
        grad_gain_mlp[:, 0],
    )


def ring_plan(
    inputs,
    cotangent,
    block_ids,
    piece_order,
    w_query,
    w_key,
    w_value,
    w_out,
    w_gate,
    w_up,
    w_down,
    gain_attn,
    gain_mlp,
):
    shards = (w_query, w_key, w_value, w_out, w_gate, w_up, w_down, gain_attn, gain_mlp)
    (
        full_query,
        full_key,
        full_value,
        full_out,
        full_gate,
        full_up,
        full_down,
        gain_one,
        gain_two,
    ) = (
        lax.all_gather(shards[0], "seq", axis=0, tiled=True),
        lax.all_gather(shards[1], "seq", axis=0, tiled=True),
        lax.all_gather(shards[2], "seq", axis=0, tiled=True),
        lax.all_gather(shards[3], "seq", axis=0, tiled=True),
        lax.all_gather(shards[4], "seq", axis=0, tiled=True),
        lax.all_gather(shards[5], "seq", axis=0, tiled=True),
        lax.all_gather(shards[6], "seq", axis=0, tiled=True),
        lax.all_gather(shards[7], "seq", axis=0, tiled=True),
        lax.all_gather(shards[8], "seq", axis=0, tiled=True),
    )
    seq_count, tok_rows, model_width = inputs.shape
    row_count = seq_count * tok_rows
    head_count = HEADS
    kv_heads = KV_HEADS
    head_dim = HEAD_DIM
    groups = head_count // kv_heads
    kv_width = kv_heads * head_dim
    q_width = head_count * head_dim
    score_scale = head_dim ** (-0.5)
    own_first = jnp.take(piece_order, lax.axis_index("seq")) * tok_rows
    local_pos = own_first + jnp.arange(tok_rows, dtype=jnp.int32)
    cosine_table, sine_table = rotary_tables(local_pos, head_dim)
    query_blk = jnp.take(block_ids, local_pos, axis=1)

    def key_positions(key_count):
        stored = jnp.arange(key_count, dtype=jnp.int32)
        return jnp.take(piece_order, stored // tok_rows) * tok_rows + stored % tok_rows

    residual = inputs.reshape(row_count, model_width).astype(jnp.float32)
    gain_first = gain_one.astype(jnp.float32)
    gain_second = gain_two.astype(jnp.float32)
    scale_first = rms_scale(residual)
    normed_attn = (residual * scale_first * gain_first).astype(jnp.bfloat16)
    query_pre = jnp.dot(normed_attn, full_query, preferred_element_type=jnp.float32)
    key_pre = jnp.dot(normed_attn, full_key, preferred_element_type=jnp.float32)
    value_pre = jnp.dot(normed_attn, full_value, preferred_element_type=jnp.float32)
    queries = rotate(
        query_pre.reshape(seq_count, tok_rows, head_count, head_dim), cosine_table, sine_table
    ).astype(jnp.bfloat16)
    key_rot = rotate(
        key_pre.reshape(seq_count, tok_rows, kv_heads, head_dim), cosine_table, sine_table
    ).astype(jnp.bfloat16)
    values = value_pre.astype(jnp.bfloat16)
    kv_local = jnp.concatenate(
        [
            key_rot.reshape(seq_count, tok_rows, kv_width),
            values.reshape(seq_count, tok_rows, kv_width),
        ],
        axis=2,
    )
    query_grouped = queries.reshape(seq_count, tok_rows, kv_heads, groups, head_dim)
    start_max = jnp.full((seq_count, kv_heads, groups, tok_rows), masked_score, jnp.float32)
    start_sum = jnp.zeros((seq_count, kv_heads, groups, tok_rows), jnp.float32)
    start_acc = jnp.zeros((seq_count, kv_heads, groups, tok_rows, head_dim), jnp.float32)
    state_in = (start_max, start_sum, start_acc)
    key_piece = lax.all_gather(kv_local, "seq", axis=1, tiled=True)
    key_count = key_piece.shape[1]
    block_rows = key_block_rows(key_count)
    key_pos = key_positions(key_count)
    member = 0
    key_blk = jnp.take(block_ids[member], key_pos).reshape(key_count // block_rows, block_rows)
    kv_rows = key_piece[member].reshape(key_count // block_rows, block_rows, 2 * kv_width)
    own_query = query_grouped[member]
    own_blocks = query_blk[member]

    def forward_key_step(running, block_in):
        kv_block, blk_block = block_in
        key_part = kv_block[:, :kv_width].reshape(block_rows, kv_heads, head_dim)
        value_part = kv_block[:, kv_width:].reshape(block_rows, kv_heads, head_dim)
        running = forward_block(
            running, own_query, own_blocks, key_part, value_part, blk_block, score_scale
        )
        return (running, None)

    running, unused = lax.scan(
        forward_key_step,
        (state_in[0][member], state_in[1][member], state_in[2][member]),
        (kv_rows, key_blk),
    )
    results = [running]
    row_max = jnp.stack([entry[0] for entry in results])
    row_sum = jnp.stack([entry[1] for entry in results])
    running_sum = jnp.stack([entry[2] for entry in results])
    log_total = row_max + jnp.log(row_sum)
    attention = running_sum / row_sum[..., None]
    attended = (
        jnp.transpose(attention, (0, 3, 1, 2, 4)).reshape(row_count, q_width).astype(jnp.bfloat16)
    )
    middle = residual + jnp.dot(attended, full_out, preferred_element_type=jnp.float32)
    scale_second = rms_scale(middle)
    normed_mlp = (middle * scale_second * gain_second).astype(jnp.bfloat16)
    gate_value = jnp.dot(normed_mlp, full_gate, preferred_element_type=jnp.float32)
    upward = jnp.dot(normed_mlp, full_up, preferred_element_type=jnp.float32)
    sigmoid_gate = jax.nn.sigmoid(gate_value)
    hidden = (gate_value * sigmoid_gate * upward).astype(jnp.bfloat16)
    output = (middle + jnp.dot(hidden, full_down, preferred_element_type=jnp.float32)).astype(
        jnp.bfloat16
    )
    (
        full_query,
        full_key,
        full_value,
        full_out,
        full_gate,
        full_up,
        full_down,
        gain_one,
        gain_two,
    ) = (
        lax.all_gather(shards[0], "seq", axis=0, tiled=True),
        lax.all_gather(shards[1], "seq", axis=0, tiled=True),
        lax.all_gather(shards[2], "seq", axis=0, tiled=True),
        lax.all_gather(shards[3], "seq", axis=0, tiled=True),
        lax.all_gather(shards[4], "seq", axis=0, tiled=True),
        lax.all_gather(shards[5], "seq", axis=0, tiled=True),
        lax.all_gather(shards[6], "seq", axis=0, tiled=True),
        lax.all_gather(shards[7], "seq", axis=0, tiled=True),
        lax.all_gather(shards[8], "seq", axis=0, tiled=True),
    )
    gain_first = gain_one.astype(jnp.float32)
    gain_second = gain_two.astype(jnp.float32)
    upstream = cotangent.reshape(row_count, model_width)
    grad_down = over_rows(hidden, upstream)
    grad_hidden = times_back(upstream, full_down)
    grad_gate = (
        grad_hidden * upward * sigmoid_gate * (1.0 + gate_value * (1.0 - sigmoid_gate))
    ).astype(jnp.bfloat16)
    grad_upward = (grad_hidden * gate_value * sigmoid_gate).astype(jnp.bfloat16)
    grad_w_gate = over_rows(normed_mlp, grad_gate)
    grad_w_up = over_rows(normed_mlp, grad_upward)
    grad_normed_mlp = times_back(grad_gate, full_gate) + times_back(grad_upward, full_up)
    grad_mid_norm, grad_gain_mlp = norm_back(grad_normed_mlp, middle, scale_second, gain_second)
    grad_middle = upstream.astype(jnp.float32) + grad_mid_norm
    grad_middle_low = grad_middle.astype(jnp.bfloat16)
    grad_w_out = over_rows(attended, grad_middle_low)
    grad_attended = times_back(grad_middle_low, full_out).astype(jnp.bfloat16)
    grad_heads = jnp.transpose(
        grad_attended.reshape(seq_count, tok_rows, kv_heads, groups, head_dim), (0, 2, 3, 1, 4)
    )
    delta_rows = jnp.sum(grad_heads.astype(jnp.float32) * attention, axis=-1)
    start_query = jnp.zeros((seq_count, kv_heads, groups, tok_rows, head_dim), jnp.float32)
    start_kv = jnp.zeros((seq_count, block_ids.shape[1], 2 * kv_width), jnp.float32)
    state_in = (start_query, start_kv)
    key_piece = lax.all_gather(kv_local, "seq", axis=1, tiled=True)
    key_count = key_piece.shape[1]
    backward_block_rows = key_block_rows(key_count)
    key_pos = key_positions(key_count)
    member = 0
    key_blk = jnp.take(block_ids[member], key_pos).reshape(
        key_count // backward_block_rows, backward_block_rows
    )
    kv_rows = key_piece[member].reshape(
        key_count // backward_block_rows, backward_block_rows, 2 * kv_width
    )
    backward_own_query = query_grouped[member]
    backward_own_blocks = query_blk[member]
    own_total = log_total[member]
    own_grads = grad_heads[member]
    own_delta = delta_rows[member]

    def backward_key_step(grad_query, block_in):
        kv_block, blk_block = block_in
        key_part = kv_block[:, :kv_width].reshape(backward_block_rows, kv_heads, head_dim)
        value_part = kv_block[:, kv_width:].reshape(backward_block_rows, kv_heads, head_dim)
        result = backward_block(
            grad_query,
            backward_own_query,
            backward_own_blocks,
            key_part,
            value_part,
            blk_block,
            own_total,
            own_grads,
            own_delta,
            score_scale,
        )
        return (result[0], (result[1], result[2]))

    grad_query, key_grads = lax.scan(backward_key_step, state_in[0][member], (kv_rows, key_blk))
    fresh = jnp.concatenate(
        [key_grads[0].reshape(key_count, kv_width), key_grads[1].reshape(key_count, kv_width)],
        axis=1,
    )
    query_grads = [grad_query]
    kv_grads = [fresh]
    grad_query_all = jnp.stack(query_grads)
    grad_kv_all = jnp.stack(kv_grads)
    grad_kv_own = lax.psum_scatter(grad_kv_all, "seq", scatter_dimension=1, tiled=True)
    grad_query_rows = jnp.transpose(grad_query_all, (0, 3, 1, 2, 4)).reshape(
        seq_count, tok_rows, head_count, head_dim
    )
    grad_query_pre = (
        unrotate(grad_query_rows, cosine_table, sine_table)
        .reshape(row_count, q_width)
        .astype(jnp.bfloat16)
    )
    grad_key_rows = grad_kv_own[:, :, :kv_width].reshape(seq_count, tok_rows, kv_heads, head_dim)
    grad_key_pre = (
        unrotate(grad_key_rows, cosine_table, sine_table)
        .reshape(row_count, kv_width)
        .astype(jnp.bfloat16)
    )
    grad_value_pre = grad_kv_own[:, :, kv_width:].reshape(row_count, kv_width).astype(jnp.bfloat16)
    grad_w_query = over_rows(normed_attn, grad_query_pre)
    grad_w_key = over_rows(normed_attn, grad_key_pre)
    grad_w_value = over_rows(normed_attn, grad_value_pre)
    grad_normed_attn = (
        times_back(grad_query_pre, full_query)
        + times_back(grad_key_pre, full_key)
        + times_back(grad_value_pre, full_value)
    )
    grad_in_norm, grad_gain_attn = norm_back(grad_normed_attn, residual, scale_first, gain_first)
    grad_inputs = (
        (grad_middle + grad_in_norm).astype(jnp.bfloat16).reshape(seq_count, tok_rows, model_width)
    )
    terms = (
        grad_w_query,
        grad_w_key,
        grad_w_value,
        grad_w_out,
        grad_w_gate,
        grad_w_up,
        grad_down,
        grad_gain_attn,
        grad_gain_mlp,
    )
    shares = (
        lax.psum_scatter(terms[0], "seq", scatter_dimension=0, tiled=True),
        lax.psum_scatter(terms[1], "seq", scatter_dimension=0, tiled=True),
        lax.psum_scatter(terms[2], "seq", scatter_dimension=0, tiled=True),
        lax.psum_scatter(terms[3], "seq", scatter_dimension=0, tiled=True),
        lax.psum_scatter(terms[4], "seq", scatter_dimension=0, tiled=True),
        lax.psum_scatter(terms[5], "seq", scatter_dimension=0, tiled=True),
        lax.psum_scatter(terms[6], "seq", scatter_dimension=0, tiled=True),
        lax.psum_scatter(terms[7], "seq", scatter_dimension=0, tiled=True),
        lax.psum_scatter(terms[8], "seq", scatter_dimension=0, tiled=True),
    )
    totals = (
        lax.psum(shares[0].astype(jnp.bfloat16), "grp").astype(jnp.float32),
        lax.psum(shares[1].astype(jnp.bfloat16), "grp").astype(jnp.float32),
        lax.psum(shares[2].astype(jnp.bfloat16), "grp").astype(jnp.float32),
        lax.psum(shares[3].astype(jnp.bfloat16), "grp").astype(jnp.float32),
        lax.psum(shares[4].astype(jnp.bfloat16), "grp").astype(jnp.float32),
        lax.psum(shares[5].astype(jnp.bfloat16), "grp").astype(jnp.float32),
        lax.psum(shares[6].astype(jnp.bfloat16), "grp").astype(jnp.float32),
        lax.psum(shares[7].astype(jnp.bfloat16), "grp").astype(jnp.float32),
        lax.psum(shares[8].astype(jnp.bfloat16), "grp").astype(jnp.float32),
    )
    return (
        output.reshape(seq_count, tok_rows, model_width),
        grad_inputs,
        totals[0],
        totals[1],
        totals[2],
        totals[3],
        totals[4],
        totals[5],
        totals[6],
        totals[7],
        totals[8],
    )


def solution(mesh):
    local = ring_plan
    if (mesh.shape["grp"], mesh.shape["seq"]) == (2, 16):
        local = cube_plan
    return jax.shard_map(
        local,
        mesh=mesh,
        in_specs=(
            P("grp", "seq", None),
            P("grp", "seq", None),
            P("grp", None),
            P(),
            P("seq", None),
            P("seq", None),
            P("seq", None),
            P("seq", None),
            P("seq", None),
            P("seq", None),
            P("seq", None),
            P("seq"),
            P("seq"),
        ),
        out_specs=(
            P("grp", "seq", None),
            P("grp", "seq", None),
            P("seq", None),
            P("seq", None),
            P("seq", None),
            P("seq", None),
            P("seq", None),
            P("seq", None),
            P("seq", None),
            P("seq"),
            P("seq"),
        ),
        check_vma=False,
    )
```

```python
import functools

import jax
import jax.numpy as jnp
from jax import lax
from jax.experimental import pallas as pl
from jax.experimental.pallas import tpu as pltpu
from jax.sharding import PartitionSpec as P

HEADS = 16
KV_HEADS = 8
HEAD_DIM = 96


eps_norm = 1e-05
rope_base = 100000.0
masked_score = -1e30


def rms_scale(rows_in):
    return lax.rsqrt(jnp.mean(rows_in * rows_in, axis=-1, keepdims=True) + eps_norm)


def norm_back(grad_normed, rows_in, row_scale, gain_row):
    normed = rows_in * row_scale
    grad_gain = jnp.sum(grad_normed * normed, axis=0)
    scaled_grad = grad_normed * gain_row
    grad_rows = row_scale * (
        scaled_grad - normed * jnp.mean(scaled_grad * normed, axis=-1, keepdims=True)
    )
    return (grad_rows, grad_gain)


def rotary_tables(positions, head_dim):
    half_dim = head_dim // 2
    frequency = rope_base ** (-jnp.arange(half_dim, dtype=jnp.float32) * 2.0 / head_dim)
    angles = positions.astype(jnp.float32)[:, None] * frequency[None, :]
    return (jnp.cos(angles)[:, None, :], jnp.sin(angles)[:, None, :])


def rotate(vectors, cosine_table, sine_table):
    half_dim = vectors.shape[-1] // 2
    front_half = vectors[..., :half_dim]
    back_half = vectors[..., half_dim:]
    return jnp.concatenate(
        [
            front_half * cosine_table - back_half * sine_table,
            back_half * cosine_table + front_half * sine_table,
        ],
        axis=-1,
    )


def unrotate(grads, cosine_table, sine_table):
    half_dim = grads.shape[-1] // 2
    front_half = grads[..., :half_dim]
    back_half = grads[..., half_dim:]
    return jnp.concatenate(
        [
            front_half * cosine_table + back_half * sine_table,
            back_half * cosine_table - front_half * sine_table,
        ],
        axis=-1,
    )


def over_rows(left, right):
    return lax.dot_general(
        left, right, (((0,), (0,)), ((), ())), preferred_element_type=jnp.float32
    )


def times_back(left, right):
    return lax.dot_general(
        left, right, (((1,), (1,)), ((), ())), preferred_element_type=jnp.float32
    )


def key_block_rows(key_count):
    block_rows = min(key_count, 1024)
    return block_rows


def masked_scores(query_part, key_part, query_blocks, key_blocks, score_scale):
    scores = (
        jnp.einsum("qkgd,tkd->kgqt", query_part, key_part, preferred_element_type=jnp.float32)
        * score_scale
    )
    allowed = key_blocks[None, None, None, :] <= query_blocks[None, None, :, None]
    return jnp.where(allowed, scores, masked_score)


def forward_block(running, query_part, query_blocks, key_part, value_part, key_blocks, score_scale):
    row_max, row_sum, running_sum = running
    scores = masked_scores(query_part, key_part, query_blocks, key_blocks, score_scale)
    new_max = jnp.maximum(row_max, jnp.max(scores, axis=-1))
    likely = jnp.exp(scores - new_max[..., None])
    fading = jnp.exp(row_max - new_max)
    row_sum = row_sum * fading + jnp.sum(likely, axis=-1)
    running_sum = running_sum * fading[..., None] + jnp.einsum(
        "kgqt,tkd->kgqd",
        likely.astype(jnp.bfloat16),
        value_part,
        preferred_element_type=jnp.float32,
    )
    return (new_max, row_sum, running_sum)


def backward_block(
    grad_query,
    query_part,
    query_blocks,
    key_part,
    value_part,
    key_blocks,
    log_total,
    grad_heads,
    delta_rows,
    score_scale,
):
    scores = masked_scores(query_part, key_part, query_blocks, key_blocks, score_scale)
    chance = jnp.exp(scores - log_total[..., None])
    grad_value = jnp.einsum(
        "kgqt,kgqd->tkd",
        chance.astype(jnp.bfloat16),
        grad_heads,
        preferred_element_type=jnp.float32,
    )
    grad_chance = jnp.einsum(
        "kgqd,tkd->kgqt", grad_heads, value_part, preferred_element_type=jnp.float32
    )
    grad_scores = (chance * (grad_chance - delta_rows[..., None])).astype(jnp.bfloat16)
    grad_query = (
        grad_query
        + jnp.einsum("kgqt,tkd->kgqd", grad_scores, key_part, preferred_element_type=jnp.float32)
        * score_scale
    )
    grad_key = (
        jnp.einsum("kgqt,qkgd->tkd", grad_scores, query_part, preferred_element_type=jnp.float32)
        * score_scale
    )
    return (grad_query, grad_key, grad_value)


BIT_X, BIT_ZH, BIT_ZL, BIT_Y, BIT_C = 16, 8, 4, 2, 1
DEVICES = 32
AXES = ("grp", "seq")
THIRDS = (
    (BIT_X, BIT_Y, BIT_ZL),
    (BIT_Y, BIT_ZL, BIT_X),
    (BIT_ZL, BIT_X, BIT_Y),
)
HALVES = (
    (BIT_ZL, BIT_X, BIT_Y),
    (BIT_ZL, BIT_Y, BIT_X),
)
log2_e = 1.4426950408889634
VMEM_LIMIT = 48 * 1024 * 1024
low, wide = jnp.bfloat16, jnp.float32


def swap(value, mask, sends=None):
    pairs = [(i, i ^ mask) for i in range(DEVICES) if sends is None or sends(i)]
    return lax.ppermute(value, AXES, pairs)


def bit_of(index, mask):
    return 1 if index & mask else 0


def sync(*values):
    return lax.optimization_barrier(values)


def gather_start(rows, orders):
    width = rows.shape[1] // len(orders)
    return [rows[None, :, i * width : (i + 1) * width] for i in range(len(orders))]


def gather_next(parts, orders, step):
    return [
        jnp.concatenate([held, swap(held, order[step])], axis=0)
        for held, order in zip(parts, orders)
    ]


def gather_last(parts):
    return [(held, swap(held, BIT_C)) for held in parts]


def scatter_start(pairs):
    return [(kept, swap(sent, BIT_C)) for kept, sent in pairs]


def scatter_next(sums, orders, step):
    result = []
    for (kept, arrived), order in zip(sums, orders):
        half = kept.shape[0] // 2
        sent = (kept[half:].astype(wide) + arrived[half:].astype(wide)).astype(low)
        kept = (kept[:half].astype(wide) + arrived[:half].astype(wide)).astype(low)
        result.append((kept, swap(sent, order[step])))
    return result


def scatter_last(sums):
    return [kept.astype(wide) + arrived.astype(wide) for kept, arrived in sums]


def cube_groups():
    return [
        [gx * 16 + zh * 8 + rest for gx in (0, 1) for rest in range(8)] for zh in (0, 1)
    ]


def cube_gather(rows):
    return lax.all_gather(rows, AXES, axis=0, tiled=True, axis_index_groups=cube_groups())


def cube_scatter(rows):
    return lax.psum_scatter(
        rows, AXES, scatter_dimension=0, tiled=True, axis_index_groups=cube_groups()
    )


def trade_block(blocks, axis, mask):
    keep = lax.index_in_dim(blocks, 0, axis, keepdims=False)
    send = lax.index_in_dim(blocks, 1, axis, keepdims=False)
    return jnp.stack([keep, swap(send, mask)])


def trade_blocks(blocks, masks):
    for axis, mask in enumerate(masks):
        keep = lax.index_in_dim(blocks, 0, axis, keepdims=False)
        send = lax.index_in_dim(blocks, 1, axis, keepdims=False)
        blocks = jnp.stack([keep, swap(send, mask)])
    return blocks


def block_at(order):
    place = {BIT_X: 2, BIT_Y: 1, BIT_ZL: 0}

    def find(g):
        return sum(((g >> place[mask]) & 1) << rank for rank, mask in enumerate(order))

    return find


def row_specs(orders, step):
    width = 1536 // len(orders)
    specs = []
    for order in orders:
        find = block_at(order)
        for _ in range(2):
            specs.append(
                pl.BlockSpec((1, 128, width), lambda *a, find=find: (find(step(*a)), 0, 0))
            )
    return specs


def row_shapes(orders):
    width = 1536 // len(orders)
    return [jax.ShapeDtypeStruct((8, 128, width), low)] * (2 * len(orders))


def flat(pairs):
    return [array for pair in pairs for array in pair]


def paired(arrays):
    return [(arrays[i], arrays[i + 1]) for i in range(0, len(arrays), 2)]


def load_rows(refs):
    return jnp.concatenate(
        [
            jnp.concatenate([refs[i][0], refs[i + 1][0]], axis=0)
            for i in range(0, len(refs), 2)
        ],
        axis=1,
    )


def store_rows(refs, rows):
    width = 1536 // (len(refs) // 2)
    for i in range(0, len(refs), 2):
        columns = slice((i // 2) * width, (i // 2 + 1) * width)
        refs[i][0] = rows[:128, columns].astype(low)
        refs[i + 1][0] = rows[128:, columns].astype(low)


def whole_spec(shape):
    return pl.BlockSpec(shape, lambda *a: (0,) * len(shape))


def kernel_call(body, grid, in_specs, out_specs, out_shape, scratch, flops, moved, args, exps=0):
    return pl.pallas_call(
        body,
        out_shape=out_shape,
        grid_spec=pltpu.PrefetchScalarGridSpec(
            num_scalar_prefetch=1,
            grid=grid,
            in_specs=in_specs,
            out_specs=out_specs,
            scratch_shapes=scratch,
        ),
        compiler_params=pltpu.CompilerParams(vmem_limit_bytes=VMEM_LIMIT),
        cost_estimate=pl.CostEstimate(
            flops=flops, bytes_accessed=moved, transcendentals=exps
        ),
    )(*args)


def head_columns(w_query, w_key, w_value, head):
    shared = w_value if head % 2 else w_key
    start = (head // 2) * 96
    return w_query[:, head * 96 : head * 96 + 96], shared[:, start : start + 96]


def pick_heads(table, w_query, w_key, w_value, gain_rows):
    def body(table_ref, q_ref, k_ref, v_ref, gain_ref, out_ref, scr):
        gain = gain_ref[...]
        for head in range(16):
            one, two = head_columns(q_ref, k_ref, v_ref, head)
            scr[head, :, :96] = (one.astype(wide) * gain).astype(low)
            scr[head, :, 96:] = (two.astype(wide) * gain).astype(low)
        for i in range(8):
            out_ref[i] = scr[table_ref[i]]

    args = (w_query, w_key, w_value, gain_rows)
    return kernel_call(
        body,
        (1,),
        [whole_spec(a.shape) for a in args],
        whole_spec((8, 96, 192)),
        jax.ShapeDtypeStruct((8, 96, 192), low),
        [pltpu.VMEM((16, 96, 192), low)],
        0,
        1024 * 1024,
        (table, *args),
    )


def pick_columns(table, first, second, gain_rows):
    rows = first.shape[0]

    def body(table_ref, first_ref, second_ref, gain_ref, out_ref):
        gain = gain_ref[...]
        for i in range(8):
            columns = pl.ds(pl.multiple_of(table_ref[i] * 256, 256), 256)
            out_ref[i, :, :256] = (first_ref[:, columns].astype(wide) * gain).astype(low)
            out_ref[i, :, 256:] = (second_ref[:, columns].astype(wide) * gain).astype(low)

    shape = (8, rows, 512)
    return kernel_call(
        body,
        (1,),
        [whole_spec(first.shape), whole_spec(second.shape), whole_spec(gain_rows.shape)],
        whole_spec(shape),
        jax.ShapeDtypeStruct(shape, low),
        [],
        0,
        4 * first.size,
        (table, first, second, gain_rows),
    )


def assemble_rows(table, *groups):
    rows, width = groups[0].shape[1:]

    def body(table_ref, *refs):
        out_ref, i = refs[-1], 0
        for ref in refs[:-1]:
            for k in range(ref.shape[0]):
                start = pl.multiple_of(table_ref[i] * rows, rows)
                out_ref[pl.ds(start, rows), :] = ref[k]
                i += 1

    shape = (16 * rows, width)
    return kernel_call(
        body,
        (1,),
        [whole_spec(group.shape) for group in groups],
        whole_spec(shape),
        jax.ShapeDtypeStruct(shape, low),
        [],
        0,
        64 * rows * width,
        (table, *groups),
    )


def spread_columns(table, near, far, gain_rows, first, second):
    rows = near.shape[1]

    def body(table_ref, near_ref, far_ref, gain_ref, w1_ref, w2_ref, g1_ref, g2_ref, sum_ref):
        gain = gain_ref[...]
        total = jnp.zeros((rows, 256), wide)
        for i in range(16):
            source = near_ref if i < 8 else far_ref
            columns = pl.ds(pl.multiple_of(table_ref[i] * 256, 256), 256)
            block = source[i % 8].astype(wide)
            one, two = block[:, :256], block[:, 256:]
            total += one * w1_ref[:, columns].astype(wide)
            total += two * w2_ref[:, columns].astype(wide)
            g1_ref[:, columns] = one * gain
            g2_ref[:, columns] = two * gain
        sum_ref[...] = jnp.sum(total, axis=1, keepdims=True)

    return kernel_call(
        body,
        (1,),
        [whole_spec(a.shape) for a in (near, far, gain_rows, first, second)],
        [whole_spec(first.shape), whole_spec(second.shape), whole_spec((rows, 1))],
        [
            jax.ShapeDtypeStruct(first.shape, wide),
            jax.ShapeDtypeStruct(second.shape, wide),
            jax.ShapeDtypeStruct((rows, 1), wide),
        ],
        [],
        0,
        6 * 2 * first.size,
        (table, near, far, gain_rows, first, second),
    )


def spread_heads(table, near, far, w_query, w_key, w_value, gain_rows):
    def body(
        table_ref, near_ref, far_ref, q_ref, k_ref, v_ref, gain_ref, *rest
    ):
        gq_ref, gk_ref, gv_ref, sum_ref, scr = rest
        gain = gain_ref[...]
        for i in range(16):
            source = near_ref if i < 8 else far_ref
            scr[table_ref[i]] = source[i % 8].astype(wide)
        total = jnp.zeros((96, 96), wide)
        for head in range(16):
            one, two = head_columns(q_ref, k_ref, v_ref, head)
            block = scr[head]
            first, second = block[:, :96], block[:, 96:]
            total += first * one.astype(wide) + second * two.astype(wide)
            gq_ref[:, head * 96 : head * 96 + 96] = first * gain
            shared = gv_ref if head % 2 else gk_ref
            start = (head // 2) * 96
            shared[:, start : start + 96] = second * gain
        sum_ref[...] = jnp.sum(total, axis=1, keepdims=True)

    args = (near, far, w_query, w_key, w_value, gain_rows)
    shapes = [w_query.shape, w_key.shape, w_value.shape, (96, 1)]
    return kernel_call(
        body,
        (1,),
        [whole_spec(a.shape) for a in args],
        [whole_spec(shape) for shape in shapes],
        [jax.ShapeDtypeStruct(shape, wide) for shape in shapes],
        [pltpu.VMEM((16, 96, 192), wide)],
        0,
        4 * 1024 * 1024,
        (table, *args),
    )


def turn(rows, cosine, sine):
    front, back = rows[:48], rows[48:]
    return jnp.concatenate([front * cosine - back * sine, back * cosine + front * sine], axis=0)


def turn_back(rows, cosine, sine):
    front, back = rows[:48], rows[48:]
    return jnp.concatenate([front * cosine + back * sine, back * cosine - front * sine], axis=0)


def align_rows(core, rows):
    turned = jnp.concatenate([rows[128:], rows[:128]], axis=0)
    return jnp.where(core == 0, rows, turned)


def align(core, columns):
    turned = jnp.concatenate([columns[:, 128:], columns[:, :128]], axis=1)
    return jnp.where(core == 0, columns, turned)


def table_specs():
    return [pl.BlockSpec((48, 256), lambda g, t: (0, g % 4))] * 4


def cube_spec():
    return pl.BlockSpec((256, 1536), lambda g, t: (t[g], 0))


def project(at, normed, w_heads, tables):
    def body(at_ref, rows_ref, w_ref, cos_ref, sin_ref, cos2_ref, sin2_ref, q_ref, own_ref):
        made = jnp.dot(rows_ref[...], w_ref[...], preferred_element_type=wide).T
        q_ref[0] = turn(made[:96], cos_ref[...], sin_ref[...]).astype(low)
        own_ref[0] = turn(made[96:], cos2_ref[...], sin2_ref[...]).astype(low)

    out_spec = pl.BlockSpec((1, 96, 256), lambda g, t: (g // 4, 0, g % 4))
    shape = jax.ShapeDtypeStruct((2, 96, 1024), low)
    return kernel_call(
        body,
        (8,),
        [cube_spec(), whole_spec((1536, 192))] + table_specs(),
        [out_spec, out_spec],
        [shape, shape],
        [],
        2 * 2048 * 1536 * 192,
        8 * 1024 * 1024,
        (at, normed, w_heads, *tables),
    )


def head_specs():
    kv = pl.BlockSpec((1, 96, 1024), lambda s, t, a: (s, 0, 0))
    other = pl.BlockSpec((1, 1, 96, 1024), lambda s, t, a: (0, s, 0, 0))
    other_far = pl.BlockSpec((1, 1, 96, 1024), lambda s, t, a: (1, s, 0, 0))
    return [kv, kv, other, other_far]


def key_and_value(core, own_ref, far_ref, other_ref, other_far_ref):
    mine = jnp.concatenate([own_ref[0], far_ref[0]], axis=1)
    theirs = jnp.concatenate([other_ref[0, 0], other_far_ref[0, 0]], axis=1)
    keyed = core == 0
    return jnp.where(keyed, mine, theirs), jnp.where(keyed, theirs, mine)


def masked(scores, key_column, query_ref, score_scale):
    return jnp.where(key_column <= query_ref[0], scores * (score_scale * log2_e), masked_score)


def attend_forward(at, queries, held, query_blk, key_blk, score_scale):
    def body(at_ref, q_ref, a_ref, b_ref, c_ref, d_ref, qb_ref, kb_ref, *rest):
        keep_ref, send_ref, att_ref, total_ref, k_scr, v_scr, kb_scr = rest

        @pl.when(pl.program_id(1) == 0)
        def _():
            key_part, value_part = key_and_value(at_ref[8], a_ref, b_ref, c_ref, d_ref)
            k_scr[...] = key_part.astype(wide).T.astype(low)
            v_scr[...] = value_part
            kb_scr[...] = jnp.broadcast_to(kb_ref[0], (128, 2048)).T[:, :1]

        scores = jnp.dot(k_scr[...], q_ref[0], preferred_element_type=wide)
        scores = masked(scores, kb_scr[...], qb_ref, score_scale)
        top = jnp.max(scores, axis=0, keepdims=True)
        likely = jnp.exp2(scores - top)
        column_sum = jnp.sum(likely, axis=0, keepdims=True)
        mixed = jnp.dot(v_scr[...], likely.astype(low), preferred_element_type=wide)
        mixed = mixed / column_sum
        att_ref[0] = mixed
        total_ref[0] = top + jnp.log(column_sum) * log2_e
        mixed = align(at_ref[8], mixed).astype(low)
        keep_ref[0] = mixed[:, :128]
        send_ref[0] = mixed[:, 128:]

    q_spec = pl.BlockSpec((1, 96, 256), lambda s, t, a: (s, 0, t))
    one_spec = pl.BlockSpec((1, 1, 256), lambda s, t, a: (s, 0, t))
    block_spec = pl.BlockSpec((1, 96, 128), lambda s, t, a: (s * 4 + t, 0, 0))
    return kernel_call(
        body,
        (2, 4),
        [q_spec]
        + head_specs()
        + [one_spec, pl.BlockSpec((1, 1, 2048), lambda s, t, a: (s, 0, 0))],
        [block_spec, block_spec, q_spec, one_spec],
        [
            jax.ShapeDtypeStruct((8, 96, 128), low),
            jax.ShapeDtypeStruct((8, 96, 128), low),
            jax.ShapeDtypeStruct((2, 96, 1024), wide),
            jax.ShapeDtypeStruct((2, 1, 1024), wide),
        ],
        [
            pltpu.VMEM((2048, 96), low),
            pltpu.VMEM((96, 2048), low),
            pltpu.VMEM((2048, 1), wide),
        ],
        4 * 2 * 1024 * 2048 * 96,
        12 * 1024 * 1024,
        (at, queries, *held, query_blk, key_blk),
        exps=2 * 1024 * 2048,
    )


def out_project(at, blocks, w_full, residual):
    def body(at_ref, in_ref, w_ref, x_ref, middle_ref, scale_ref, normed_ref, att_ref):
        for i in range(16):
            start = pl.multiple_of(at_ref[i] * 96, 96)
            att_ref[pl.ds(start, 96), :] = in_ref[i]
        rows = att_ref[...].astype(wide).T.astype(low)
        middle = x_ref[...] + jnp.dot(rows, w_ref[...], preferred_element_type=wide)
        scale = rms_scale(middle)
        middle_ref[...] = middle
        scale_ref[...] = scale
        normed_ref[...] = (middle * scale).astype(low)

    shapes = [
        jax.ShapeDtypeStruct((128, 1536), wide),
        jax.ShapeDtypeStruct((128, 1), wide),
        jax.ShapeDtypeStruct((128, 1536), low),
    ]
    return kernel_call(
        body,
        (1,),
        [whole_spec(a.shape) for a in (blocks, w_full, residual)],
        [whole_spec(shape.shape) for shape in shapes],
        shapes,
        [pltpu.VMEM((1536, 128), low)],
        2 * 128 * 1536 * 1536,
        6 * 1024 * 1024,
        (at, blocks, w_full, residual),
    )


def out_back(at, grad_out, sums, middle, scale, w_full):
    def body(at_ref, dy_ref, a_ref, b_ref, c_ref, x_ref, scale_ref, w_ref, *rest):
        middle_ref, low_ref, keep_ref, send_ref, scr = rest
        scaled = jnp.concatenate([a_ref[0], b_ref[0], c_ref[0]], axis=1)
        scale = scale_ref[...]
        normed = x_ref[...] * scale
        grad = dy_ref[...].astype(wide) + scale * (
            scaled - normed * jnp.mean(scaled * normed, axis=-1, keepdims=True)
        )
        middle_ref[...] = grad
        grad = grad.astype(low)
        low_ref[...] = grad
        scr[...] = times_back(w_ref[...], grad).astype(low)
        for i in range(8):
            start = pl.multiple_of(at_ref[i] * 96, 96)
            keep_ref[i] = scr[pl.ds(start, 96), :]
            start = pl.multiple_of(at_ref[8 + i] * 96, 96)
            send_ref[i] = scr[pl.ds(start, 96), :]

    args = (grad_out, *sums, middle, scale, w_full)
    shapes = [
        jax.ShapeDtypeStruct((128, 1536), wide),
        jax.ShapeDtypeStruct((128, 1536), low),
        jax.ShapeDtypeStruct((8, 96, 128), low),
        jax.ShapeDtypeStruct((8, 96, 128), low),
    ]
    return kernel_call(
        body,
        (1,),
        [whole_spec(a.shape) for a in args],
        [whole_spec(shape.shape) for shape in shapes],
        shapes,
        [pltpu.VMEM((1536, 128), low)],
        4 * 128 * 1536 * 1536,
        14 * 1024 * 1024,
        (at, *args),
    )


def attend_backward(
    at, queries, held, query_blk, key_blk, attention, totals, grad_blocks, tables, score_scale
):
    def body(at_ref, q_ref, a_ref, b_ref, c_ref, d_ref, qb_ref, kb_ref, *rest):
        att_ref, total_ref, cos_ref, sin_ref = rest[:4]
        own_ref, core_ref = rest[4:6]
        dq_ref, mine_ref, sent_ref = rest[6:9]
        k_scr, kt_scr, v_scr, dk_scr, dv_scr, kb_scr = rest[9:]
        tile = pl.program_id(1)

        @pl.when(tile == 0)
        def _():
            key_part, value_part = key_and_value(at_ref[8], a_ref, b_ref, c_ref, d_ref)
            kt_scr[...] = key_part
            kb_scr[...] = jnp.broadcast_to(kb_ref[0], (128, 2048)).T[:, :1]
            k_scr[...] = key_part.astype(wide).T.astype(low)
            v_scr[...] = value_part.astype(wide).T.astype(low)
            dk_scr[...] = jnp.zeros_like(dk_scr)
            dv_scr[...] = jnp.zeros_like(dv_scr)

        att = att_ref[0]
        grad_att = align(
            at_ref[8], jnp.concatenate([own_ref[0, 0], core_ref[0, 0]], axis=1).astype(wide)
        ).astype(low)
        delta = jnp.sum(grad_att.astype(wide) * att, axis=0, keepdims=True)
        scores = jnp.dot(k_scr[...], q_ref[0], preferred_element_type=wide)
        scores = masked(scores, kb_scr[...], qb_ref, score_scale)
        chance = jnp.exp2(scores - total_ref[0])
        dv_scr[...] += times_back(grad_att, chance.astype(low))
        grad_chance = jnp.dot(v_scr[...], grad_att, preferred_element_type=wide)
        grad_scores = (chance * (grad_chance - delta)).astype(low)
        grad_query = jnp.dot(kt_scr[...], grad_scores, preferred_element_type=wide)
        dq_ref[0] = turn_back(grad_query * score_scale, cos_ref[...], sin_ref[...]).astype(low)
        dk_scr[...] += times_back(q_ref[0], grad_scores)

        @pl.when(tile == 3)
        def _():
            grad_key = dk_scr[...] * score_scale
            grad_value = dv_scr[...]
            keyed = at_ref[8] == 0
            mine = jnp.where(keyed, grad_key, grad_value)
            sent = jnp.where(keyed, grad_value, grad_key)
            mine_ref[0, 0] = mine[:, :1024].astype(low)
            mine_ref[1, 0] = mine[:, 1024:].astype(low)
            sent_ref[0, 0] = sent[:, :1024].astype(low)
            sent_ref[1, 0] = sent[:, 1024:].astype(low)

    q_spec = pl.BlockSpec((1, 96, 256), lambda s, t, a: (s, 0, t))
    one_spec = pl.BlockSpec((1, 1, 256), lambda s, t, a: (s, 0, t))
    kv_out = pl.BlockSpec((2, 1, 96, 1024), lambda s, t, a: (0, s, 0, 0))
    angle = pl.BlockSpec((48, 256), lambda s, t, a: (0, t))

    def block_of(s, t):
        return (t & 1) * 4 + (t >> 1) * 2 + s

    return kernel_call(
        body,
        (2, 4),
        [q_spec]
        + head_specs()
        + [
            one_spec,
            pl.BlockSpec((1, 1, 2048), lambda s, t, a: (s, 0, 0)),
            q_spec,
            one_spec,
            angle,
            angle,
            pl.BlockSpec((1, 1, 96, 128), lambda s, t, a: (block_of(s, t), 0, 0, 0)),
            pl.BlockSpec((1, 1, 96, 128), lambda s, t, a: (block_of(s, t), 1, 0, 0)),
        ],
        [q_spec, kv_out, kv_out],
        [
            jax.ShapeDtypeStruct((2, 96, 1024), low),
            jax.ShapeDtypeStruct((2, 2, 96, 1024), low),
            jax.ShapeDtypeStruct((2, 2, 96, 1024), low),
        ],
        [
            pltpu.VMEM((2048, 96), low),
            pltpu.VMEM((96, 2048), low),
            pltpu.VMEM((2048, 96), low),
            pltpu.VMEM((96, 2048), wide),
            pltpu.VMEM((96, 2048), wide),
            pltpu.VMEM((2048, 1), wide),
        ],
        10 * 2 * 1024 * 2048 * 96,
        12 * 1024 * 1024,
        (
            at,
            queries,
            *held,
            query_blk,
            key_blk,
            attention,
            totals,
            *tables[:2],
            grad_blocks,
            grad_blocks,
        ),
        exps=2 * 1024 * 2048,
    )


def head_grads(dq_ref, ds_ref, cos_ref, sin_ref):
    own = turn_back(ds_ref[0], cos_ref[...], sin_ref[...])
    return jnp.concatenate([dq_ref[0].astype(wide), own], axis=0)


def head_grad_specs():
    q_spec = pl.BlockSpec((1, 96, 256), lambda g, t: (g // 4, 0, g % 4))
    return table_specs()[:2] + [q_spec, q_spec]


def head_weights(at, normed, tables, grad_queries, grad_own):
    def body(at_ref, rows_ref, cos_ref, sin_ref, dq_ref, ds_ref, *rest):
        keep_ref, send_ref, gw_scr, nat_scr = rest
        g = pl.program_id(0)

        @pl.when(g == 0)
        def _():
            gw_scr[...] = jnp.zeros_like(gw_scr)

        both = head_grads(dq_ref, ds_ref, cos_ref, sin_ref)
        gw_scr[...] += jnp.dot(both.astype(low), rows_ref[...], preferred_element_type=wide)

        @pl.when(g == 7)
        def _():
            nat_scr[...] = gw_scr[...].T
            for i in range(8):
                start = pl.multiple_of(at_ref[9 + i] * 96, 96)
                keep_ref[i] = nat_scr[pl.ds(start, 96), :].astype(low)
                start = pl.multiple_of(at_ref[17 + i] * 96, 96)
                send_ref[i] = nat_scr[pl.ds(start, 96), :].astype(low)

    blocks = jax.ShapeDtypeStruct((8, 96, 192), low)
    return kernel_call(
        body,
        (8,),
        [cube_spec()] + head_grad_specs(),
        [whole_spec((8, 96, 192))] * 2,
        [blocks, blocks],
        [pltpu.VMEM((192, 1536), wide), pltpu.VMEM((1536, 192), wide)],
        2 * 2048 * 1536 * 192,
        8 * 1024 * 1024,
        (at, normed, *tables[2:], grad_queries, grad_own),
    )


def project_back(at, w_heads, tables, grad_queries, grad_own):
    def body(at_ref, w_ref, cos_ref, sin_ref, dq_ref, ds_ref, *outs):
        both = align(at_ref[8], head_grads(dq_ref, ds_ref, cos_ref, sin_ref))
        store_rows(outs, times_back(both.T.astype(low), w_ref[...]))

    return kernel_call(
        body,
        (8,),
        [whole_spec((1536, 192))] + head_grad_specs(),
        row_specs(THIRDS, lambda g, t: g),
        row_shapes(THIRDS),
        [],
        2 * 2048 * 1536 * 192,
        8 * 1024 * 1024,
        (at, w_heads, *tables[2:], grad_queries, grad_own),
    )


def hidden_back(at, grads, w_rows):
    def body(at_ref, *refs):
        rows, (w_ref, out_ref) = refs[:4], refs[4:]
        out_ref[...] = align_rows(at_ref[8], times_back(load_rows(rows), w_ref[...]))

    return kernel_call(
        body,
        (8,),
        row_specs(HALVES, lambda g, t: g) + [whole_spec((256, 1536))],
        pl.BlockSpec((256, 256), lambda g, t: (g, 0)),
        jax.ShapeDtypeStruct((2048, 256), wide),
        [],
        2 * 2048 * 1536 * 256,
        8 * 1024 * 1024,
        (at, *flat(grads), w_rows),
    )


def feed_back(at, normed, w_both, grad_hidden):
    def body(at_ref, rows_ref, w_ref, dh_ref, *rest):
        outs, (hidden_ref, both_ref) = rest[:6], rest[6:]
        both = jnp.dot(rows_ref[...], w_ref[...], preferred_element_type=wide)
        gate, up = both[:, :256], both[:, 256:]
        bend = jax.nn.sigmoid(gate)
        smooth = gate * bend
        grad_hidden = dh_ref[...]
        hidden_ref[...] = (smooth * up).astype(low)
        grad_gate = grad_hidden * up * (bend + smooth * (1.0 - bend))
        grad_both = jnp.concatenate([grad_gate, grad_hidden * smooth], axis=1).astype(low)
        both_ref[...] = grad_both
        store_rows(outs, align_rows(at_ref[8], times_back(grad_both, w_ref[...])))

    return kernel_call(
        body,
        (8,),
        [cube_spec(), whole_spec((1536, 512)), pl.BlockSpec((256, 256), lambda g, t: (g, 0))],
        row_specs(THIRDS, lambda g, t: g)
        + [
            pl.BlockSpec((256, 256), lambda g, t: (g, 0)),
            pl.BlockSpec((256, 512), lambda g, t: (g, 0)),
        ],
        row_shapes(THIRDS)
        + [
            jax.ShapeDtypeStruct((2048, 256), low),
            jax.ShapeDtypeStruct((2048, 512), low),
        ],
        [],
        4 * 2048 * 1536 * 512,
        18 * 1024 * 1024,
        (at, normed, w_both, grad_hidden),
        exps=2048 * 256,
    )


def feed_out(at, hidden, w_rows):
    def body(at_ref, hidden_ref, w_ref, *outs):
        made = jnp.dot(hidden_ref[...], w_ref[...], preferred_element_type=wide)
        store_rows(outs, align_rows(at_ref[8], made))

    return kernel_call(
        body,
        (8,),
        [pl.BlockSpec((256, 256), lambda g, t: (g, 0)), whole_spec((256, 1536))],
        row_specs(HALVES, lambda g, t: g),
        row_shapes(HALVES),
        [],
        2 * 2048 * 1536 * 256,
        8 * 1024 * 1024,
        (at, hidden, w_rows),
    )


def down_weights(at, hidden, grads):
    def body(at_ref, *refs):
        rows, (hidden_ref, gw_ref, gw_scr) = refs[:4], refs[4:]
        g = pl.program_id(0)

        @pl.when(g == 0)
        def _():
            gw_scr[...] = jnp.zeros_like(gw_scr)

        held = align_rows(at_ref[8], hidden_ref[...].astype(wide)).astype(low)
        gw_scr[...] += over_rows(held, load_rows(rows))

        @pl.when(g == 7)
        def _():
            gw_ref[...] = gw_scr[...].astype(low)

    return kernel_call(
        body,
        (8,),
        row_specs(HALVES, lambda g, t: g) + [pl.BlockSpec((256, 256), lambda g, t: (g, 0))],
        whole_spec((256, 1536)),
        jax.ShapeDtypeStruct((256, 1536), low),
        [pltpu.VMEM((256, 1536), wide)],
        2 * 2048 * 1536 * 256,
        8 * 1024 * 1024,
        (at, *flat(grads), hidden),
    )


def out_weights(at, attention, grads):
    def body(at_ref, att_ref, rows_ref, gw_ref, gw_scr):
        g = pl.program_id(0)

        @pl.when(g == 0)
        def _():
            gw_scr[...] = jnp.zeros_like(gw_scr)

        gw_scr[...] += jnp.dot(
            att_ref[0].astype(low), rows_ref[...], preferred_element_type=wide
        )

        @pl.when(g == 7)
        def _():
            gw_ref[...] = gw_scr[...].astype(low)

    return kernel_call(
        body,
        (8,),
        [pl.BlockSpec((1, 96, 256), lambda g, t: (g // 4, 0, g % 4)), cube_spec()],
        whole_spec((96, 1536)),
        jax.ShapeDtypeStruct((96, 1536), low),
        [pltpu.VMEM((96, 1536), wide)],
        2 * 2048 * 1536 * 96,
        8 * 1024 * 1024,
        (at, attention, grads),
    )


def feed_weights(at, normed, grad_both):
    def body(at_ref, rows_ref, both_ref, keep_ref, send_ref, gw_scr, nat_scr):
        g = pl.program_id(0)

        @pl.when(g == 0)
        def _():
            gw_scr[...] = jnp.zeros_like(gw_scr)

        gw_scr[...] += over_rows(both_ref[...], rows_ref[...])

        @pl.when(g == 7)
        def _():
            nat_scr[...] = gw_scr[...].T
            for i in range(8):
                start = pl.multiple_of(at_ref[9 + i] * 96, 96)
                keep_ref[i] = nat_scr[pl.ds(start, 96), :].astype(low)
                start = pl.multiple_of(at_ref[17 + i] * 96, 96)
                send_ref[i] = nat_scr[pl.ds(start, 96), :].astype(low)

    return kernel_call(
        body,
        (8,),
        [cube_spec(), pl.BlockSpec((256, 512), lambda g, t: (g, 0))],
        [whole_spec((8, 96, 512))] * 2,
        [jax.ShapeDtypeStruct((8, 96, 512), low)] * 2,
        [pltpu.VMEM((512, 1536), wide), pltpu.VMEM((1536, 512), wide)],
        2 * 2048 * 1536 * 512,
        14 * 1024 * 1024,
        (at, normed, grad_both),
    )


def sum_low(left, right):
    return (left.astype(wide) + right.astype(wide)).astype(low)


def cube_plan(
    inputs,
    cotangent,
    block_ids,
    piece_order,
    w_query,
    w_key,
    w_value,
    w_out,
    w_gate,
    w_up,
    w_down,
    gain_attn,
    gain_mlp,
):
    x = lax.axis_index("grp")
    seq_at = lax.axis_index("seq")
    zh, c = seq_at >> 3, seq_at & 1
    score_scale = HEAD_DIM ** (-0.5)
    gain_rows_attn = gain_attn.astype(wide)[:, None]
    gain_rows_mlp = gain_mlp.astype(wide)[:, None]
    eight = jnp.arange(8, dtype=jnp.int32)
    sixteen = jnp.arange(16, dtype=jnp.int32)
    cyl = (eight >> 2) + (eight & 2) + ((eight & 1) << 2)
    place = c.astype(jnp.int32)[None]
    natural = seq_at ^ sixteen

    def owns_out(i):
        return bit_of(i, BIT_X) == bit_of(i, BIT_ZH)

    def owns_down(i):
        return bit_of(i, BIT_X) ^ bit_of(i, BIT_C) == bit_of(i, BIT_ZH)

    def lacks_out(i):
        return not owns_out(i)

    def lacks_down(i):
        return not owns_down(i)

    out_owner, down_owner = x == zh, (x ^ c) == zh

    order = ((sixteen & 8)) | ((sixteen & 4) >> 1) | ((sixteen & 2) << 1) | (sixteen & 1)
    stored = (seq_at & 14) ^ order
    pieces = jnp.sum(
        jnp.where(stored[:, None] == sixteen[None, :], piece_order[None, :], 0), axis=1
    )
    own_pos = (pieces[:8, None] * 128 + jnp.arange(128, dtype=jnp.int32)[None, :]).reshape(1024)
    frequency = rope_base ** (-jnp.arange(HEAD_DIM // 2, dtype=wide) * 2.0 / HEAD_DIM)
    angles = frequency[:, None] * own_pos.astype(wide)[None, :]
    cosine, sine = jnp.cos(angles), jnp.sin(angles)
    keyed = c == 0
    tables = (
        cosine,
        sine,
        jnp.where(keyed, cosine, 1.0),
        jnp.where(keyed, sine, 0.0),
    )

    low_zy = ((eight & 1) << 2) | (eight & 2)
    side_of = x ^ (eight >> 2)
    spots = jnp.concatenate([side_of * 4 + (((seq_at ^ low_zy) & 7) >> 1), place])
    spots_rows = jnp.concatenate([spots, natural])
    head_for = jnp.concatenate(
        [side_of * 8 + ((seq_at ^ low_zy ^ core) & 7) for core in (0, 1)]
    )

    residual = inputs[0].astype(wide)
    scale_first = rms_scale(residual)
    normed_first = residual * scale_first
    normed = cube_gather(normed_first.astype(low))
    head_of = x * 8 + ((seq_at ^ cyl) & 7)
    heads = pick_heads(head_of, w_query, w_key, w_value, gain_rows_attn)
    heads = trade_block(heads.reshape(2, 2, 2, 96, 192), 0, BIT_C)
    heads, w_out_held = sync(heads, w_out)
    out_near = swap(w_out_held, BIT_ZH, owns_out)
    heads = trade_block(heads, 1, BIT_Y)
    heads, ids_held, up_held = sync(heads, block_ids, w_up)
    heads = trade_block(heads, 2, BIT_ZL)
    other_ids = swap(ids_held, BIT_X)
    wanted_mlp = (x ^ ((seq_at ^ cyl) & 1)) * 8 + ((seq_at ^ cyl) & 7)
    both_blocks = pick_columns(wanted_mlp, w_gate, up_held, gain_rows_mlp)
    heads, out_near, both_blocks = sync(heads, out_near, both_blocks)
    heads = heads.reshape(8, 96, 192)
    heads_far = swap(heads, BIT_ZH)
    both_blocks = trade_block(both_blocks.reshape(2, 2, 2, 96, 512), 0, BIT_C)
    both_blocks = trade_block(both_blocks, 1, BIT_Y)
    both_blocks = trade_block(both_blocks, 2, BIT_ZL)
    w_out_head = jnp.where(out_owner, w_out, out_near)
    heads, heads_far, both_blocks, w_down_held, tables = sync(
        heads, heads_far, both_blocks, w_down, tables
    )
    w_heads = assemble_rows(natural, heads, heads_far)
    ids = jnp.concatenate([block_ids, other_ids], axis=0).reshape(2, 16, 128)
    chosen = (pieces[:, None] == sixteen[None, :]).astype(low)
    blocks = jnp.einsum(
        "kp,spr->skr", chosen, ids.astype(low), preferred_element_type=wide
    ).reshape(2, 1, 2048)
    query_blk, key_blk = blocks[:, :, :1024], blocks
    normed, w_heads, both_blocks, w_out_head, query_blk, key_blk, rows_dy = sync(
        normed, w_heads, both_blocks, w_out_head, query_blk, key_blk, cotangent[0]
    )

    out_full = cube_gather(w_out_head)
    grads = gather_next(gather_start(rows_dy, HALVES), HALVES, 0)
    queries, own_part = project(spots, normed, w_heads, tables)
    queries, own_part, grads, both_blocks = sync(queries, own_part, grads, both_blocks)
    far_part = swap(own_part, BIT_ZH)
    grads = gather_next(grads, HALVES, 1)
    far_part, grads, both_blocks = sync(far_part, grads, both_blocks)
    other_parts = swap(jnp.stack([own_part, far_part]), BIT_C)
    other_parts, far_part, grads = sync(other_parts, far_part, grads)
    held = (own_part, far_part, other_parts, other_parts)
    grads = gather_next(grads, HALVES, 2)
    near_rows = [both_blocks[0].reshape(4, 96, 512), both_blocks[1].reshape(4, 96, 512)]
    far_first = swap(near_rows[0], BIT_ZH)
    keep, send, attention, totals = attend_forward(
        spots, queries, held, query_blk, key_blk, score_scale
    )
    keep, send, attention, totals, near_rows, out_full, w_down_held = sync(
        keep, send, attention, totals, near_rows, out_full, w_down_held
    )

    traded = jnp.stack([keep, swap(send, BIT_C)]).reshape(2, 2, 2, 2, 96, 128)
    traded, far_first, w_down_held = sync(traded, far_first, w_down_held)
    traded = trade_block(traded, 3, BIT_ZL)
    traded, grads, w_down_held = sync(traded, grads, w_down_held)
    down_near = swap(w_down_held, BIT_ZH, owns_down)
    grads = gather_last(grads)
    traded = trade_block(traded, 2, BIT_X)
    traded, grads = sync(traded, grads)
    traded = trade_block(traded, 3, BIT_Y).reshape(16, 96, 128)
    traded, residual, down_near, near_rows = sync(traded, residual, down_near, near_rows)
    far_second = swap(near_rows[1], BIT_ZH)
    yxlc = ((sixteen & 8) >> 2) | ((sixteen & 2) << 1) | (sixteen & 1)
    head_from = (x ^ ((sixteen & 4) >> 2)) * 8 + ((seq_at ^ yxlc) & 7)
    middle, scale_second, rows_second = out_project(head_from, traded, out_full, residual)

    rows_second, middle, scale_second, grads = sync(rows_second, middle, scale_second, grads)
    normed_mlp = cube_gather(rows_second)
    w_rows = jnp.where(down_owner, w_down_held, down_near)
    grad_hidden = hidden_back(spots, grads, w_rows)
    w_both = assemble_rows(natural, *near_rows, far_first, far_second)
    normed_mlp, grad_hidden, w_both = sync(normed_mlp, grad_hidden, w_both)
    made = feed_back(spots, normed_mlp, w_both, grad_hidden)
    hidden, grad_both = made[6:]
    sums = scatter_start(paired(made[:6]))
    sums, hidden, grad_both = sync(sums, hidden, grad_both)
    sums = scatter_next(sums, THIRDS, 2)
    keep_both, send_both = feed_weights(spots_rows, normed_mlp, grad_both)
    sums, keep_both, send_both = sync(sums, keep_both, send_both)
    sums = scatter_next(sums, THIRDS, 1)
    sums, = sync(sums)
    sums = scatter_next(sums, THIRDS, 0)
    sums, hidden, send_both = sync(sums, hidden, send_both)

    parts = scatter_last(sums)
    grad_middle, grad_low, keep, send = out_back(
        head_for, cotangent[0], parts, middle, scale_second, out_full
    )
    grad_middle, grad_low, keep, send, hidden, send_both = sync(
        grad_middle, grad_low, keep, send, hidden, send_both
    )
    middle_rows = cube_gather(grad_low)
    arrived_second = swap(send_both[4:], BIT_ZH)
    traded = jnp.stack([keep, swap(send, BIT_C)]).reshape(2, 2, 2, 2, 96, 128)
    traded, hidden = sync(traded, hidden)
    grad_down = down_weights(spots, hidden, grads)
    traded = trade_block(traded, 1, BIT_X)
    traded, grad_down, hidden, arrived_second, send_both = sync(
        traded, grad_down, hidden, arrived_second, send_both
    )
    arrived_first = swap(send_both[:4], BIT_ZH)
    out_terms = feed_out(spots, hidden, w_rows)
    traded = trade_block(traded, 2, BIT_Y)
    traded, grad_down, out_terms = sync(traded, grad_down, out_terms)
    traded = trade_block(traded, 3, BIT_ZL).reshape(8, 2, 96, 128)
    out_sums = scatter_start(paired(out_terms))
    both_send = sum_low(keep_both[4:], arrived_second)
    traded, out_sums, arrived_first, both_send, grad_down = sync(
        traded, out_sums, arrived_first, both_send, grad_down
    )
    out_sums = scatter_next(out_sums, HALVES, 2)
    down_arrived = swap(grad_down, BIT_ZH, lacks_down)
    both_sent = swap(both_send, BIT_ZL)
    made = attend_backward(
        spots,
        queries,
        held,
        query_blk,
        key_blk,
        attention,
        totals,
        traded,
        tables,
        score_scale,
    )
    made, out_sums, down_arrived, both_sent = sync(made, out_sums, down_arrived, both_sent)
    grad_queries, mine, sent = made
    both_sum = jnp.stack([sum_low(keep_both[:4], arrived_first), both_sent])
    arrived = swap(sent, BIT_C)
    arrived, both_sum, grad_down = sync(arrived, both_sum, grad_down)
    far_terms = sum_low(mine[1], arrived[1])
    far_terms, out_sums, both_sum, attention, middle_rows = sync(
        far_terms, out_sums, both_sum, attention, middle_rows
    )
    far_sum = swap(far_terms, BIT_ZH)
    out_sums = scatter_next(out_sums, HALVES, 1)
    grad_out_head = out_weights(spots, attention, middle_rows)
    far_sum, out_sums, both_sum, grad_out_head = sync(
        far_sum, out_sums, both_sum, grad_out_head
    )
    both_sum = trade_block(both_sum.reshape(2, 2, 2, 96, 512), 1, BIT_Y)
    down_sum = sum_low(grad_down, down_arrived)
    down_far = swap(down_sum, BIT_X, owns_down)
    out_sums = scatter_next(out_sums, HALVES, 0)
    grad_own = mine[0].astype(wide) + arrived[0].astype(wide) + far_sum.astype(wide)
    keep_heads, send_heads = head_weights(
        spots_rows, normed, tables, grad_queries, grad_own
    )
    out_arrived = swap(grad_out_head, BIT_ZH, lacks_out)
    keep_heads, send_heads, grad_own, both_sum, down_far, out_arrived = sync(
        keep_heads, send_heads, grad_own, both_sum, down_far, out_arrived
    )
    both_near = trade_block(both_sum, 2, BIT_C).reshape(8, 96, 512)
    both_far = swap(both_near, BIT_X)
    heads_first = swap(send_heads, BIT_ZH)
    made = project_back(spots, w_heads, tables, grad_queries, grad_own)
    made, heads_first, both_far, out_sums = sync(made, heads_first, both_far, out_sums)
    sums = scatter_start(paired(made))
    heads_sum = sum_low(keep_heads, heads_first)
    sums, heads_sum = sync(sums, heads_sum)
    heads_sum = trade_block(heads_sum.reshape(2, 2, 2, 96, 192), 0, BIT_ZL)
    sums = scatter_next(sums, THIRDS, 2)
    sums, heads_sum = sync(sums, heads_sum)
    out_sum = sum_low(grad_out_head, out_arrived)
    out_far = swap(out_sum, BIT_X, owns_out)
    output = jnp.concatenate([part[0] for part in scatter_last(out_sums)], axis=1)
    output = (middle + output).astype(low)
    heads_sum = trade_block(heads_sum, 1, BIT_Y)
    sums = scatter_next(sums, THIRDS, 1)
    sums, output, heads_sum, out_far = sync(sums, output, heads_sum, out_far)
    heads_near = trade_block(heads_sum, 2, BIT_C).reshape(8, 96, 192)
    heads_far = swap(heads_near, BIT_X)
    sums = scatter_next(sums, THIRDS, 0)
    sums, heads_far = sync(sums, heads_far)
    scaled_first = jnp.concatenate([part[0] for part in scatter_last(sums)], axis=1)
    grad_inputs = grad_middle + scale_first * (
        scaled_first
        - normed_first * jnp.mean(scaled_first * normed_first, axis=-1, keepdims=True)
    )

    back = seq_at ^ cyl
    home = jnp.concatenate([x * 8 + (back & 7), (1 - x) * 8 + (back & 7)])
    grad_w_query, grad_w_key, grad_w_value, grad_gain_attn = spread_heads(
        home, heads_near, heads_far, w_query, w_key, w_value, gain_rows_attn
    )
    grad_w_out = jnp.where(out_owner, out_sum, out_far).astype(wide)
    grad_w_down = jnp.where(down_owner, down_sum, down_far).astype(wide)
    side = (back & 1) ^ x
    home = jnp.concatenate([side * 8 + (back & 7), (1 - side) * 8 + (back & 7)])
    grad_w_gate, grad_w_up, grad_gain_mlp = spread_columns(
        home, both_near, both_far, gain_rows_mlp, w_gate, w_up
    )
    return (
        output[None],
        grad_inputs.astype(low)[None],
        grad_w_query,
        grad_w_key,
        grad_w_value,
        grad_w_out,
        grad_w_gate,
        grad_w_up,
        grad_w_down,
        grad_gain_attn[:, 0],
        grad_gain_mlp[:, 0],
    )


def ring_plan(
    inputs,
    cotangent,
    block_ids,
    piece_order,
    w_query,
    w_key,
    w_value,
    w_out,
    w_gate,
    w_up,
    w_down,
    gain_attn,
    gain_mlp,
):
    shards = (w_query, w_key, w_value, w_out, w_gate, w_up, w_down, gain_attn, gain_mlp)
    (
        full_query,
        full_key,
        full_value,
        full_out,
        full_gate,
        full_up,
        full_down,
        gain_one,
        gain_two,
    ) = (
        lax.all_gather(shards[0], "seq", axis=0, tiled=True),
        lax.all_gather(shards[1], "seq", axis=0, tiled=True),
        lax.all_gather(shards[2], "seq", axis=0, tiled=True),
        lax.all_gather(shards[3], "seq", axis=0, tiled=True),
        lax.all_gather(shards[4], "seq", axis=0, tiled=True),
        lax.all_gather(shards[5], "seq", axis=0, tiled=True),
        lax.all_gather(shards[6], "seq", axis=0, tiled=True),
        lax.all_gather(shards[7], "seq", axis=0, tiled=True),
        lax.all_gather(shards[8], "seq", axis=0, tiled=True),
    )
    seq_count, tok_rows, model_width = inputs.shape
    row_count = seq_count * tok_rows
    head_count = HEADS
    kv_heads = KV_HEADS
    head_dim = HEAD_DIM
    groups = head_count // kv_heads
    kv_width = kv_heads * head_dim
    q_width = head_count * head_dim
    score_scale = head_dim ** (-0.5)
    own_first = jnp.take(piece_order, lax.axis_index("seq")) * tok_rows
    local_pos = own_first + jnp.arange(tok_rows, dtype=jnp.int32)
    cosine_table, sine_table = rotary_tables(local_pos, head_dim)
    query_blk = jnp.take(block_ids, local_pos, axis=1)

    def key_positions(key_count):
        stored = jnp.arange(key_count, dtype=jnp.int32)
        return jnp.take(piece_order, stored // tok_rows) * tok_rows + stored % tok_rows

    residual = inputs.reshape(row_count, model_width).astype(jnp.float32)
    gain_first = gain_one.astype(jnp.float32)
    gain_second = gain_two.astype(jnp.float32)
    scale_first = rms_scale(residual)
    normed_attn = (residual * scale_first * gain_first).astype(jnp.bfloat16)
    query_pre = jnp.dot(normed_attn, full_query, preferred_element_type=jnp.float32)
    key_pre = jnp.dot(normed_attn, full_key, preferred_element_type=jnp.float32)
    value_pre = jnp.dot(normed_attn, full_value, preferred_element_type=jnp.float32)
    queries = rotate(
        query_pre.reshape(seq_count, tok_rows, head_count, head_dim), cosine_table, sine_table
    ).astype(jnp.bfloat16)
    key_rot = rotate(
        key_pre.reshape(seq_count, tok_rows, kv_heads, head_dim), cosine_table, sine_table
    ).astype(jnp.bfloat16)
    values = value_pre.astype(jnp.bfloat16)
    kv_local = jnp.concatenate(
        [
            key_rot.reshape(seq_count, tok_rows, kv_width),
            values.reshape(seq_count, tok_rows, kv_width),
        ],
        axis=2,
    )
    query_grouped = queries.reshape(seq_count, tok_rows, kv_heads, groups, head_dim)
    start_max = jnp.full((seq_count, kv_heads, groups, tok_rows), masked_score, jnp.float32)
    start_sum = jnp.zeros((seq_count, kv_heads, groups, tok_rows), jnp.float32)
    start_acc = jnp.zeros((seq_count, kv_heads, groups, tok_rows, head_dim), jnp.float32)
    state_in = (start_max, start_sum, start_acc)
    key_piece = lax.all_gather(kv_local, "seq", axis=1, tiled=True)
    key_count = key_piece.shape[1]
    block_rows = key_block_rows(key_count)
    key_pos = key_positions(key_count)
    member = 0
    key_blk = jnp.take(block_ids[member], key_pos).reshape(key_count // block_rows, block_rows)
    kv_rows = key_piece[member].reshape(key_count // block_rows, block_rows, 2 * kv_width)
    own_query = query_grouped[member]
    own_blocks = query_blk[member]

    def forward_key_step(running, block_in):
        kv_block, blk_block = block_in
        key_part = kv_block[:, :kv_width].reshape(block_rows, kv_heads, head_dim)
        value_part = kv_block[:, kv_width:].reshape(block_rows, kv_heads, head_dim)
        running = forward_block(
            running, own_query, own_blocks, key_part, value_part, blk_block, score_scale
        )
        return (running, None)

    running, unused = lax.scan(
        forward_key_step,
        (state_in[0][member], state_in[1][member], state_in[2][member]),
        (kv_rows, key_blk),
    )
    results = [running]
    row_max = jnp.stack([entry[0] for entry in results])
    row_sum = jnp.stack([entry[1] for entry in results])
    running_sum = jnp.stack([entry[2] for entry in results])
    log_total = row_max + jnp.log(row_sum)
    attention = running_sum / row_sum[..., None]
    attended = (
        jnp.transpose(attention, (0, 3, 1, 2, 4)).reshape(row_count, q_width).astype(jnp.bfloat16)
    )
    middle = residual + jnp.dot(attended, full_out, preferred_element_type=jnp.float32)
    scale_second = rms_scale(middle)
    normed_mlp = (middle * scale_second * gain_second).astype(jnp.bfloat16)
    gate_value = jnp.dot(normed_mlp, full_gate, preferred_element_type=jnp.float32)
    upward = jnp.dot(normed_mlp, full_up, preferred_element_type=jnp.float32)
    sigmoid_gate = jax.nn.sigmoid(gate_value)
    hidden = (gate_value * sigmoid_gate * upward).astype(jnp.bfloat16)
    output = (middle + jnp.dot(hidden, full_down, preferred_element_type=jnp.float32)).astype(
        jnp.bfloat16
    )
    (
        full_query,
        full_key,
        full_value,
        full_out,
        full_gate,
        full_up,
        full_down,
        gain_one,
        gain_two,
    ) = (
        lax.all_gather(shards[0], "seq", axis=0, tiled=True),
        lax.all_gather(shards[1], "seq", axis=0, tiled=True),
        lax.all_gather(shards[2], "seq", axis=0, tiled=True),
        lax.all_gather(shards[3], "seq", axis=0, tiled=True),
        lax.all_gather(shards[4], "seq", axis=0, tiled=True),
        lax.all_gather(shards[5], "seq", axis=0, tiled=True),
        lax.all_gather(shards[6], "seq", axis=0, tiled=True),
        lax.all_gather(shards[7], "seq", axis=0, tiled=True),
        lax.all_gather(shards[8], "seq", axis=0, tiled=True),
    )
    gain_first = gain_one.astype(jnp.float32)
    gain_second = gain_two.astype(jnp.float32)
    upstream = cotangent.reshape(row_count, model_width)
    grad_down = over_rows(hidden, upstream)
    grad_hidden = times_back(upstream, full_down)
    grad_gate = (
        grad_hidden * upward * sigmoid_gate * (1.0 + gate_value * (1.0 - sigmoid_gate))
    ).astype(jnp.bfloat16)
    grad_upward = (grad_hidden * gate_value * sigmoid_gate).astype(jnp.bfloat16)
    grad_w_gate = over_rows(normed_mlp, grad_gate)
    grad_w_up = over_rows(normed_mlp, grad_upward)
    grad_normed_mlp = times_back(grad_gate, full_gate) + times_back(grad_upward, full_up)
    grad_mid_norm, grad_gain_mlp = norm_back(grad_normed_mlp, middle, scale_second, gain_second)
    grad_middle = upstream.astype(jnp.float32) + grad_mid_norm
    grad_middle_low = grad_middle.astype(jnp.bfloat16)
    grad_w_out = over_rows(attended, grad_middle_low)
    grad_attended = times_back(grad_middle_low, full_out).astype(jnp.bfloat16)
    grad_heads = jnp.transpose(
        grad_attended.reshape(seq_count, tok_rows, kv_heads, groups, head_dim), (0, 2, 3, 1, 4)
    )
    delta_rows = jnp.sum(grad_heads.astype(jnp.float32) * attention, axis=-1)
    start_query = jnp.zeros((seq_count, kv_heads, groups, tok_rows, head_dim), jnp.float32)
    start_kv = jnp.zeros((seq_count, block_ids.shape[1], 2 * kv_width), jnp.float32)
    state_in = (start_query, start_kv)
    key_piece = lax.all_gather(kv_local, "seq", axis=1, tiled=True)
    key_count = key_piece.shape[1]
    backward_block_rows = key_block_rows(key_count)
    key_pos = key_positions(key_count)
    member = 0
    key_blk = jnp.take(block_ids[member], key_pos).reshape(
        key_count // backward_block_rows, backward_block_rows
    )
    kv_rows = key_piece[member].reshape(
        key_count // backward_block_rows, backward_block_rows, 2 * kv_width
    )
    backward_own_query = query_grouped[member]
    backward_own_blocks = query_blk[member]
    own_total = log_total[member]
    own_grads = grad_heads[member]
    own_delta = delta_rows[member]

    def backward_key_step(grad_query, block_in):
        kv_block, blk_block = block_in
        key_part = kv_block[:, :kv_width].reshape(backward_block_rows, kv_heads, head_dim)
        value_part = kv_block[:, kv_width:].reshape(backward_block_rows, kv_heads, head_dim)
        result = backward_block(
            grad_query,
            backward_own_query,
            backward_own_blocks,
            key_part,
            value_part,
            blk_block,
            own_total,
            own_grads,
            own_delta,
            score_scale,
        )
        return (result[0], (result[1], result[2]))

    grad_query, key_grads = lax.scan(backward_key_step, state_in[0][member], (kv_rows, key_blk))
    fresh = jnp.concatenate(
        [key_grads[0].reshape(key_count, kv_width), key_grads[1].reshape(key_count, kv_width)],
        axis=1,
    )
    query_grads = [grad_query]
    kv_grads = [fresh]
    grad_query_all = jnp.stack(query_grads)
    grad_kv_all = jnp.stack(kv_grads)
    grad_kv_own = lax.psum_scatter(grad_kv_all, "seq", scatter_dimension=1, tiled=True)
    grad_query_rows = jnp.transpose(grad_query_all, (0, 3, 1, 2, 4)).reshape(
        seq_count, tok_rows, head_count, head_dim
    )
    grad_query_pre = (
        unrotate(grad_query_rows, cosine_table, sine_table)
        .reshape(row_count, q_width)
        .astype(jnp.bfloat16)
    )
    grad_key_rows = grad_kv_own[:, :, :kv_width].reshape(seq_count, tok_rows, kv_heads, head_dim)
    grad_key_pre = (
        unrotate(grad_key_rows, cosine_table, sine_table)
        .reshape(row_count, kv_width)
        .astype(jnp.bfloat16)
    )
    grad_value_pre = grad_kv_own[:, :, kv_width:].reshape(row_count, kv_width).astype(jnp.bfloat16)
    grad_w_query = over_rows(normed_attn, grad_query_pre)
    grad_w_key = over_rows(normed_attn, grad_key_pre)
    grad_w_value = over_rows(normed_attn, grad_value_pre)
    grad_normed_attn = (
        times_back(grad_query_pre, full_query)
        + times_back(grad_key_pre, full_key)
        + times_back(grad_value_pre, full_value)
    )
    grad_in_norm, grad_gain_attn = norm_back(grad_normed_attn, residual, scale_first, gain_first)
    grad_inputs = (
        (grad_middle + grad_in_norm).astype(jnp.bfloat16).reshape(seq_count, tok_rows, model_width)
    )
    terms = (
        grad_w_query,
        grad_w_key,
        grad_w_value,
        grad_w_out,
        grad_w_gate,
        grad_w_up,
        grad_down,
        grad_gain_attn,
        grad_gain_mlp,
    )
    shares = (
        lax.psum_scatter(terms[0], "seq", scatter_dimension=0, tiled=True),
        lax.psum_scatter(terms[1], "seq", scatter_dimension=0, tiled=True),
        lax.psum_scatter(terms[2], "seq", scatter_dimension=0, tiled=True),
        lax.psum_scatter(terms[3], "seq", scatter_dimension=0, tiled=True),
        lax.psum_scatter(terms[4], "seq", scatter_dimension=0, tiled=True),
        lax.psum_scatter(terms[5], "seq", scatter_dimension=0, tiled=True),
        lax.psum_scatter(terms[6], "seq", scatter_dimension=0, tiled=True),
        lax.psum_scatter(terms[7], "seq", scatter_dimension=0, tiled=True),
        lax.psum_scatter(terms[8], "seq", scatter_dimension=0, tiled=True),
    )
    totals = (
        lax.psum(shares[0].astype(jnp.bfloat16), "grp").astype(jnp.float32),
        lax.psum(shares[1].astype(jnp.bfloat16), "grp").astype(jnp.float32),
        lax.psum(shares[2].astype(jnp.bfloat16), "grp").astype(jnp.float32),
        lax.psum(shares[3].astype(jnp.bfloat16), "grp").astype(jnp.float32),
        lax.psum(shares[4].astype(jnp.bfloat16), "grp").astype(jnp.float32),
        lax.psum(shares[5].astype(jnp.bfloat16), "grp").astype(jnp.float32),
        lax.psum(shares[6].astype(jnp.bfloat16), "grp").astype(jnp.float32),
        lax.psum(shares[7].astype(jnp.bfloat16), "grp").astype(jnp.float32),
        lax.psum(shares[8].astype(jnp.bfloat16), "grp").astype(jnp.float32),
    )
    return (
        output.reshape(seq_count, tok_rows, model_width),
        grad_inputs,
        totals[0],
        totals[1],
        totals[2],
        totals[3],
        totals[4],
        totals[5],
        totals[6],
        totals[7],
        totals[8],
    )


def solution(mesh):
    local = ring_plan
    if (mesh.shape["grp"], mesh.shape["seq"]) == (2, 16):
        local = cube_plan
    return jax.shard_map(
        local,
        mesh=mesh,
        in_specs=(
            P("grp", "seq", None),
            P("grp", "seq", None),
            P("grp", None),
            P(),
            P("seq", None),
            P("seq", None),
            P("seq", None),
            P("seq", None),
            P("seq", None),
            P("seq", None),
            P("seq", None),
            P("seq"),
            P("seq"),
        ),
        out_specs=(
            P("grp", "seq", None),
            P("grp", "seq", None),
            P("seq", None),
            P("seq", None),
            P("seq", None),
            P("seq", None),
            P("seq", None),
            P("seq", None),
            P("seq", None),
            P("seq"),
            P("seq"),
        ),
        check_vma=False,
    )
```
